32 devices in a mesh: dp: 16 (over z, y, x), tensor: 2 (over core).
Axes of the slice: x: 2, y: 2, z: 4, core: 2. Of those that a mesh axis runs over, the one named last changes fastest.
Arguments:
- layer_input: bfloat16 [32768, 1024], P(('dp', 'tensor')), may hold values from -6 to 6
- segment_ids: int32 [32768], P('dp'), may hold values from 0 to 2, as said below
- out_grad: bfloat16 [32768, 1024], P(('dp', 'tensor')), may hold values from -6 to 6
- norm_gain: float32 [1024], replicated, may hold values from 0.5 to 1.5
- query_w: bfloat16 [1024, 512], P('dp', 'tensor'), may hold values from -0.1875 to 0.1875
- key_w: bfloat16 [1024, 128], P('dp'), may hold values from -0.1875 to 0.1875
- value_w: bfloat16 [1024, 128], P('dp'), may hold values from -0.1875 to 0.1875
- out_w: bfloat16 [512, 1024], P('tensor', 'dp'), may hold values from -0.75 to 0.75
- mamba_gate_w: bfloat16 [1024, 1536], P('dp', 'tensor'), may hold values from -0.1875 to 0.1875
- mamba_in_w: bfloat16 [1024, 1536], P('dp', 'tensor'), may hold values from -0.1875 to 0.1875
- state_in_w: bfloat16 [1024, 256], P('dp'), may hold values from -0.1875 to 0.1875
- step_w: bfloat16 [1024, 24], P('dp', 'tensor'), may hold values from -0.1875 to 0.1875
- channel_conv: float32 [4, 1536], P(None, 'tensor'), may hold values from -3 to 3
- state_conv: float32 [4, 256], replicated, may hold values from -3 to 3
- step_bias: float32 [24], P('tensor'), may hold values from -4 to -1
- decay_log: float32 [24], P('tensor'), may hold values from -3 to 1
- skip_gain: float32 [24], P('tensor'), may hold values from 0.5 to 2
- mamba_out_w: bfloat16 [1536, 1024], P('tensor', 'dp'), may hold values from -0.0390625 to 0.0390625
- ffn_gain: float32 [1024], replicated, may hold values from 0.5 to 1.5
- ffn_gate_w: bfloat16 [1024, 2048], P('dp', 'tensor'), may hold values from -0.1875 to 0.1875
- ffn_up_w: bfloat16 [1024, 2048], P('dp', 'tensor'), may hold values from -0.1875 to 0.1875
- ffn_down_w: bfloat16 [2048, 1024], P('tensor', 'dp'), may hold values from -0.125 to 0.125
Outputs:
- block_out: bfloat16 [32768, 1024], P(('dp', 'tensor'))
- input_grad: float32 [32768, 1024], P(('dp', 'tensor'))
- norm_gain_grad: float32 [1024], replicated
- query_w_grad: float32 [1024, 512], P('dp', 'tensor')
- key_w_grad: float32 [1024, 128], P('dp')
- value_w_grad: float32 [1024, 128], P('dp')
- out_w_grad: float32 [512, 1024], P('tensor', 'dp')
- mamba_gate_w_grad: float32 [1024, 1536], P('dp', 'tensor')
- mamba_in_w_grad: float32 [1024, 1536], P('dp', 'tensor')
- state_in_w_grad: float32 [1024, 256], P('dp')
- step_w_grad: float32 [1024, 24], P('dp', 'tensor')
- channel_conv_grad: float32 [4, 1536], P(None, 'tensor')
- state_conv_grad: float32 [4, 256], replicated
- step_bias_grad: float32 [24], P('tensor')
- decay_log_grad: float32 [24], P('tensor')
- skip_gain_grad: float32 [24], P('tensor')
- mamba_out_w_grad: float32 [1536, 1024], P('tensor', 'dp')
- ffn_gain_grad: float32 [1024], replicated
- ffn_gate_w_grad: float32 [1024, 2048], P('dp', 'tensor')
- ffn_up_w_grad: float32 [1024, 2048], P('dp', 'tensor')
- ffn_down_w_grad: float32 [2048, 1024], P('tensor', 'dp')
The draws below stay inside these ranges and needn't reach their ends.
Inputs may be any that keep to these rules, and one draw needn't show every extreme that they name: `segment_ids`: within each sequence of 2048 tokens the segment numbers start at 0, never fall, and rise by one at each of 2 document starts.
All inputs are finite; a program needn't handle non-finite values.
Results may differ from the reference program's by a relative error of at most 0.024.
Values may be sent and summed in bfloat16 or wider, within the bound.
No kernel may reach another device: no remote copies, remote signals or barrier semaphores. Data moves between devices by JAX's collectives and lax.ppermute only.
A program may use at most 512 MiB of HBM per device.

```python
import math
import jax
import jax.numpy as jnp
from jax import lax

D = 1024
HEADS = 8
KV_HEADS = 2
HEAD_DIM = 64
SSM_HEADS = 24
SSM_DIM = 64
STATE = 128
CONV = 4
FF = 2048
LEN = 2048
SCAN_BLOCK = 256
BLOCK = 512
DOCS = 3
TOKENS = 32768


def draw_segment_ids(key, part):
    key = jax.random.fold_in(key, 11)
    seq_count = TOKENS // LEN
    seq_keys = jax.random.split(key, seq_count)

    def one_sequence(seq_key):
        shuffled = jax.random.permutation(seq_key, LEN - 1)
        starts = jnp.sort(shuffled[:DOCS - 1] + 1)
        places = jnp.arange(LEN, dtype=jnp.int32)
        return jnp.sum((places[:, None] >= starts[None, :]).astype(jnp.int32), axis=1)
    return jax.vmap(one_sequence)(seq_keys).reshape(-1).astype(jnp.int32)


def levels(rng, shape, cuts, least, high):
    def one(dim, parts):
        heights = jax.random.uniform(jax.random.fold_in(jax.random.fold_in(rng, 6), dim), (parts,), jnp.float32, least / len(cuts), high / len(cuts))
        return jnp.repeat(jnp.exp(heights), shape[dim] // parts).reshape((-1,) + (1,) * (len(shape) - dim - 1))

    factor_of = one(*cuts[0])
    for cut in cuts[1:]:
        factor_of = factor_of * one(*cut)
    return factor_of


def bell_draw(key, shape, spread, bound, cuts=(), kind=jnp.bfloat16):
    values = jax.random.normal(key, shape, jnp.float32) * spread
    if len(cuts) > 0:
        values = levels(key, shape, cuts, -0.22, 0.18) * values
    return jnp.clip(values, min=-bound, max=bound).astype(kind)


def setup_inputs(seed: int = 0) -> dict:
    key_of = jax.random.split(jax.random.key(seed), 23)
    return {
        "layer_input": bell_draw(key_of[0], (TOKENS, D), 1.0, 6.0, ((0, 32),)),
        "segment_ids": draw_segment_ids(jax.random.fold_in(key_of[22], 71), 0),
        "out_grad": bell_draw(key_of[2], (TOKENS, D), 1.0, 6.0, ((0, 32),)),
        "norm_gain": jnp.clip(1.0 + 0.1 * jax.random.normal(key_of[3], (D,), jnp.float32), 0.5, 1.5),
        "query_w": bell_draw(key_of[4], (D, HEADS * HEAD_DIM), D ** -0.5, 0.1875, ((0, 16), (1, 2))),
        "key_w": bell_draw(key_of[5], (D, KV_HEADS * HEAD_DIM), D ** -0.5, 0.1875, ((0, 16),)),
        "value_w": bell_draw(key_of[6], (D, KV_HEADS * HEAD_DIM), D ** -0.5, 0.1875, ((0, 16),)),
        "out_w": bell_draw(key_of[7], (HEADS * HEAD_DIM, D), (HEADS * HEAD_DIM // 8) ** -0.5, 0.75, ((0, 2), (1, 16))),
        "mamba_gate_w": bell_draw(key_of[8], (D, SSM_HEADS * SSM_DIM), D ** -0.5, 0.1875, ((0, 16), (1, 2))),
        "mamba_in_w": bell_draw(key_of[9], (D, SSM_HEADS * SSM_DIM), D ** -0.5, 0.1875, ((0, 16), (1, 2))),
        "state_in_w": bell_draw(key_of[10], (D, 2 * STATE), D ** -0.5, 0.1875, ((0, 16),)),
        "step_w": bell_draw(key_of[11], (D, SSM_HEADS), D ** -0.5, 0.1875, ((0, 16), (1, 2))),
        "channel_conv": bell_draw(key_of[12], (CONV, SSM_HEADS * SSM_DIM), CONV ** -0.5, 3.0, ((1, 2),), jnp.float32),
        "state_conv": bell_draw(key_of[13], (CONV, 2 * STATE), CONV ** -0.5, 3.0, (), jnp.float32),
        "step_bias": jnp.clip(-4.0 + 3.0 * jax.random.uniform(key_of[14], (SSM_HEADS,), jnp.float32) ** levels(key_of[14], (SSM_HEADS,), ((0, 2),), -0.2, 0.2), -4.0, -1.0),
        "decay_log": jnp.clip(-3.0 + 4.0 * jax.random.uniform(key_of[15], (SSM_HEADS,), jnp.float32) ** levels(key_of[15], (SSM_HEADS,), ((0, 2),), -0.2, 0.2), -3.0, 1.0),
        "skip_gain": jnp.clip(0.5 + 1.5 * jax.random.uniform(key_of[16], (SSM_HEADS,), jnp.float32) ** levels(key_of[16], (SSM_HEADS,), ((0, 2),), -0.2, 0.2), 0.5, 2.0),
        "mamba_out_w": bell_draw(key_of[17], (SSM_HEADS * SSM_DIM, D), (16 * SSM_HEADS * SSM_DIM) ** -0.5, 0.0390625, ((0, 2), (1, 16))),
        "ffn_gain": jnp.clip(1.0 + 0.1 * jax.random.normal(key_of[18], (D,), jnp.float32), 0.5, 1.5),
        "ffn_gate_w": bell_draw(key_of[19], (D, FF), D ** -0.5, 0.1875, ((0, 16), (1, 2))),
        "ffn_up_w": bell_draw(key_of[20], (D, FF), D ** -0.5, 0.1875, ((0, 16), (1, 2))),
        "ffn_down_w": bell_draw(key_of[21], (FF, D), FF ** -0.5, 0.125, ((0, 2), (1, 16))),
    }


NORM_EPS = 1e-05
ROPE_THETA = 100000000000.0
MASKED_SCORE = -1e+30
PRECISE = lax.Precision.HIGHEST

@jax.custom_vjp
def low(v):
    return lax.optimization_barrier(v.astype(jnp.bfloat16)).astype(jnp.float32)

@jax.custom_vjp
def low_back(v):
    return v

def low_keep(v):
    return (low(v), None)

def low_pass(kept, grad):
    return (grad,)

def back_keep(v):
    return (v, None)

def back_low(kept, grad):
    return (low(grad),)
low.defvjp(low_keep, low_pass)
low_back.defvjp(back_keep, back_low)

def rms_norm(values, gain):
    return values * lax.rsqrt(lax.optimization_barrier(jnp.mean(values * values, axis=-1, keepdims=True)) + NORM_EPS) * gain

def rotate(values, positions, turn_sign):
    half_width = values.shape[-1] // 2
    freq_index = jnp.arange(half_width, dtype=jnp.float32)
    frequency = jnp.exp(freq_index * (-2.0 * math.log(ROPE_THETA) / values.shape[-1]))
    angles = positions.astype(jnp.float32)[:, None] * frequency[None, :]
    cosine = jnp.cos(angles)[:, None, :]
    sine_part = turn_sign * jnp.sin(angles)[:, None, :]
    first_half = values[..., :half_width]
    second = values[..., half_width:]
    return jnp.concatenate([first_half * cosine - second * sine_part, second * cosine + first_half * sine_part], axis=-1)

def causal_conv(values, kernel, seg_ids):
    length = values.shape[0]
    tap_count = kernel.shape[0]
    padded = jnp.pad(values, ((tap_count - 1, 0), (0, 0)))
    seg_pad = jnp.concatenate([jnp.full((tap_count - 1,), -1, jnp.int32), seg_ids.astype(jnp.int32)])
    summed = values * kernel[tap_count - 1]
    for lag_step in range(1, tap_count):
        shifted = padded[tap_count - 1 - lag_step:tap_count - 1 - lag_step + length]
        same_doc = seg_pad[tap_count - 1 - lag_step:tap_count - 1 - lag_step + length] == seg_ids
        summed = summed + jnp.where(same_doc[:, None], shifted, 0.0) * kernel[tap_count - 1 - lag_step]
    return summed

def state_scan(inputs, step_size, log_decay, entry, readout, seg_ids):
    length, head_count, head_width = inputs.shape
    block_count = length // SCAN_BLOCK
    before = jnp.concatenate([jnp.full((1,), -1, jnp.int32), seg_ids[SCAN_BLOCK - 1:length - 1:SCAN_BLOCK].astype(jnp.int32)])
    block_pos = jnp.arange(SCAN_BLOCK, dtype=jnp.int32)
    lower_tri = block_pos[:, None] >= block_pos[None, :]

    def block_step(carry_state, pieces):
        part_in, part_step, part_decay, part_entry, part_read, part_seg, prior_seg = pieces
        cum_decay = jnp.cumsum(part_decay, axis=0)
        causal = lower_tri & (part_seg[:, None] == part_seg[None, :])
        causal_cube = causal[:, :, None]
        decay_gap = cum_decay[:, None, :] - cum_decay[None, :, :]
        kernel = jnp.where(causal_cube, jnp.exp(jnp.where(causal_cube, decay_gap, 0.0)), 0.0)
        read_entry = jnp.dot(part_read, part_entry.T, precision=PRECISE)
        mixing = read_entry[:, :, None] * kernel * part_step[None, :, :]
        within = jnp.einsum('ijh,jhp->ihp', mixing, part_in, precision=PRECISE)
        carried = jnp.where(part_seg == prior_seg, 1.0, 0.0)
        from_state = jnp.einsum('in,hpn->ihp', part_read, carry_state, precision=PRECISE)
        from_state = from_state * (jnp.exp(cum_decay) * carried[:, None])[:, :, None]
        last_seg = part_seg[SCAN_BLOCK - 1]
        tail_weight = jnp.where((part_seg == last_seg)[:, None], jnp.exp(cum_decay[SCAN_BLOCK - 1][None, :] - cum_decay), 0.0) * part_step
        fresh_state = jnp.einsum('jh,jn,jhp->hpn', tail_weight, part_entry, part_in, precision=PRECISE)
        keep_factor = jnp.where(last_seg == prior_seg, jnp.exp(cum_decay[SCAN_BLOCK - 1]), 0.0)
        return (fresh_state + carry_state * keep_factor[:, None, None], within + from_state)

    def by_block(array):
        return array.reshape((block_count, SCAN_BLOCK) + array.shape[1:])
    start_state = jnp.zeros((head_count, head_width, entry.shape[1]), inputs.dtype)
    final_state, outputs = lax.scan(jax.checkpoint(block_step), start_state, (by_block(inputs), by_block(step_size), by_block(log_decay), by_block(entry), by_block(readout), by_block(seg_ids), before))
    return outputs.reshape(length, head_count, head_width)

def mamba_mix(gate_pre, inner_pre, state_pre, step_pre, channel_conv, state_conv, step_bias, decay_log, skip_gain, seg_ids):
    length = gate_pre.shape[0]
    head_count = step_pre.shape[1]
    inner = jax.nn.silu(causal_conv(inner_pre, channel_conv, seg_ids)).reshape(length, head_count, -1)
    states = jax.nn.silu(causal_conv(state_pre, state_conv, seg_ids))
    step_size = jax.nn.softplus(step_pre + step_bias)
    log_decay = -step_size * jnp.exp(decay_log)
    scanned = state_scan(inner, step_size, log_decay, states[:, :STATE], states[:, STATE:], seg_ids)
    scanned = scanned + skip_gain[None, :, None] * inner
    return scanned.reshape(length, -1) * jax.nn.silu(gate_pre)

def exact_dot(left, right):
    return jnp.dot(left, right, precision=PRECISE)

def attend(queries, key_rows, value_rows, seg_ids):
    length = queries.shape[0]
    groups = key_rows.shape[1]
    grouped = queries.reshape(length // BLOCK, BLOCK, groups, -1, queries.shape[-1])
    starts = jnp.arange(length // BLOCK, dtype=jnp.int32) * BLOCK
    key_pos = jnp.arange(length, dtype=jnp.int32)
    score_scale = queries.shape[-1] ** (-0.5)

    def one_block(pieces):
        q_block, row_start = pieces
        row_pos = row_start + jnp.arange(BLOCK, dtype=jnp.int32)
        seg_block = lax.dynamic_slice_in_dim(seg_ids, row_start.astype(jnp.int32), BLOCK, 0)
        allowed = (key_pos[None, :] <= row_pos[:, None]) & (seg_ids[None, :] == seg_block[:, None])
        scores = low_back(jnp.einsum('qgrd,kgd->grqk', q_block, key_rows, precision=PRECISE) * score_scale)
        scores = jnp.where(allowed[None, None], scores, MASKED_SCORE)
        prob_rows = low(jax.nn.softmax(scores, axis=-1))
        mixed = jnp.einsum('grqk,kgd->qgrd', prob_rows, value_rows, precision=PRECISE)
        return low(low_back(mixed))
    blocks = lax.map(jax.checkpoint(one_block), (grouped, starts))
    return blocks.reshape(length, -1)

def layer(params, tokens, seg_ids):
    norm_gain, query_w, key_w, value_w, out_w, mamba_gate_w, mamba_in_w, state_in_w, step_w, channel_conv, state_conv, step_bias, decay_log, skip_gain, mamba_out_w, ffn_gain, ffn_gate_w, ffn_up_w, ffn_down_w = params
    length = tokens.shape[0]
    positions = jnp.arange(length, dtype=jnp.int32)
    normed = low(rms_norm(tokens, norm_gain))
    queries = low(rotate(low_back(exact_dot(normed, query_w)).reshape(length, HEADS, HEAD_DIM), positions, 1.0))
    key_rows = low(rotate(low_back(exact_dot(normed, key_w)).reshape(length, KV_HEADS, HEAD_DIM), positions, 1.0))
    value_rows = low(low_back(exact_dot(normed, value_w)).reshape(length, KV_HEADS, HEAD_DIM))
    attended = attend(queries, key_rows, value_rows, seg_ids)
    gate_pre = low_back(exact_dot(normed, mamba_gate_w))
    inner_pre = low_back(exact_dot(normed, mamba_in_w))
    state_pre = low_back(exact_dot(normed, state_in_w))
    step_pre = low_back(exact_dot(normed, step_w))
    gated = low(mamba_mix(gate_pre, inner_pre, state_pre, step_pre, channel_conv, state_conv, step_bias, decay_log, skip_gain, seg_ids))
    branch = low_back(exact_dot(attended, out_w) + exact_dot(gated, mamba_out_w))
    middle = tokens + branch
    normed_mid = low(rms_norm(middle, ffn_gain))
    gate_vals = low_back(exact_dot(normed_mid, ffn_gate_w))
    up_vals = low_back(exact_dot(normed_mid, ffn_up_w))
    act = low(jax.nn.silu(gate_vals) * up_vals)
    return middle + low_back(exact_dot(act, ffn_down_w))

def reference(layer_input, segment_ids, out_grad, norm_gain, query_w, key_w, value_w, out_w, mamba_gate_w, mamba_in_w, state_in_w, step_w, channel_conv, state_conv, step_bias, decay_log, skip_gain, mamba_out_w, ffn_gain, ffn_gate_w, ffn_up_w, ffn_down_w):
    params = tuple((array.astype(jnp.float32) for array in (norm_gain, query_w, key_w, value_w, out_w, mamba_gate_w, mamba_in_w, state_in_w, step_w, channel_conv, state_conv, step_bias, decay_log, skip_gain, mamba_out_w, ffn_gain, ffn_gate_w, ffn_up_w, ffn_down_w)))
    seq_count = segment_ids.shape[0] // LEN
    tokens = layer_input.astype(jnp.float32).reshape(seq_count, LEN, -1)
    grads_in = out_grad.astype(jnp.float32).reshape(seq_count, LEN, -1)
    seg_rows = segment_ids.astype(jnp.int32).reshape(seq_count, LEN)

    def one_sequence(running, pieces):
        seq_tokens, seq_grad, seq_seg = pieces
        result, pullback = jax.vjp(lambda param_set, token_set: layer(param_set, token_set, seq_seg), params, seq_tokens)
        par_grads, tok_grad = pullback(seq_grad)
        running = jax.tree.map(lambda running_part, new_part: running_part + new_part, running, par_grads)
        return (running, (result.astype(jnp.bfloat16), tok_grad))
    zero_grads = jax.tree.map(jnp.zeros_like, params)
    totals, (outputs, input_grads) = lax.scan(one_sequence, zero_grads, (tokens, grads_in, seg_rows))
    g_norm, g_query, g_key, g_value, g_out, g_mgate, g_min, g_state, g_step, g_cconv, g_sconv, g_sbias, g_dlog, g_skip, g_mout, g_ffn_gain, g_fgate, g_fup, g_fdown = totals
    return (outputs.reshape(-1, outputs.shape[-1]), input_grads.reshape(-1, input_grads.shape[-1]), g_norm, g_query, g_key, g_value, g_out, g_mgate, g_min, g_state, g_step, g_cconv, g_sconv, g_sbias, g_dlog, g_skip, g_mout, g_ffn_gain, g_fgate, g_fup, g_fdown)
```

```python
import functools
import math

import jax
import jax.numpy as jnp
from jax import lax
from jax.experimental import pallas as pl
from jax.experimental.pallas import tpu as pltpu
from jax.sharding import PartitionSpec as P

HEAD_DIM = 64
STATE = 128
LEN = 2048
BQ = 512
Q = 128
HALO = 8
NEG = -1e30
PRECISE = lax.Precision.HIGHEST
F32 = jnp.float32
BF16 = jnp.bfloat16
VMEM_BYTES = 48 * 1024 * 1024


def dot_nn(left, right):
    return lax.dot_general(left, right, (((1,), (0,)), ((), ())), preferred_element_type=F32)


def dot_nt(left, right):
    return lax.dot_general(left, right, (((1,), (1,)), ((), ())), preferred_element_type=F32)


def dot_tn(left, right):
    return lax.dot_general(left, right, (((0,), (0,)), ((), ())), preferred_element_type=F32)


def exact_nn(left, right):
    return lax.dot_general(
        left, right, (((1,), (0,)), ((), ())), precision=PRECISE, preferred_element_type=F32
    )


def exact_nt(left, right):
    return lax.dot_general(
        left, right, (((1,), (1,)), ((), ())), precision=PRECISE, preferred_element_type=F32
    )


def attend_fwd_kernel(heads, first_ref, q_ref, k_ref, v_ref, seg_ref, segrow_ref, out_ref, lse_ref,
                      top_ref, sum_ref, acc_ref):
    seq = pl.program_id(0)
    block = pl.program_id(1)
    top_ref[...] = jnp.full_like(top_ref, NEG)
    sum_ref[...] = jnp.zeros_like(sum_ref)
    acc_ref[...] = jnp.zeros_like(acc_ref)
    scale = HEAD_DIM ** -0.5
    row = lax.broadcasted_iota(jnp.int32, (BQ, BQ), 0)
    col = lax.broadcasted_iota(jnp.int32, (BQ, BQ), 1)

    def step(j, carry):
        k = k_ref[pl.ds(pl.multiple_of(j * BQ, BQ), BQ), :]
        v = v_ref[pl.ds(pl.multiple_of(j * BQ, BQ), BQ), :]
        segrow = segrow_ref[0, pl.ds(j, 1), :]
        allowed = (segrow == seg_ref[...]) & (col + (j - block) * BQ <= row)
        bias = jnp.where(allowed, 0.0, NEG)
        for h in range(heads):
            s = dot_nt(q_ref[:, h * HEAD_DIM:(h + 1) * HEAD_DIM], k) * scale + bias
            old = top_ref[h]
            new = jnp.maximum(old, jnp.max(s, axis=1, keepdims=True))
            shrink = jnp.exp(old - new)
            p = jnp.exp(s - new)
            sum_ref[h] = sum_ref[h] * shrink + jnp.sum(p, axis=1, keepdims=True)
            acc_ref[h] = acc_ref[h] * shrink + dot_nn(p.astype(BF16), v)
            top_ref[h] = new
        return carry

    lax.fori_loop(first_ref[seq * (LEN // BQ) + block], block + 1, step, 0)
    for h in range(heads):
        total = sum_ref[h]
        out_ref[:, h * HEAD_DIM:(h + 1) * HEAD_DIM] = (acc_ref[h] / total).astype(BF16)
        lse_ref[:, h:h + 1] = top_ref[h] + jnp.log(total)


def attend_fwd(first, q, k, v, seg_col, seg_rows):
    rows, width = q.shape
    heads = width // HEAD_DIM
    seqs = rows // LEN
    per = LEN // BQ
    return pl.pallas_call(
        functools.partial(attend_fwd_kernel, heads),
        grid_spec=pltpu.PrefetchScalarGridSpec(
            num_scalar_prefetch=1,
            grid=(seqs, per),
            in_specs=[
                pl.BlockSpec((BQ, width), lambda s, i, f: (s * per + i, 0)),
                pl.BlockSpec((LEN, HEAD_DIM), lambda s, i, f: (s, 0)),
                pl.BlockSpec((LEN, HEAD_DIM), lambda s, i, f: (s, 0)),
                pl.BlockSpec((BQ, 1), lambda s, i, f: (s * per + i, 0)),
                pl.BlockSpec((1, per, BQ), lambda s, i, f: (s, 0, 0)),
            ],
            out_specs=[
                pl.BlockSpec((BQ, width), lambda s, i, f: (s * per + i, 0)),
                pl.BlockSpec((BQ, heads), lambda s, i, f: (s * per + i, 0)),
            ],
            scratch_shapes=[
                pltpu.VMEM((heads, BQ, 1), F32),
                pltpu.VMEM((heads, BQ, 1), F32),
                pltpu.VMEM((heads, BQ, HEAD_DIM), F32),
            ],
        ),
        out_shape=[
            jax.ShapeDtypeStruct((rows, width), BF16),
            jax.ShapeDtypeStruct((rows, heads), F32),
        ],
        compiler_params=pltpu.CompilerParams(vmem_limit_bytes=VMEM_BYTES),
        cost_estimate=pl.CostEstimate(
            flops=2 * rows * LEN * width, bytes_accessed=4 * rows * width,
            transcendentals=rows * LEN * heads // 2),
        name="attend_fwd",
    )(first, q, k, v, seg_col, seg_rows)


def attend_bwd_kernel(heads, first_ref, q_ref, k_ref, v_ref, g_ref, seg_ref, segrow_ref, lse_ref,
                      delta_ref, cos_ref, sin_ref, cosk_ref, sink_ref, dq_ref, dk_ref, dv_ref,
                      dqs_ref, dks_ref, dvs_ref):
    seq = pl.program_id(0)
    block = pl.program_id(1)
    half = HEAD_DIM // 2
    scale = HEAD_DIM ** -0.5

    @pl.when(block == 0)
    def _():
        dks_ref[...] = jnp.zeros_like(dks_ref)
        dvs_ref[...] = jnp.zeros_like(dvs_ref)

    dqs_ref[...] = jnp.zeros_like(dqs_ref)
    key_pos = lax.broadcasted_iota(jnp.int32, (BQ, BQ), 0)
    row_pos = lax.broadcasted_iota(jnp.int32, (BQ, BQ), 1)

    def step(j, carry):
        at = pl.ds(pl.multiple_of(j * BQ, BQ), BQ)
        k = k_ref[at, :]
        v = v_ref[at, :]
        allowed = (segrow_ref[0] == seg_ref[at, :]) & (key_pos + (j - block) * BQ <= row_pos)
        bias = jnp.where(allowed, 0.0, NEG)
        dk = jnp.zeros((BQ, HEAD_DIM), F32)
        dv = jnp.zeros((BQ, HEAD_DIM), F32)
        for h in range(heads):
            lanes = slice(h * HEAD_DIM, (h + 1) * HEAD_DIM)
            q = q_ref[:, lanes]
            g = g_ref[:, lanes]
            s = dot_nt(k, q) * scale + bias
            p = jnp.exp(s - lse_ref[0, h:h + 1, :])
            dp = dot_nt(v, g)
            ds = (p * (dp - delta_ref[0, h:h + 1, :])).astype(BF16)
            dv = dv + dot_nn(p.astype(BF16), g)
            dk = dk + dot_nn(ds, q)
            dqs_ref[h] = dqs_ref[h] + dot_tn(ds, k)
        dks_ref[at, :] = dks_ref[at, :] + dk
        dvs_ref[at, :] = dvs_ref[at, :] + dv
        return carry

    lax.fori_loop(first_ref[seq * (LEN // BQ) + block], block + 1, step, 0)

    def turn_back(x, cos, sin):
        swapped = jnp.concatenate([x[:, half:], -x[:, :half]], axis=1)
        return x * cos + swapped * sin

    for h in range(heads):
        dq = turn_back(dqs_ref[h] * scale, cos_ref[...], sin_ref[...])
        dq_ref[:, h * HEAD_DIM:(h + 1) * HEAD_DIM] = dq.astype(BF16)

    @pl.when(block == pl.num_programs(1) - 1)
    def _():
        dk_ref[...] = turn_back(dks_ref[...] * scale, cosk_ref[...], sink_ref[...]).astype(BF16)
        dv_ref[...] = dvs_ref[...].astype(BF16)


def attend_bwd(first, q, k, v, g, seg_col, seg_rows, lse_rows, delta_rows, cos, sin):
    rows, width = q.shape
    heads = width // HEAD_DIM
    seqs = rows // LEN
    per = LEN // BQ
    return pl.pallas_call(
        functools.partial(attend_bwd_kernel, heads),
        grid_spec=pltpu.PrefetchScalarGridSpec(
            num_scalar_prefetch=1,
            grid=(seqs, per),
            in_specs=[
                pl.BlockSpec((BQ, width), lambda s, i, f: (s * per + i, 0)),
                pl.BlockSpec((LEN, HEAD_DIM), lambda s, i, f: (s, 0)),
                pl.BlockSpec((LEN, HEAD_DIM), lambda s, i, f: (s, 0)),
                pl.BlockSpec((BQ, width), lambda s, i, f: (s * per + i, 0)),
                pl.BlockSpec((LEN, 1), lambda s, i, f: (s, 0)),
                pl.BlockSpec((1, 1, BQ), lambda s, i, f: (s * per + i, 0, 0)),
                pl.BlockSpec((1, heads, BQ), lambda s, i, f: (s * per + i, 0, 0)),
                pl.BlockSpec((1, heads, BQ), lambda s, i, f: (s * per + i, 0, 0)),
                pl.BlockSpec((BQ, HEAD_DIM), lambda s, i, f: (i, 0)),
                pl.BlockSpec((BQ, HEAD_DIM), lambda s, i, f: (i, 0)),
                pl.BlockSpec((LEN, HEAD_DIM), lambda s, i, f: (0, 0)),
                pl.BlockSpec((LEN, HEAD_DIM), lambda s, i, f: (0, 0)),
            ],
            out_specs=[
                pl.BlockSpec((BQ, width), lambda s, i, f: (s * per + i, 0)),
                pl.BlockSpec((LEN, HEAD_DIM), lambda s, i, f: (s, 0)),
                pl.BlockSpec((LEN, HEAD_DIM), lambda s, i, f: (s, 0)),
            ],
            scratch_shapes=[
                pltpu.VMEM((heads, BQ, HEAD_DIM), F32),
                pltpu.VMEM((LEN, HEAD_DIM), F32),
                pltpu.VMEM((LEN, HEAD_DIM), F32),
            ],
        ),
        out_shape=[
            jax.ShapeDtypeStruct((rows, width), BF16),
            jax.ShapeDtypeStruct((rows, HEAD_DIM), BF16),
            jax.ShapeDtypeStruct((rows, HEAD_DIM), BF16),
        ],
        compiler_params=pltpu.CompilerParams(vmem_limit_bytes=VMEM_BYTES),
        cost_estimate=pl.CostEstimate(
            flops=5 * rows * LEN * width, bytes_accessed=8 * rows * width,
            transcendentals=rows * LEN * heads // 2),
        name="attend_bwd",
    )(first, q, k, v, g, seg_col, seg_rows, lse_rows, delta_rows, cos, sin, cos, sin)


LAG, LEAD, CARRIED, ENDING = 0, 3, 6, 7


def token_masks(seg):
    seqs = seg.shape[0]
    padded = jnp.pad(seg, ((0, 0), (3, 3)), constant_values=-1)
    columns = [padded[:, 3 - k:3 - k + LEN] == seg for k in (1, 2, 3)]
    columns += [padded[:, 3 + k:3 + k + LEN] == seg for k in (1, 2, 3)]
    chunks = seg.reshape(seqs, LEN // Q, Q)
    prior = jnp.pad(chunks[:, :-1, -1:], ((0, 0), (1, 0), (0, 0)), constant_values=-1)
    columns.append((chunks == prior).reshape(seqs, LEN))
    columns.append((chunks == chunks[:, :, -1:]).reshape(seqs, LEN))
    return jnp.stack(columns, axis=-1).astype(F32).reshape(seqs * LEN, 8)


def shifted_conv(buf_ref, width, masks, taps):
    rows = [buf_ref[HALO - k:HALO - k + Q, :width] for k in range(4)]
    rows = [rows[0]] + [rows[k] * masks[:, LAG + k - 1:LAG + k] for k in (1, 2, 3)]
    total = rows[0] * taps[3:4, :]
    for k in (1, 2, 3):
        total = total + rows[k] * taps[3 - k:4 - k, :]
    return total, rows


def softplus(x):
    return jnp.maximum(x, 0.0) + jnp.log1p(jnp.exp(-jnp.abs(x)))


def chunk_masks(seg_ref, segrow_ref):
    row = lax.broadcasted_iota(jnp.int32, (Q, Q), 0)
    col = lax.broadcasted_iota(jnp.int32, (Q, Q), 1)
    same = seg_ref[...] == segrow_ref[0]
    return row, col, same


def split_pre(ref, width):
    return (ref.at[:, pl.ds(0, width)], ref.at[:, pl.ds(width, width)],
            ref.at[:, pl.ds(2 * width, 3 * STATE)])


def mix_fwd_kernel(heads, seg_ref, segrow_ref, mask_ref, pre_ref, cw_ref,
                   sw_ref, bias_ref, rate_ref, skip_ref, spread_ref, gated_ref, y_ref, states_ref,
                   carry_ref, buf_ref, sbuf_ref):
    width = y_ref.shape[1]
    gate_ref, inner_ref, ss_ref = split_pre(pre_ref, width)

    @pl.when(pl.program_id(1) == 0)
    def _():
        carry_ref[...] = jnp.zeros_like(carry_ref)
        buf_ref[0:HALO, :] = jnp.zeros((HALO, buf_ref.shape[1]), F32)
        sbuf_ref[0:HALO, :] = jnp.zeros((HALO, sbuf_ref.shape[1]), F32)

    masks = mask_ref[...]
    buf_ref[HALO:HALO + Q, :] = inner_ref[...]
    sbuf_ref[HALO:HALO + Q, :] = ss_ref[:, :2 * STATE]
    z, _ = shifted_conv(buf_ref, buf_ref.shape[1], masks, cw_ref[...])
    zs, _ = shifted_conv(sbuf_ref, 2 * STATE, masks, sw_ref[...])
    buf_ref[0:HALO, :] = buf_ref[Q:Q + HALO, :]
    sbuf_ref[0:HALO, :] = sbuf_ref[Q:Q + HALO, :]
    x = z * jax.nn.sigmoid(z)
    states = (zs * jax.nn.sigmoid(zs)).astype(BF16)
    entry = states[:, :STATE]
    readout = states[:, STATE:]
    size = softplus(ss_ref[:, 2 * STATE:] + bias_ref[...])
    decay = -size * jnp.exp(rate_ref[...])
    row, col, same = chunk_masks(seg_ref, segrow_ref)
    tri = jnp.where(row >= col, 1.0, 0.0)
    cum = exact_nn(tri, decay)
    cum_rows = cum.T
    bias = jnp.where((row >= col) & same, 0.0, NEG)
    spread = spread_ref[...]
    into = jnp.exp(cum) * masks[:, CARRIED:CARRIED + 1]
    tail = jnp.exp(cum[Q - 1:Q, :] - cum) * masks[:, ENDING:ENDING + 1]
    size_wide = exact_nn(size, spread)
    into_wide = exact_nn(into, spread)
    tail_wide = exact_nn(tail, spread)
    xs = (x * size_wide)
    xs_low = xs.astype(BF16)
    pair = dot_nt(readout, entry)
    prior = carry_ref[...]
    states_ref[0] = prior
    y = dot_nn(readout, prior.astype(BF16)) * into_wide
    for h in range(heads):
        lanes = slice(h * HEAD_DIM, (h + 1) * HEAD_DIM)
        mix = (pair * jnp.exp(cum[:, h:h + 1] - cum_rows[h:h + 1, :] + bias)).astype(BF16)
        y_ref[:, lanes] = dot_nn(mix, xs_low[:, lanes])
    y = y + y_ref[...]
    y_ref[...] = y
    fresh = dot_tn(entry, (xs * tail_wide).astype(BF16))
    carry_ref[...] = prior * into_wide[Q - 1:Q, :] + fresh
    gate = gate_ref[...]
    gated_ref[...] = ((y + skip_ref[...] * x) * (gate * jax.nn.sigmoid(gate))).astype(BF16)


def mix_fwd(seg_col, seg_rows, masks, pre, cw, sw, bias, rate, skip, spread,
            heads):
    rows, width = pre.shape[0], cw.shape[1]
    seqs = rows // LEN
    per = LEN // Q
    pre_width = pre.shape[1]
    blk = lambda w: pl.BlockSpec((Q, w), lambda s, c: (s * per + c, 0))
    whole = lambda a: pl.BlockSpec(a.shape, lambda s, c: (0, 0))
    return pl.pallas_call(
        functools.partial(mix_fwd_kernel, heads),
        grid=(seqs, per),
        in_specs=[
            blk(1),
            pl.BlockSpec((1, 1, Q), lambda s, c: (s * per + c, 0, 0)),
            blk(8), blk(pre_width),
            whole(cw), whole(sw), whole(bias), whole(rate), whole(skip), whole(spread),
        ],
        out_specs=[
            blk(width), blk(width),
            pl.BlockSpec((1, STATE, width), lambda s, c: (s * per + c, 0, 0)),
        ],
        out_shape=[
            jax.ShapeDtypeStruct((rows, width), BF16),
            jax.ShapeDtypeStruct((rows, width), F32),
            jax.ShapeDtypeStruct((seqs * per, STATE, width), F32),
        ],
        scratch_shapes=[
            pltpu.VMEM((STATE, width), F32),
            pltpu.VMEM((Q + HALO, width), F32),
            pltpu.VMEM((Q + HALO, 2 * STATE), F32),
        ],
        compiler_params=pltpu.CompilerParams(vmem_limit_bytes=VMEM_BYTES),
        cost_estimate=pl.CostEstimate(
            flops=rows * width * 1200, bytes_accessed=rows * width * 22,
            transcendentals=rows * width * 4),
        name="mix_fwd",
    )(seg_col, seg_rows, masks, pre, cw, sw, bias, rate, skip, spread)


def lead_sum(buf_ref, masks, taps):
    total = buf_ref[0:Q, :] * taps[3:4, :]
    for k in (1, 2, 3):
        total = total + buf_ref[k:k + Q, :] * masks[:, LEAD + k - 1:LEAD + k] * taps[3 - k:4 - k, :]
    return total


def column_sum(a):
    return jnp.sum(a, axis=0, keepdims=True)


def silu_slope(v, sig):
    return sig * (1.0 + v * (1.0 - sig))


def mix_bwd_kernel(heads, seg_ref, segrow_ref, mask_ref, pre_ref, pre_prev_ref, y_ref, states_ref, dout_ref, cw_ref, sw_ref, bias_ref, rate_ref,
                   skip_ref, spread_ref, dpre_ref, dcw_ref, dsw_ref, dhead_ref,
                   dskip_ref, carry_ref, buf_ref, sbuf_ref, dxs_ref, dz_ref, dzs_ref):
    width = y_ref.shape[1]
    gate_ref, inner_ref, ss_ref = split_pre(pre_ref, width)
    _, inner_prev_ref, ss_prev_ref = split_pre(pre_prev_ref, width)
    dgate_ref, dinner_ref, dss_ref = split_pre(dpre_ref, width)

    @pl.when((pl.program_id(0) == 0) & (pl.program_id(1) == 0))
    def _():
        dcw_ref[...] = jnp.zeros_like(dcw_ref)
        dsw_ref[...] = jnp.zeros_like(dsw_ref)
        dhead_ref[...] = jnp.zeros_like(dhead_ref)
        dskip_ref[...] = jnp.zeros_like(dskip_ref)

    @pl.when(pl.program_id(1) == 0)
    def _():
        carry_ref[...] = jnp.zeros_like(carry_ref)
        dz_ref[Q:Q + HALO, :] = jnp.zeros((HALO, width), F32)
        dzs_ref[Q:Q + HALO, :] = jnp.zeros((HALO, 2 * STATE), F32)

    masks = mask_ref[...]
    buf_ref[0:HALO, :] = inner_prev_ref[...]
    buf_ref[HALO:HALO + Q, :] = inner_ref[...]
    sbuf_ref[0:HALO, :] = ss_prev_ref[:, :2 * STATE]
    sbuf_ref[HALO:HALO + Q, :] = ss_ref[:, :2 * STATE]
    z, z_rows = shifted_conv(buf_ref, width, masks, cw_ref[...])
    zs, zs_rows = shifted_conv(sbuf_ref, 2 * STATE, masks, sw_ref[...])
    sig_z = jax.nn.sigmoid(z)
    sig_zs = jax.nn.sigmoid(zs)
    x = z * sig_z
    states = (zs * sig_zs).astype(BF16)
    entry = states[:, :STATE]
    readout = states[:, STATE:]
    raw = ss_ref[:, 2 * STATE:] + bias_ref[...]
    size = softplus(raw)
    rate = jnp.exp(rate_ref[...])
    decay = -size * rate
    row, col, same = chunk_masks(seg_ref, segrow_ref)
    tri = jnp.where(row >= col, 1.0, 0.0)
    cum = exact_nn(tri, decay)
    cum_rows = cum.T
    bias = jnp.where((row <= col) & same, 0.0, NEG)
    spread = spread_ref[...]
    into = jnp.exp(cum) * masks[:, CARRIED:CARRIED + 1]
    tail = jnp.exp(cum[Q - 1:Q, :] - cum) * masks[:, ENDING:ENDING + 1]
    size_wide = exact_nn(size, spread)
    into_wide = exact_nn(into, spread)
    tail_wide = exact_nn(tail, spread)
    xs = x * size_wide
    xs_low = xs.astype(BF16)
    gate = gate_ref[...]
    sig = jax.nn.sigmoid(gate)
    dout = dout_ref[...]
    y = y_ref[...]
    skip = skip_ref[...]
    dgate_ref[...] = (dout * (y + skip * x) * silu_slope(gate, sig)).astype(BF16)
    g = dout * (gate * sig)
    g_low = g.astype(BF16)
    dskip_ref[...] += column_sum(g * x)
    pair = dot_nt(entry, readout)
    dpair = jnp.zeros((Q, Q), F32)
    for h in range(heads):
        lanes = slice(h * HEAD_DIM, (h + 1) * HEAD_DIM)
        fade = jnp.exp(cum_rows[h:h + 1, :] - cum[:, h:h + 1] + bias)
        dxs_ref[:, lanes] = dot_nn((pair * fade).astype(BF16), g_low[:, lanes])
        dpair = dpair + dot_nt(xs_low[:, lanes], g_low[:, lanes]) * fade
    prior = states_ref[0]
    after = carry_ref[...]
    after_low = after.astype(BF16)
    from_tail = dot_nn(entry, after_low) * tail_wide
    dxs = dxs_ref[...] + from_tail
    g_into = (g * into_wide).astype(BF16)
    dpair_low = dpair.astype(BF16)
    dreadout = dot_tn(dpair_low, entry) + dot_nt(g_into, prior.astype(BF16))
    dentry = dot_nn(dpair_low, readout) + dot_nt((xs * tail_wide).astype(BF16), after_low)
    keep = into_wide[Q - 1:Q, :]
    carry_ref[...] = after * keep + dot_tn(readout, g_into)
    xs_round = xs_low.astype(F32)
    end_sum = column_sum(xs_round * from_tail) + keep * column_sum(after * prior)
    sums = exact_nt(
        jnp.concatenate([g_low.astype(F32) * y - xs_round * dxs, x * dxs], axis=0), spread
    )
    end_heads = exact_nt(jnp.broadcast_to(end_sum, (8, width)), spread)[0:1, :]
    last_row = lax.broadcasted_iota(jnp.int32, (Q, STATE), 0) == Q - 1
    dcum = sums[:Q] + jnp.where(last_row, end_heads, 0.0)
    ddecay = exact_nn(jnp.where(row <= col, 1.0, 0.0), dcum)
    dsize = sums[Q:] - ddecay * rate
    draw = dsize * jax.nn.sigmoid(raw)
    dhead_ref[0:1, :] += column_sum(draw)
    dhead_ref[1:2, :] += column_sum(ddecay * decay)
    dz = (size_wide * dxs + skip * g) * silu_slope(z, sig_z)
    dz_ref[0:Q, :] = dz
    for k in range(4):
        dcw_ref[3 - k:4 - k, :] += column_sum(dz * z_rows[k])
    dinner_ref[...] = lead_sum(dz_ref, masks, cw_ref[...]).astype(BF16)
    dz_ref[Q:Q + HALO, :] = dz_ref[0:HALO, :]
    dzs = jnp.concatenate([dentry, dreadout], axis=1) * silu_slope(zs, sig_zs)
    dzs_ref[0:Q, :] = dzs
    for k in range(4):
        dsw_ref[3 - k:4 - k, :] += column_sum(dzs * zs_rows[k])
    dss_ref[:, :2 * STATE] = lead_sum(dzs_ref, masks, sw_ref[...]).astype(BF16)
    dzs_ref[Q:Q + HALO, :] = dzs_ref[0:HALO, :]
    dss_ref[:, 2 * STATE:] = draw.astype(BF16)


def mix_bwd(seg_col, seg_rows, masks, pre, y, states, dout, cw, sw, bias, rate, skip, spread, heads):
    rows, width = pre.shape[0], cw.shape[1]
    seqs = rows // LEN
    per = LEN // Q
    pre_width = pre.shape[1]
    at = lambda s, c: s * per + per - 1 - c
    blk = lambda w: pl.BlockSpec((Q, w), lambda s, c: (at(s, c), 0))
    prev = lambda w: pl.BlockSpec(
        (HALO, w), lambda s, c: (jnp.maximum(at(s, c) * (Q // HALO) - 1, 0), 0))
    whole = lambda shape: pl.BlockSpec(shape, lambda s, c: (0, 0))
    return pl.pallas_call(
        functools.partial(mix_bwd_kernel, heads),
        grid=(seqs, per),
        in_specs=[
            blk(1),
            pl.BlockSpec((1, 1, Q), lambda s, c: (at(s, c), 0, 0)),
            blk(8), blk(pre_width), prev(pre_width), blk(width),
            pl.BlockSpec((1, STATE, width), lambda s, c: (at(s, c), 0, 0)),
            blk(width),
            whole(cw.shape), whole(sw.shape), whole(bias.shape), whole(rate.shape),
            whole(skip.shape), whole(spread.shape),
        ],
        out_specs=[
            blk(pre_width),
            whole((4, width)), whole((4, 2 * STATE)), whole((8, STATE)), whole((1, width)),
        ],
        out_shape=[
            jax.ShapeDtypeStruct((rows, pre_width), BF16),
            jax.ShapeDtypeStruct((4, width), F32),
            jax.ShapeDtypeStruct((4, 2 * STATE), F32),
            jax.ShapeDtypeStruct((8, STATE), F32),
            jax.ShapeDtypeStruct((1, width), F32),
        ],
        scratch_shapes=[
            pltpu.VMEM((STATE, width), F32),
            pltpu.VMEM((Q + HALO, width), F32),
            pltpu.VMEM((Q + HALO, 2 * STATE), F32),
            pltpu.VMEM((Q, width), F32),
            pltpu.VMEM((Q + HALO, width), F32),
            pltpu.VMEM((Q + HALO, 2 * STATE), F32),
        ],
        compiler_params=pltpu.CompilerParams(vmem_limit_bytes=VMEM_BYTES),
        cost_estimate=pl.CostEstimate(
            flops=rows * width * 3000, bytes_accessed=rows * width * 28,
            transcendentals=rows * width * 4),
        name="mix_bwd",
    )(seg_col, seg_rows, masks, pre, pre, y, states, dout, cw, sw, bias,
      rate, skip, spread)


NORM_EPS = 1e-05
ROPE_THETA = 100000000000.0
KV_HEADS = 2
HEADS = 8
LANES = 128


def permute_bit(x, axis, bit):
    n = lax.axis_size(axis)
    return lax.ppermute(x, axis, [(i, i ^ bit) for i in range(n)])


def bit_orders(axis):
    n = lax.axis_size(axis)
    bits = [n >> (k + 1) for k in range(n.bit_length() - 1)]
    rest = bits[1:]
    turn = lambda j: rest[j % len(rest):] + rest[:j % len(rest)] if rest else []
    return [bits[:1] + turn(j) for j in range(3)]


def gather_rel(piece, axis, order):
    held = piece[None]
    places = [0]
    for bit in order:
        held = jnp.concatenate([held, permute_bit(held, axis, bit)], axis=0)
        places = places + [p ^ bit for p in places]
    return held, places


def assemble_kernel(plan, count, me_ref, *refs):
    sources = refs[:len(plan)]
    dests = refs[len(plan):len(plan) + count]
    sems = refs[-1]
    copies = []
    for j, (places, dest, row_off, lane_off, block_rows) in enumerate(plan):
        rows, width = sources[j].shape[1:]
        for p, place in enumerate(places):
            start = pl.multiple_of((me_ref[0] ^ place) * block_rows + row_off, 16)
            copies.append(pltpu.make_async_copy(
                sources[j].at[p],
                dests[dest].at[pl.ds(start, rows), pl.ds(lane_off, width)],
                sems.at[j, p]))
    for copy in copies:
        copy.start()
    for copy in copies:
        copy.wait()


def assemble(me, rels, plan, shapes):
    hbm = pl.BlockSpec(memory_space=pl.ANY)
    return pl.pallas_call(
        functools.partial(assemble_kernel, plan, len(shapes)),
        grid_spec=pltpu.PrefetchScalarGridSpec(
            num_scalar_prefetch=1,
            grid=(1,),
            in_specs=[hbm] * len(rels),
            out_specs=[hbm] * len(shapes),
            scratch_shapes=[pltpu.SemaphoreType.DMA((len(rels), rels[0].shape[0]))],
        ),
        out_shape=[jax.ShapeDtypeStruct(s, BF16) for s in shapes],
        compiler_params=pltpu.CompilerParams(vmem_limit_bytes=4 * 1024 * 1024),
        cost_estimate=pl.CostEstimate(
            flops=0, bytes_accessed=sum(4 * s[0] * s[1] for s in shapes), transcendentals=0),
        name="assemble",
    )(me, *rels)


def thirds(width):
    cuts = [0] + [min(width, -(-width * k // (3 * LANES)) * LANES) for k in (1, 2)] + [width]
    return [(a, b) for a, b in zip(cuts, cuts[1:]) if b > a]


def reduce_cube(part, axis, order, row_off, row_count):
    n = lax.axis_size(axis)
    me = lax.axis_index(axis)
    levels = n.bit_length() - 1
    own = part.shape[0] // n
    cur = part.reshape((2,) * levels + (own, part.shape[1]))
    if (row_off, row_count) != (0, own):
        cur = lax.slice_in_dim(cur, row_off, row_off + row_count, axis=levels)
    for bit in reversed(order):
        dim = levels - bit.bit_length()
        mine = (me // bit) % 2
        keep = lax.dynamic_slice_in_dim(cur, mine, 1, dim)
        send = lax.dynamic_slice_in_dim(cur, 1 - mine, 1, dim)
        total = keep.astype(F32) + permute_bit(send.astype(BF16), axis, bit).astype(F32)
        cur = total.astype(BF16) if bit != order[0] else total
    return cur.reshape(row_count, part.shape[1])


def sum_cube(x, axis):
    n = lax.axis_size(axis)
    bit = 1
    while bit < n:
        x = (x.astype(F32) + permute_bit(x, axis, bit).astype(F32)).astype(x.dtype)
        bit *= 2
    return x


def tensor_gather(x, natural):
    n = lax.axis_size("tensor")
    rank = lax.axis_index("tensor")
    bit = 1
    while bit < n:
        other = permute_bit(x, "tensor", bit)
        if natural:
            low = (rank // bit) % 2 == 0
            x = jnp.concatenate([jnp.where(low, x, other), jnp.where(low, other, x)], axis=0)
        else:
            x = jnp.concatenate([x, other], axis=0)
        bit *= 2
    return x


def tensor_scatter(x, natural):
    bit = lax.axis_size("tensor") // 2
    rank = lax.axis_index("tensor")
    while bit >= 1:
        half = x.shape[0] // 2
        if natural:
            mine = (rank // bit) % 2
            keep = lax.dynamic_slice_in_dim(x, mine * half, half, 0)
            send = lax.dynamic_slice_in_dim(x, (1 - mine) * half, half, 0)
        else:
            keep, send = x[:half], x[half:]
        x = keep.astype(F32) + permute_bit(send.astype(BF16), "tensor", bit).astype(F32)
        bit //= 2
    return x


def inverse_rms(v):
    return lax.rsqrt(jnp.mean(v * v, axis=-1, keepdims=True) + NORM_EPS)


def norm_back(v, inverse, gain, grad):
    u = grad * gain
    into = inverse * u - inverse ** 3 * v * jnp.mean(u * v, axis=-1, keepdims=True)
    return into, jnp.sum(grad * v * inverse, axis=0)


def rope_tables():
    half = HEAD_DIM // 2
    frequency = jnp.exp(jnp.arange(half, dtype=F32) * (-2.0 * math.log(ROPE_THETA) / HEAD_DIM))
    angles = jnp.arange(LEN, dtype=jnp.int32).astype(F32)[:, None] * frequency[None, :]
    return jnp.tile(jnp.cos(angles), (1, 2)), jnp.tile(jnp.sin(angles), (1, 2))


def turn_columns(weights):
    rows, width = weights.shape
    halves = weights.reshape(rows, width // HEAD_DIM, 2, HEAD_DIM // 2)
    return jnp.stack([-halves[:, :, 1], halves[:, :, 0]], axis=2).reshape(rows, width)


def per_device(
    layer_input, segment_ids, out_grad, norm_gain, query_w, key_w, value_w, out_w, mamba_gate_w,
    mamba_in_w, state_in_w, step_w, channel_conv, state_conv, step_bias, decay_log, skip_gain,
    mamba_out_w, ffn_gain, ffn_gate_w, ffn_up_w, ffn_down_w,
):
    dp = lax.axis_size("dp")
    rank = lax.axis_index("tensor")
    me = lax.axis_index("dp").astype(jnp.int32).reshape(1)
    heads = query_w.shape[1] // HEAD_DIM
    ssm = step_w.shape[1]
    width = mamba_in_w.shape[1]
    q_width = query_w.shape[1]
    units = ffn_gate_w.shape[1]
    kv_index = rank * heads // (HEADS // KV_HEADS)
    features = layer_input.shape[1]
    block_rows = query_w.shape[0]
    half_rows = block_rows // 2
    orders = bit_orders("dp")

    key_own = lax.dynamic_slice_in_dim(key_w, kv_index * HEAD_DIM, HEAD_DIM, 1)
    value_own = lax.dynamic_slice_in_dim(value_w, kv_index * HEAD_DIM, HEAD_DIM, 1)
    qkv_shard = jnp.concatenate([query_w, key_own, value_own], axis=1)
    mix_shard = jnp.concatenate(
        [mamba_gate_w, mamba_in_w, state_in_w, jnp.pad(step_w, ((0, 0), (0, STATE - ssm)))], axis=1)
    total_cols = mix_shard.shape[1] + qkv_shard.shape[1]
    mix_cols = thirds(total_cols)
    mix_cols = [(a, min(b, mix_shard.shape[1])) for a, b in mix_cols if a < mix_shard.shape[1]]
    rels, plan = [], []
    for j, (a, b) in enumerate(mix_cols):
        rel, places = gather_rel(mix_shard[:, a:b], "dp", orders[j])
        rels.append(rel)
        plan.append((places, 0, 0, a, block_rows))
    rel, places = gather_rel(qkv_shard, "dp", orders[2])
    rels.append(rel)
    plan.append((places, 1, 0, 0, block_rows))
    mix_w, qkv_w = assemble(me, rels, plan, [(features, mix_shard.shape[1]),
                                            (features, qkv_shard.shape[1])])

    later = (out_w.T, mamba_out_w.T, ffn_gate_w, ffn_up_w, ffn_down_w.T)
    later, rels = lax.optimization_barrier((later, tuple(rels)))
    out_shard, mout_shard, gate_shard, up_shard, down_shard = later
    rels2, plan2 = [], []
    for piece, dest, row_off, order in (
        (mout_shard[:half_rows], 1, 0, 0), (mout_shard[half_rows:], 1, half_rows, 1),
        (out_shard, 0, 0, 2),
    ):
        rel, places = gather_rel(piece, "dp", orders[order])
        rels2.append(rel)
        plan2.append((places, dest, row_off, 0, block_rows))
    out_t, mout_t = assemble(me, rels2, plan2, [(features, q_width), (features, width)])
    rels3, plan3 = [], []
    for j, piece in enumerate((gate_shard, up_shard, down_shard)):
        rel, places = gather_rel(piece, "dp", orders[j])
        rels3.append(rel)
        plan3.append((places, j, 0, 0, block_rows))
    ffn_gate, ffn_up, ffn_down_t = assemble(me, rels3, plan3, [(features, units)] * 3)

    tokens = layer_input.astype(F32)
    inverse = inverse_rms(tokens)
    normed = tensor_gather((tokens * inverse * norm_gain).astype(BF16), True)
    top_grad = tensor_gather(out_grad, False)
    rows = normed.shape[0]
    seqs = rows // LEN

    seg = segment_ids.reshape(seqs, LEN)
    seg_col = segment_ids[:, None]
    masks = token_masks(seg)
    starts = jnp.sum(seg[:, None, :] < seg[:, ::BQ, None], axis=-1, dtype=jnp.int32)
    first = (starts // BQ).reshape(-1)
    cos, sin = rope_tables()

    turned = turn_columns(qkv_w[:, :q_width + HEAD_DIM])
    qkv = dot_nn(normed, qkv_w)
    qk_turned = dot_nn(normed, turned)
    cos_rows = jnp.tile(cos, (seqs, heads + 1))
    sin_rows = jnp.tile(sin, (seqs, heads + 1))
    qk = (qkv[:, :q_width + HEAD_DIM] * cos_rows + qk_turned * sin_rows).astype(BF16)
    queries = qk[:, :q_width]
    key_rows = qk[:, q_width:]
    value_rows = qkv[:, q_width + HEAD_DIM:].astype(BF16)
    attended, lse = attend_fwd(
        first, queries, key_rows, value_rows, seg_col, segment_ids.reshape(seqs, LEN // BQ, BQ))

    pre = dot_nn(normed, mix_w)
    pad_heads = lambda a: jnp.pad(a[None], ((0, 0), (0, STATE - ssm)))
    bias, rate = pad_heads(step_bias), pad_heads(decay_log)
    skip = jnp.repeat(skip_gain, HEAD_DIM)[None]
    spread = jnp.pad(jnp.repeat(jnp.eye(ssm, dtype=F32), HEAD_DIM, axis=1), ((0, STATE - ssm), (0, 0)))
    chunk_rows = segment_ids.reshape(-1, 1, Q)
    gated, scanned, states = mix_fwd(
        seg_col, chunk_rows, masks, pre, channel_conv, state_conv, bias, rate, skip, spread, ssm)

    branch = tensor_scatter(dot_nt(attended, out_t) + dot_nt(gated, mout_t), True)
    middle = tokens + branch
    mid_inverse = inverse_rms(middle)
    mid = tensor_gather((middle * mid_inverse * ffn_gain).astype(BF16), False)
    gate_vals = dot_nn(mid, ffn_gate)
    up_vals = dot_nn(mid, ffn_up)
    act = (jax.nn.silu(gate_vals) * up_vals).astype(BF16)
    block_out = (middle + tensor_scatter(dot_nt(act, ffn_down_t), False)).astype(BF16)

    act_grad = dot_nn(top_grad, ffn_down_t)
    gate_sig = jax.nn.sigmoid(gate_vals)
    gate_grad = (act_grad * up_vals * silu_slope(gate_vals, gate_sig)).astype(BF16)
    up_grad = (act_grad * (gate_vals * gate_sig)).astype(BF16)
    mid_norm_grad = tensor_scatter(dot_nt(gate_grad, ffn_gate) + dot_nt(up_grad, ffn_up), False)
    down_part = dot_tn(top_grad, act).astype(BF16)
    gate_part = dot_tn(mid, gate_grad).astype(BF16)
    up_part = dot_tn(mid, up_grad).astype(BF16)
    ffn_down_w_grad = reduce_cube(down_part, "dp", orders[0], 0, block_rows).T
    ffn_gate_w_grad = reduce_cube(gate_part, "dp", orders[1], 0, block_rows)
    ffn_up_w_grad = reduce_cube(up_part, "dp", orders[2], 0, block_rows)

    mid_into, ffn_gain_part = norm_back(middle, mid_inverse, ffn_gain, mid_norm_grad)
    middle_grad = out_grad.astype(F32) + mid_into
    branch_grad = tensor_gather(middle_grad.astype(BF16), True)
    attended_grad = dot_nn(branch_grad, out_t).astype(BF16)
    gated_grad = dot_nn(branch_grad, mout_t)
    out_part = dot_tn(branch_grad, attended).astype(BF16)
    mout_part = dot_tn(branch_grad, gated).astype(BF16)
    out_w_grad = reduce_cube(out_part, "dp", orders[2], 0, block_rows).T
    mamba_out_w_grad = jnp.concatenate([
        reduce_cube(mout_part, "dp", orders[0], 0, half_rows),
        reduce_cube(mout_part, "dp", orders[1], half_rows, half_rows)], axis=0).T

    by_block = lambda a: a.reshape(rows // BQ, BQ, heads).transpose(0, 2, 1)
    delta = jnp.sum((attended_grad.astype(F32) * attended.astype(F32)).reshape(rows, heads, HEAD_DIM),
                    axis=-1)
    query_grad, key_grad, value_grad = attend_bwd(
        first, queries, key_rows, value_rows, attended_grad, seg_col,
        segment_ids.reshape(-1, 1, BQ), by_block(lse), by_block(delta), cos, sin)
    qkv_grad = jnp.concatenate([query_grad, key_grad, value_grad], axis=1)
    mix_grad, conv_part, state_conv_part, head_part, skip_part = mix_bwd(
        seg_col, chunk_rows, masks, pre, scanned, states, gated_grad, channel_conv, state_conv, bias,
        rate, skip, spread, ssm)

    qkv_part = dot_tn(normed, qkv_grad).astype(BF16)
    mix_part = dot_tn(normed, mix_grad).astype(BF16)
    qkv_sum = reduce_cube(qkv_part, "dp", orders[2], 0, block_rows)
    mix_sum = jnp.concatenate([
        reduce_cube(mix_part[:, a:b], "dp", orders[j], 0, block_rows)
        for j, (a, b) in enumerate(mix_cols)], axis=1)
    normed_grad = tensor_scatter(dot_nt(qkv_grad, qkv_w) + dot_nt(mix_grad, mix_w), True)
    norm_into, norm_gain_part = norm_back(tokens, inverse, norm_gain, normed_grad)
    input_grad = middle_grad + norm_into

    place = lambda a, whole: lax.dynamic_update_slice_in_dim(
        jnp.zeros((block_rows, whole.shape[1]), BF16), a.astype(BF16), kv_index * HEAD_DIM, 1)
    shared = sum_cube(jnp.concatenate([
        place(qkv_sum[:, q_width:q_width + HEAD_DIM], key_w),
        place(qkv_sum[:, q_width + HEAD_DIM:], value_w),
        mix_sum[:, 2 * width:2 * width + 2 * STATE].astype(BF16)], axis=1), "tensor").astype(F32)
    kv_cols = key_w.shape[1]

    heads_part = jnp.concatenate([
        head_part[0, :ssm], head_part[1, :ssm],
        jnp.sum(skip_part.reshape(ssm, HEAD_DIM), axis=1)])
    small = jnp.concatenate([
        conv_part.reshape(-1), heads_part, state_conv_part.reshape(-1), ffn_gain_part])
    small = sum_cube(small, "dp")
    gain = sum_cube(sum_cube(norm_gain_part, "dp"), "tensor")
    own = 4 * width
    conv_grad = small[:own].reshape(4, width)
    bias_grad, decay_grad, skip_grad = (small[own + k * ssm:own + (k + 1) * ssm] for k in range(3))
    both = sum_cube(small[own + 3 * ssm:], "tensor")
    state_conv_grad = both[:8 * STATE].reshape(4, 2 * STATE)
    ffn_gain_grad = both[8 * STATE:]
    return (
        block_out,
        input_grad,
        gain,
        qkv_sum[:, :q_width],
        shared[:, :kv_cols],
        shared[:, kv_cols:2 * kv_cols],
        out_w_grad,
        mix_sum[:, :width],
        mix_sum[:, width:2 * width],
        shared[:, 2 * kv_cols:],
        mix_sum[:, 2 * width + 2 * STATE:2 * width + 2 * STATE + ssm],
        conv_grad,
        state_conv_grad,
        bias_grad,
        decay_grad,
        skip_grad,
        mamba_out_w_grad,
        ffn_gain_grad,
        ffn_gate_w_grad,
        ffn_up_w_grad,
        ffn_down_w_grad,
    )


def solution(mesh):
    in_specs = (
        P(("dp", "tensor"), None),
        P("dp"),
        P(("dp", "tensor"), None),
        P(),
        P("dp", "tensor"),
        P("dp", None),
        P("dp", None),
        P("tensor", "dp"),
        P("dp", "tensor"),
        P("dp", "tensor"),
        P("dp", None),
        P("dp", "tensor"),
        P(None, "tensor"),
        P(),
        P("tensor"),
        P("tensor"),
        P("tensor"),
        P("tensor", "dp"),
        P(),
        P("dp", "tensor"),
        P("dp", "tensor"),
        P("tensor", "dp"),
    )
    out_specs = (
        P(("dp", "tensor"), None),
        P(("dp", "tensor"), None),
        P(),
        P("dp", "tensor"),
        P("dp", None),
        P("dp", None),
        P("tensor", "dp"),
        P("dp", "tensor"),
        P("dp", "tensor"),
        P("dp", None),
        P("dp", "tensor"),
        P(None, "tensor"),
        P(),
        P("tensor"),
        P("tensor"),
        P("tensor"),
        P("tensor", "dp"),
        P(),
        P("dp", "tensor"),
        P("dp", "tensor"),
        P("tensor", "dp"),
    )
    return jax.shard_map(
        per_device, mesh=mesh, in_specs=in_specs, out_specs=out_specs, check_vma=False
    )
```

```python
import functools
import math

import jax
import jax.numpy as jnp
from jax import lax
from jax.experimental import pallas as pl
from jax.experimental.pallas import tpu as pltpu
from jax.sharding import PartitionSpec as P

HEAD_DIM = 64
STATE = 128
LEN = 2048
BQ = 512
Q = 128
HALO = 8
NEG = -1e30
PRECISE = lax.Precision.HIGHEST
F32 = jnp.float32
BF16 = jnp.bfloat16
VMEM_BYTES = 48 * 1024 * 1024


def dot_nn(left, right):
    return lax.dot_general(left, right, (((1,), (0,)), ((), ())), preferred_element_type=F32)


def dot_nt(left, right):
    return lax.dot_general(left, right, (((1,), (1,)), ((), ())), preferred_element_type=F32)


def dot_tn(left, right):
    return lax.dot_general(left, right, (((0,), (0,)), ((), ())), preferred_element_type=F32)


def pieces(a, count):
    parts = []
    for _ in range(count):
        parts.append(a.astype(BF16))
        a = a - parts[-1].astype(F32)
    return parts


def rope_kernel(heads, qkv_ref, cos_ref, sin_ref, q_ref, k_ref, v_ref):
    half = HEAD_DIM // 2
    cos, sin = cos_ref[...], sin_ref[...]

    def turn(x):
        return x * cos + jnp.concatenate([-x[:, half:], x[:, :half]], axis=1) * sin

    for h in range(heads):
        lanes = slice(h * HEAD_DIM, (h + 1) * HEAD_DIM)
        q_ref[:, lanes] = (turn(qkv_ref[:, lanes]).astype(BF16) * HEAD_DIM ** -0.5).astype(BF16)
    edge = heads * HEAD_DIM
    k_ref[...] = turn(qkv_ref[:, edge:edge + HEAD_DIM]).astype(BF16)
    v_ref[:, :HEAD_DIM] = qkv_ref[:, edge + HEAD_DIM:].astype(BF16)
    v_ref[:, HEAD_DIM:] = jnp.ones((v_ref.shape[0], HEAD_DIM), BF16)


def rope(qkv, cos, sin):
    rows, width = qkv.shape
    heads = width // HEAD_DIM - 2
    per = LEN // BQ
    blk = lambda w: pl.BlockSpec((BQ, w), lambda i: (i, 0))
    table = pl.BlockSpec((BQ, HEAD_DIM), lambda i: (lax.rem(i, per), 0))
    return pl.pallas_call(
        functools.partial(rope_kernel, heads),
        grid=(rows // BQ,),
        in_specs=[blk(width), table, table],
        out_specs=[blk(heads * HEAD_DIM), blk(HEAD_DIM), blk(2 * HEAD_DIM)],
        out_shape=[
            jax.ShapeDtypeStruct((rows, heads * HEAD_DIM), BF16),
            jax.ShapeDtypeStruct((rows, HEAD_DIM), BF16),
            jax.ShapeDtypeStruct((rows, 2 * HEAD_DIM), BF16),
        ],
        compiler_params=pltpu.CompilerParams(vmem_limit_bytes=VMEM_BYTES),
        cost_estimate=pl.CostEstimate(
            flops=rows * width * 8, bytes_accessed=rows * width * 6, transcendentals=0),
        name="rope",
    )(qkv, cos, sin)


def attend_fwd_kernel(heads, first_ref, q_ref, k_ref, v_ref, seg_ref, segrow_ref, out_ref, lse_ref,
                      top_ref, acc_ref):
    seq = pl.program_id(0)
    block = pl.program_id(1)
    top_ref[...] = jnp.full_like(top_ref, NEG)
    acc_ref[...] = jnp.zeros_like(acc_ref)
    key_pos = lax.broadcasted_iota(jnp.int32, (BQ, BQ), 0)
    row_pos = lax.broadcasted_iota(jnp.int32, (BQ, BQ), 1)

    def step(j, carry):
        at = pl.ds(pl.multiple_of(j * BQ, BQ), BQ)
        k = k_ref[at, :]
        v = v_ref[at, :]
        allowed = (segrow_ref[0] == seg_ref[at, :]) & (key_pos + (j - block) * BQ <= row_pos)
        bias = jnp.where(allowed, 0.0, NEG)
        for h in range(heads):
            s = dot_nt(k, q_ref[:, h * HEAD_DIM:(h + 1) * HEAD_DIM]) + bias
            old = top_ref[h]
            new = jnp.maximum(old, jnp.max(s, axis=0, keepdims=True))
            shrink = jnp.broadcast_to(jnp.exp(old - new), (2 * HEAD_DIM, BQ)).T
            p = jnp.exp(s - new).astype(BF16)
            acc_ref[h] = acc_ref[h] * shrink + dot_tn(p, v)
            top_ref[h] = new
        return carry

    lax.fori_loop(first_ref[seq * (LEN // BQ) + block], block + 1, step, 0)
    for h in range(heads):
        acc = acc_ref[h]
        out_ref[:, h * HEAD_DIM:(h + 1) * HEAD_DIM] = (
            acc[:, :HEAD_DIM] / acc[:, HEAD_DIM:]).astype(BF16)
        lse_ref[0, h:h + 1, :] = top_ref[h] + jnp.log(acc.T[HEAD_DIM:HEAD_DIM + 1, :])


def attend_fwd(first, q, k, v, seg_col, seg_rows):
    rows, width = q.shape
    heads = width // HEAD_DIM
    seqs = rows // LEN
    per = LEN // BQ
    return pl.pallas_call(
        functools.partial(attend_fwd_kernel, heads),
        grid_spec=pltpu.PrefetchScalarGridSpec(
            num_scalar_prefetch=1,
            grid=(seqs, per),
            in_specs=[
                pl.BlockSpec((BQ, width), lambda s, i, f: (s * per + i, 0)),
                pl.BlockSpec((LEN, HEAD_DIM), lambda s, i, f: (s, 0)),
                pl.BlockSpec((LEN, 2 * HEAD_DIM), lambda s, i, f: (s, 0)),
                pl.BlockSpec((LEN, 1), lambda s, i, f: (s, 0)),
                pl.BlockSpec((1, 1, BQ), lambda s, i, f: (s * per + i, 0, 0)),
            ],
            out_specs=[
                pl.BlockSpec((BQ, width), lambda s, i, f: (s * per + i, 0)),
                pl.BlockSpec((1, heads, BQ), lambda s, i, f: (s * per + i, 0, 0)),
            ],
            scratch_shapes=[
                pltpu.VMEM((heads, 1, BQ), F32),
                pltpu.VMEM((heads, BQ, 2 * HEAD_DIM), F32),
            ],
        ),
        out_shape=[
            jax.ShapeDtypeStruct((rows, width), BF16),
            jax.ShapeDtypeStruct((seqs * per, heads, BQ), F32),
        ],
        compiler_params=pltpu.CompilerParams(vmem_limit_bytes=VMEM_BYTES),
        cost_estimate=pl.CostEstimate(
            flops=2 * rows * LEN * width, bytes_accessed=4 * rows * width,
            transcendentals=rows * LEN * heads // 2),
        name="attend_fwd",
    )(first, q, k, v, seg_col, seg_rows)


def attend_bwd_kernel(heads, first_ref, q_ref, k_ref, v_ref, g_ref, seg_ref, segrow_ref, lse_ref,
                      out_ref, cos_ref, sin_ref, cosk_ref, sink_ref, dq_ref, dk_ref, dv_ref,
                      dqs_ref, dks_ref, dvs_ref, delta_ref):
    seq = pl.program_id(0)
    block = pl.program_id(1)
    half = HEAD_DIM // 2
    scale = HEAD_DIM ** -0.5

    @pl.when(block == 0)
    def _():
        dks_ref[...] = jnp.zeros_like(dks_ref)
        dvs_ref[...] = jnp.zeros_like(dvs_ref)

    dqs_ref[...] = jnp.zeros_like(dqs_ref)
    ones = jnp.ones((16, HEAD_DIM), BF16)
    high, less = pieces(g_ref[...].astype(F32) * out_ref[...].astype(F32), 2)
    for h in range(heads):
        lanes = slice(h * HEAD_DIM, (h + 1) * HEAD_DIM)
        delta_ref[h] = (dot_nt(ones, high[:, lanes]) + dot_nt(ones, less[:, lanes]))[0:1, :]
    key_pos = lax.broadcasted_iota(jnp.int32, (BQ, BQ), 0)
    row_pos = lax.broadcasted_iota(jnp.int32, (BQ, BQ), 1)

    def step(j, carry):
        at = pl.ds(pl.multiple_of(j * BQ, BQ), BQ)
        k = k_ref[at, :]
        v = v_ref[at, :HEAD_DIM]
        allowed = (segrow_ref[0] == seg_ref[at, :]) & (key_pos + (j - block) * BQ <= row_pos)
        bias = jnp.where(allowed, 0.0, NEG)
        dk = jnp.zeros((BQ, HEAD_DIM), F32)
        dv = jnp.zeros((BQ, HEAD_DIM), F32)
        for h in range(heads):
            lanes = slice(h * HEAD_DIM, (h + 1) * HEAD_DIM)
            q = q_ref[:, lanes]
            g = g_ref[:, lanes]
            s = dot_nt(k, q) + bias
            p = jnp.exp(s - lse_ref[0, h:h + 1, :])
            dp = dot_nt(v, g)
            ds = (p * (dp - delta_ref[h])).astype(BF16)
            dv = dv + dot_nn(p.astype(BF16), g)
            dk = dk + dot_nn(ds, q)
            dqs_ref[h] = dqs_ref[h] + dot_tn(ds, k)
        dks_ref[at, :] = dks_ref[at, :] + dk
        dvs_ref[at, :] = dvs_ref[at, :] + dv
        return carry

    lax.fori_loop(first_ref[seq * (LEN // BQ) + block], block + 1, step, 0)

    def turn_back(x, cos, sin):
        swapped = jnp.concatenate([x[:, half:], -x[:, :half]], axis=1)
        return x * cos + swapped * sin

    for h in range(heads):
        dq = turn_back(dqs_ref[h] * scale, cos_ref[...], sin_ref[...])
        dq_ref[:, h * HEAD_DIM:(h + 1) * HEAD_DIM] = dq.astype(BF16)

    @pl.when(block == pl.num_programs(1) - 1)
    def _():
        dk_ref[...] = turn_back(dks_ref[...], cosk_ref[...], sink_ref[...]).astype(BF16)
        dv_ref[...] = dvs_ref[...].astype(BF16)


def attend_bwd(first, q, k, v, g, seg_col, seg_rows, lse_rows, attended, cos, sin):
    rows, width = q.shape
    heads = width // HEAD_DIM
    seqs = rows // LEN
    per = LEN // BQ
    return pl.pallas_call(
        functools.partial(attend_bwd_kernel, heads),
        grid_spec=pltpu.PrefetchScalarGridSpec(
            num_scalar_prefetch=1,
            grid=(seqs, per),
            in_specs=[
                pl.BlockSpec((BQ, width), lambda s, i, f: (s * per + i, 0)),
                pl.BlockSpec((LEN, HEAD_DIM), lambda s, i, f: (s, 0)),
                pl.BlockSpec((LEN, 2 * HEAD_DIM), lambda s, i, f: (s, 0)),
                pl.BlockSpec((BQ, width), lambda s, i, f: (s * per + i, 0)),
                pl.BlockSpec((LEN, 1), lambda s, i, f: (s, 0)),
                pl.BlockSpec((1, 1, BQ), lambda s, i, f: (s * per + i, 0, 0)),
                pl.BlockSpec((1, heads, BQ), lambda s, i, f: (s * per + i, 0, 0)),
                pl.BlockSpec((BQ, width), lambda s, i, f: (s * per + i, 0)),
                pl.BlockSpec((BQ, HEAD_DIM), lambda s, i, f: (i, 0)),
                pl.BlockSpec((BQ, HEAD_DIM), lambda s, i, f: (i, 0)),
                pl.BlockSpec((LEN, HEAD_DIM), lambda s, i, f: (0, 0)),
                pl.BlockSpec((LEN, HEAD_DIM), lambda s, i, f: (0, 0)),
            ],
            out_specs=[
                pl.BlockSpec((BQ, width), lambda s, i, f: (s * per + i, 0)),
                pl.BlockSpec((LEN, HEAD_DIM), lambda s, i, f: (s, 0)),
                pl.BlockSpec((LEN, HEAD_DIM), lambda s, i, f: (s, 0)),
            ],
            scratch_shapes=[
                pltpu.VMEM((heads, BQ, HEAD_DIM), F32),
                pltpu.VMEM((LEN, HEAD_DIM), F32),
                pltpu.VMEM((LEN, HEAD_DIM), F32),
                pltpu.VMEM((heads, 1, BQ), F32),
            ],
        ),
        out_shape=[
            jax.ShapeDtypeStruct((rows, width), BF16),
            jax.ShapeDtypeStruct((rows, HEAD_DIM), BF16),
            jax.ShapeDtypeStruct((rows, HEAD_DIM), BF16),
        ],
        compiler_params=pltpu.CompilerParams(vmem_limit_bytes=VMEM_BYTES),
        cost_estimate=pl.CostEstimate(
            flops=5 * rows * LEN * width, bytes_accessed=8 * rows * width,
            transcendentals=rows * LEN * heads // 2),
        name="attend_bwd",
    )(first, q, k, v, g, seg_col, seg_rows, lse_rows, attended, cos, sin, cos, sin)


LAG, LEAD, CARRIED, ENDING = 0, 3, 6, 7


def token_masks(seg):
    seqs = seg.shape[0]
    padded = jnp.pad(seg, ((0, 0), (3, 3)), constant_values=-1)
    columns = [padded[:, 3 - k:3 - k + LEN] == seg for k in (1, 2, 3)]
    columns += [padded[:, 3 + k:3 + k + LEN] == seg for k in (1, 2, 3)]
    chunks = seg.reshape(seqs, LEN // Q, Q)
    prior = jnp.pad(chunks[:, :-1, -1:], ((0, 0), (1, 0), (0, 0)), constant_values=-1)
    columns.append((chunks == prior).reshape(seqs, LEN))
    columns.append((chunks == chunks[:, :, -1:]).reshape(seqs, LEN))
    return jnp.stack(columns, axis=-1).astype(F32).reshape(seqs * LEN, 8)


def shifted_conv(buf_ref, width, masks, taps):
    rows = [buf_ref[HALO - k:HALO - k + Q, :width] for k in range(4)]
    rows = [rows[0]] + [rows[k] * masks[:, LAG + k - 1:LAG + k] for k in (1, 2, 3)]
    total = rows[0] * taps[3:4, :]
    for k in (1, 2, 3):
        total = total + rows[k] * taps[3 - k:4 - k, :]
    return total, rows


def softplus(x):
    return jnp.maximum(x, 0.0) + jnp.log1p(jnp.exp(-jnp.abs(x)))


def spread_heads(columns, spread):
    stack = jnp.concatenate(columns, axis=0)
    high, less = pieces(stack, 2)
    wide = dot_nn(high, spread) + dot_nn(less, spread)
    return [wide[k * Q:(k + 1) * Q] for k in range(len(columns))]


def ones_times(ones, a, count):
    width = a.shape[1]
    total = dot_nn(ones, jnp.concatenate(pieces(a, count), axis=1))
    parts = [total[:, k * width:(k + 1) * width] for k in range(count)]
    return functools.reduce(jnp.add, parts)


def chunk_masks(seg_ref, segrow_ref):
    row = lax.broadcasted_iota(jnp.int32, (Q, Q), 0)
    col = lax.broadcasted_iota(jnp.int32, (Q, Q), 1)
    same = seg_ref[...] == segrow_ref[0]
    return row, col, same


def split_pre(ref, width):
    return (ref.at[:, pl.ds(0, width)], ref.at[:, pl.ds(width, width)],
            ref.at[:, pl.ds(2 * width, 3 * STATE)])


def mix_fwd_kernel(heads, seg_ref, segrow_ref, mask_ref, pre_ref, cw_ref,
                   sw_ref, bias_ref, rate_ref, skip_ref, spread_ref, gated_ref, y_ref, states_ref,
                   carry_ref, buf_ref, sbuf_ref):
    width = y_ref.shape[1]
    gate_ref, inner_ref, ss_ref = split_pre(pre_ref, width)

    @pl.when(pl.program_id(1) == 0)
    def _():
        carry_ref[...] = jnp.zeros_like(carry_ref)
        buf_ref[0:HALO, :] = jnp.zeros((HALO, buf_ref.shape[1]), F32)
        sbuf_ref[0:HALO, :] = jnp.zeros((HALO, sbuf_ref.shape[1]), F32)

    masks = mask_ref[...]
    buf_ref[HALO:HALO + Q, :] = inner_ref[...]
    sbuf_ref[HALO:HALO + Q, :] = ss_ref[:, :2 * STATE]
    z, _ = shifted_conv(buf_ref, buf_ref.shape[1], masks, cw_ref[...])
    zs, _ = shifted_conv(sbuf_ref, 2 * STATE, masks, sw_ref[...])
    buf_ref[0:HALO, :] = buf_ref[Q:Q + HALO, :]
    sbuf_ref[0:HALO, :] = sbuf_ref[Q:Q + HALO, :]
    x = z * jax.nn.sigmoid(z)
    states = (zs * jax.nn.sigmoid(zs)).astype(BF16)
    entry = states[:, :STATE]
    readout = states[:, STATE:]
    size = softplus(ss_ref[:, 2 * STATE:] + bias_ref[...])
    decay = -size * jnp.exp(rate_ref[...])
    row, col, same = chunk_masks(seg_ref, segrow_ref)
    cum = ones_times(jnp.where(row >= col, 1.0, 0.0).astype(BF16), decay, 3)
    cum_rows = cum.T
    bias = jnp.where((row >= col) & same, 0.0, NEG)
    spread = spread_ref[...]
    into = jnp.exp(cum) * masks[:, CARRIED:CARRIED + 1]
    tail = jnp.exp(cum[Q - 1:Q, :] - cum) * masks[:, ENDING:ENDING + 1]
    size_wide, into_wide, tail_wide = spread_heads([size, into, tail], spread)
    xs = (x * size_wide)
    xs_low = xs.astype(BF16)
    pair = dot_nt(readout, entry)
    prior = carry_ref[...]
    states_ref[0] = prior
    y = dot_nn(readout, prior.astype(BF16)) * into_wide
    for h in range(heads):
        lanes = slice(h * HEAD_DIM, (h + 1) * HEAD_DIM)
        mix = (pair * jnp.exp(cum[:, h:h + 1] - cum_rows[h:h + 1, :] + bias)).astype(BF16)
        y_ref[:, lanes] = dot_nn(mix, xs_low[:, lanes])
    y = y + y_ref[...]
    y_ref[...] = y
    fresh = dot_tn(entry, (xs * tail_wide).astype(BF16))
    carry_ref[...] = prior * into_wide[Q - 1:Q, :] + fresh
    gate = gate_ref[...]
    gated_ref[...] = ((y + skip_ref[...] * x) * (gate * jax.nn.sigmoid(gate))).astype(BF16)


def mix_fwd(seg_col, seg_rows, masks, pre, cw, sw, bias, rate, skip, spread,
            heads):
    rows, width = pre.shape[0], cw.shape[1]
    seqs = rows // LEN
    per = LEN // Q
    pre_width = pre.shape[1]
    blk = lambda w: pl.BlockSpec((Q, w), lambda s, c: (s * per + c, 0))
    whole = lambda a: pl.BlockSpec(a.shape, lambda s, c: (0, 0))
    return pl.pallas_call(
        functools.partial(mix_fwd_kernel, heads),
        grid=(seqs, per),
        in_specs=[
            blk(1),
            pl.BlockSpec((1, 1, Q), lambda s, c: (s * per + c, 0, 0)),
            blk(8), blk(pre_width),
            whole(cw), whole(sw), whole(bias), whole(rate), whole(skip), whole(spread),
        ],
        out_specs=[
            blk(width), blk(width),
            pl.BlockSpec((1, STATE, width), lambda s, c: (s * per + c, 0, 0)),
        ],
        out_shape=[
            jax.ShapeDtypeStruct((rows, width), BF16),
            jax.ShapeDtypeStruct((rows, width), F32),
            jax.ShapeDtypeStruct((seqs * per, STATE, width), F32),
        ],
        scratch_shapes=[
            pltpu.VMEM((STATE, width), F32),
            pltpu.VMEM((Q + HALO, width), F32),
            pltpu.VMEM((Q + HALO, 2 * STATE), F32),
        ],
        compiler_params=pltpu.CompilerParams(vmem_limit_bytes=VMEM_BYTES),
        cost_estimate=pl.CostEstimate(
            flops=rows * width * 1200, bytes_accessed=rows * width * 22,
            transcendentals=rows * width * 4),
        name="mix_fwd",
    )(seg_col, seg_rows, masks, pre, cw, sw, bias, rate, skip, spread)


def lead_sum(buf_ref, masks, taps):
    total = buf_ref[0:Q, :] * taps[3:4, :]
    for k in (1, 2, 3):
        total = total + buf_ref[k:k + Q, :] * masks[:, LEAD + k - 1:LEAD + k] * taps[3 - k:4 - k, :]
    return total


def column_sum(a):
    return jnp.sum(a, axis=0, keepdims=True)


def silu_slope(v, sig):
    return sig * (1.0 + v * (1.0 - sig))


def mix_bwd_kernel(heads, seg_ref, segrow_ref, mask_ref, pre_ref, pre_prev_ref, y_ref, states_ref, dout_ref, cw_ref, sw_ref, bias_ref, rate_ref,
                   skip_ref, spread_ref, dpre_ref, dcw_ref, dsw_ref, dhead_ref,
                   dskip_ref, carry_ref, buf_ref, sbuf_ref, dxs_ref, dz_ref, dzs_ref):
    width = y_ref.shape[1]
    gate_ref, inner_ref, ss_ref = split_pre(pre_ref, width)
    _, inner_prev_ref, ss_prev_ref = split_pre(pre_prev_ref, width)
    dgate_ref, dinner_ref, dss_ref = split_pre(dpre_ref, width)

    @pl.when((pl.program_id(0) == 0) & (pl.program_id(1) == 0))
    def _():
        dcw_ref[...] = jnp.zeros_like(dcw_ref)
        dsw_ref[...] = jnp.zeros_like(dsw_ref)
        dhead_ref[...] = jnp.zeros_like(dhead_ref)
        dskip_ref[...] = jnp.zeros_like(dskip_ref)

    @pl.when(pl.program_id(1) == 0)
    def _():
        carry_ref[...] = jnp.zeros_like(carry_ref)
        dz_ref[Q:Q + HALO, :] = jnp.zeros((HALO, width), F32)
        dzs_ref[Q:Q + HALO, :] = jnp.zeros((HALO, 2 * STATE), F32)

    masks = mask_ref[...]
    buf_ref[0:HALO, :] = inner_prev_ref[...]
    buf_ref[HALO:HALO + Q, :] = inner_ref[...]
    sbuf_ref[0:HALO, :] = ss_prev_ref[:, :2 * STATE]
    sbuf_ref[HALO:HALO + Q, :] = ss_ref[:, :2 * STATE]
    z, z_rows = shifted_conv(buf_ref, width, masks, cw_ref[...])
    zs, zs_rows = shifted_conv(sbuf_ref, 2 * STATE, masks, sw_ref[...])
    sig_z = jax.nn.sigmoid(z)
    sig_zs = jax.nn.sigmoid(zs)
    x = z * sig_z
    states = (zs * sig_zs).astype(BF16)
    entry = states[:, :STATE]
    readout = states[:, STATE:]
    raw = ss_ref[:, 2 * STATE:] + bias_ref[...]
    size = softplus(raw)
    rate = jnp.exp(rate_ref[...])
    decay = -size * rate
    row, col, same = chunk_masks(seg_ref, segrow_ref)
    cum = ones_times(jnp.where(row >= col, 1.0, 0.0).astype(BF16), decay, 3)
    cum_rows = cum.T
    bias = jnp.where((row <= col) & same, 0.0, NEG)
    spread = spread_ref[...]
    into = jnp.exp(cum) * masks[:, CARRIED:CARRIED + 1]
    tail = jnp.exp(cum[Q - 1:Q, :] - cum) * masks[:, ENDING:ENDING + 1]
    size_wide, into_wide, tail_wide = spread_heads([size, into, tail], spread)
    xs = x * size_wide
    xs_low = xs.astype(BF16)
    gate = gate_ref[...]
    sig = jax.nn.sigmoid(gate)
    dout = dout_ref[...]
    y = y_ref[...]
    skip = skip_ref[...]
    dgate_ref[...] = (dout * (y + skip * x) * silu_slope(gate, sig)).astype(BF16)
    g = dout * (gate * sig)
    g_low = g.astype(BF16)
    dskip_ref[...] += column_sum(g * x)
    pair = dot_nt(entry, readout)
    dpair = jnp.zeros((Q, Q), F32)
    for h in range(heads):
        lanes = slice(h * HEAD_DIM, (h + 1) * HEAD_DIM)
        fade = jnp.exp(cum_rows[h:h + 1, :] - cum[:, h:h + 1] + bias)
        dxs_ref[:, lanes] = dot_nn((pair * fade).astype(BF16), g_low[:, lanes])
        dpair = dpair + dot_nt(xs_low[:, lanes], g_low[:, lanes]) * fade
    prior = states_ref[0]
    after = carry_ref[...]
    after_low = after.astype(BF16)
    from_tail = dot_nn(entry, after_low) * tail_wide
    dxs = dxs_ref[...] + from_tail
    g_into = (g * into_wide).astype(BF16)
    dpair_low = dpair.astype(BF16)
    dreadout = dot_tn(dpair_low, entry) + dot_nt(g_into, prior.astype(BF16))
    dentry = dot_nn(dpair_low, readout) + dot_nt((xs * tail_wide).astype(BF16), after_low)
    keep = into_wide[Q - 1:Q, :]
    carry_ref[...] = after * keep + dot_tn(readout, g_into)
    xs_round = xs_low.astype(F32)
    end_sum = column_sum(xs_round * from_tail) + keep * column_sum(after * prior)
    terms = jnp.concatenate([
        g_low.astype(F32) * y - xs_round * dxs, x * dxs, jnp.broadcast_to(end_sum, (16, width))], axis=0)
    high, less = pieces(terms, 2)
    sums = dot_nt(high, spread) + dot_nt(less, spread)
    end_heads = sums[2 * Q:2 * Q + 1]
    last_row = lax.broadcasted_iota(jnp.int32, (Q, STATE), 0) == Q - 1
    dcum = sums[:Q] + jnp.where(last_row, end_heads, 0.0)
    ddecay = ones_times(jnp.where(row <= col, 1.0, 0.0).astype(BF16), dcum, 3)
    dsize = sums[Q:2 * Q] - ddecay * rate
    draw = dsize * jax.nn.sigmoid(raw)
    dhead_ref[0:1, :] += column_sum(draw)
    dhead_ref[1:2, :] += column_sum(ddecay * decay)
    dz = (size_wide * dxs + skip * g) * silu_slope(z, sig_z)
    dz_ref[0:Q, :] = dz
    for k in range(4):
        dcw_ref[3 - k:4 - k, :] += column_sum(dz * z_rows[k])
    dinner_ref[...] = lead_sum(dz_ref, masks, cw_ref[...]).astype(BF16)
    dz_ref[Q:Q + HALO, :] = dz_ref[0:HALO, :]
    dzs = jnp.concatenate([dentry, dreadout], axis=1) * silu_slope(zs, sig_zs)
    dzs_ref[0:Q, :] = dzs
    for k in range(4):
        dsw_ref[3 - k:4 - k, :] += column_sum(dzs * zs_rows[k])
    dss_ref[:, :2 * STATE] = lead_sum(dzs_ref, masks, sw_ref[...]).astype(BF16)
    dzs_ref[Q:Q + HALO, :] = dzs_ref[0:HALO, :]
    dss_ref[:, 2 * STATE:] = draw.astype(BF16)


def mix_bwd(seg_col, seg_rows, masks, pre, y, states, dout, cw, sw, bias, rate, skip, spread, heads):
    rows, width = pre.shape[0], cw.shape[1]
    seqs = rows // LEN
    per = LEN // Q
    pre_width = pre.shape[1]
    at = lambda s, c: s * per + per - 1 - c
    blk = lambda w: pl.BlockSpec((Q, w), lambda s, c: (at(s, c), 0))
    prev = lambda w: pl.BlockSpec(
        (HALO, w), lambda s, c: (jnp.maximum(at(s, c) * (Q // HALO) - 1, 0), 0))
    whole = lambda shape: pl.BlockSpec(shape, lambda s, c: (0, 0))
    return pl.pallas_call(
        functools.partial(mix_bwd_kernel, heads),
        grid=(seqs, per),
        in_specs=[
            blk(1),
            pl.BlockSpec((1, 1, Q), lambda s, c: (at(s, c), 0, 0)),
            blk(8), blk(pre_width), prev(pre_width), blk(width),
            pl.BlockSpec((1, STATE, width), lambda s, c: (at(s, c), 0, 0)),
            blk(width),
            whole(cw.shape), whole(sw.shape), whole(bias.shape), whole(rate.shape),
            whole(skip.shape), whole(spread.shape),
        ],
        out_specs=[
            blk(pre_width),
            whole((4, width)), whole((4, 2 * STATE)), whole((8, STATE)), whole((1, width)),
        ],
        out_shape=[
            jax.ShapeDtypeStruct((rows, pre_width), BF16),
            jax.ShapeDtypeStruct((4, width), F32),
            jax.ShapeDtypeStruct((4, 2 * STATE), F32),
            jax.ShapeDtypeStruct((8, STATE), F32),
            jax.ShapeDtypeStruct((1, width), F32),
        ],
        scratch_shapes=[
            pltpu.VMEM((STATE, width), F32),
            pltpu.VMEM((Q + HALO, width), F32),
            pltpu.VMEM((Q + HALO, 2 * STATE), F32),
            pltpu.VMEM((Q, width), F32),
            pltpu.VMEM((Q + HALO, width), F32),
            pltpu.VMEM((Q + HALO, 2 * STATE), F32),
        ],
        compiler_params=pltpu.CompilerParams(vmem_limit_bytes=VMEM_BYTES),
        cost_estimate=pl.CostEstimate(
            flops=rows * width * 3000, bytes_accessed=rows * width * 28,
            transcendentals=rows * width * 4),
        name="mix_bwd",
    )(seg_col, seg_rows, masks, pre, pre, y, states, dout, cw, sw, bias,
      rate, skip, spread)


NORM_EPS = 1e-05
ROPE_THETA = 100000000000.0
KV_HEADS = 2
HEADS = 8
LANES = 128


def permute_bit(x, axis, bit):
    n = lax.axis_size(axis)
    return lax.ppermute(x, axis, [(i, i ^ bit) for i in range(n)])


def bit_orders(axis):
    n = lax.axis_size(axis)
    bits = [n >> (k + 1) for k in range(n.bit_length() - 1)]
    rest = bits[1:]
    turn = lambda j: rest[j % len(rest):] + rest[:j % len(rest)] if rest else []
    return [bits[:1] + turn(j) for j in range(3)]


def gather_rel(piece, axis, order):
    held = piece[None]
    places = [0]
    for bit in order:
        before = held
        held = jnp.concatenate([held, permute_bit(held, axis, bit)], axis=0)
        places = places + [p ^ bit for p in places]
    return held, places, before


def assemble_kernel(plan, count, me_ref, *refs):
    sources = refs[:len(plan)]
    dests = refs[len(plan):len(plan) + count]
    sems = refs[-1]
    copies = []
    for j, (places, dest, row_off, lane_off, block_rows) in enumerate(plan):
        rows, width = sources[j].shape[1:]
        for p, place in enumerate(places):
            start = pl.multiple_of((me_ref[0] ^ place) * block_rows + row_off, 16)
            copies.append(pltpu.make_async_copy(
                sources[j].at[p],
                dests[dest].at[pl.ds(start, rows), pl.ds(lane_off, width)],
                sems.at[j, p]))
    for copy in copies:
        copy.start()
    for copy in copies:
        copy.wait()


def assemble(me, rels, plan, shapes):
    hbm = pl.BlockSpec(memory_space=pl.ANY)
    return pl.pallas_call(
        functools.partial(assemble_kernel, plan, len(shapes)),
        grid_spec=pltpu.PrefetchScalarGridSpec(
            num_scalar_prefetch=1,
            grid=(1,),
            in_specs=[hbm] * len(rels),
            out_specs=[hbm] * len(shapes),
            scratch_shapes=[pltpu.SemaphoreType.DMA((len(rels), rels[0].shape[0]))],
        ),
        out_shape=[jax.ShapeDtypeStruct(s, BF16) for s in shapes],
        compiler_params=pltpu.CompilerParams(vmem_limit_bytes=4 * 1024 * 1024),
        cost_estimate=pl.CostEstimate(
            flops=0, bytes_accessed=sum(4 * s[0] * s[1] for s in shapes), transcendentals=0),
        name="assemble",
    )(me, *rels)


def thirds(width):
    cuts = [0] + [min(width, -(-width * k // (3 * LANES)) * LANES) for k in (1, 2)] + [width]
    return [(a, b) for a, b in zip(cuts, cuts[1:]) if b > a]


def reduce_open(part, axis, row_off, row_count):
    n = lax.axis_size(axis)
    levels = n.bit_length() - 1
    own = part.shape[0] // n
    cur = part.reshape((2,) * levels + (own, part.shape[1]))
    if (row_off, row_count) != (0, own):
        cur = lax.slice_in_dim(cur, row_off, row_off + row_count, axis=levels)
    return cur


def reduce_halves(cur, axis, bit):
    mine = (lax.axis_index(axis) // bit) % 2
    dim = cur.ndim - 2 - bit.bit_length()
    return lax.dynamic_slice_in_dim(cur, mine, 1, dim), lax.dynamic_slice_in_dim(cur, 1 - mine, 1, dim)


def reduce_step(halves, axis, bit, last):
    keep, send = halves
    total = keep.astype(F32) + permute_bit(send, axis, bit).astype(F32)
    return total if last else total.astype(BF16)


def reduce_rest(cur, axis, order):
    for bit in reversed(order):
        cur = reduce_step(reduce_halves(cur, axis, bit), axis, bit, bit == order[0])
    return cur.reshape(cur.shape[-2:])


def sum_cube(x, axis):
    n = lax.axis_size(axis)
    bit = 1
    while bit < n:
        x = (x.astype(F32) + permute_bit(x, axis, bit).astype(F32)).astype(x.dtype)
        bit *= 2
    return x


def tensor_gather(x, natural):
    n = lax.axis_size("tensor")
    rank = lax.axis_index("tensor")
    bit = 1
    while bit < n:
        other = permute_bit(x, "tensor", bit)
        if natural:
            low = (rank // bit) % 2 == 0
            x = jnp.concatenate([jnp.where(low, x, other), jnp.where(low, other, x)], axis=0)
        else:
            x = jnp.concatenate([x, other], axis=0)
        bit *= 2
    return x


def tensor_scatter(product, arrays, natural):
    n = lax.axis_size("tensor")
    rank = lax.axis_index("tensor")
    if n == 2:
        half = arrays[0].shape[0] // 2
        cut = lambda a, k: lax.dynamic_slice_in_dim(a, k * half, half, 0) if natural else (
            lax.slice_in_dim(a, k * half, (k + 1) * half, axis=0))
        mine, other = (rank, 1 - rank) if natural else (0, 1)
        send = product(*[cut(a, other) for a in arrays]).astype(BF16)
        arrived = permute_bit(send, "tensor", 1)
        return product(*[cut(a, mine) for a in arrays]) + arrived.astype(F32)
    x = product(*arrays)
    bit = n // 2
    while bit >= 1:
        half = x.shape[0] // 2
        if natural:
            mine = (rank // bit) % 2
            keep = lax.dynamic_slice_in_dim(x, mine * half, half, 0)
            send = lax.dynamic_slice_in_dim(x, (1 - mine) * half, half, 0)
        else:
            keep, send = x[:half], x[half:]
        x = keep.astype(F32) + permute_bit(send.astype(BF16), "tensor", bit).astype(F32)
        bit //= 2
    return x


def inverse_rms(v):
    return lax.rsqrt(jnp.mean(v * v, axis=-1, keepdims=True) + NORM_EPS)


def norm_back(v, inverse, gain, grad):
    u = grad * gain
    into = inverse * u - inverse ** 3 * v * jnp.mean(u * v, axis=-1, keepdims=True)
    return into, jnp.sum(grad * v * inverse, axis=0)


def rope_tables():
    half = HEAD_DIM // 2
    index = (jnp.arange(HEAD_DIM, dtype=jnp.int32) % half).astype(F32)
    frequency = jnp.exp(index * (-2.0 * math.log(ROPE_THETA) / HEAD_DIM))
    angles = jnp.arange(LEN, dtype=jnp.int32).astype(F32)[:, None] * frequency[None, :]
    return jnp.cos(angles), jnp.sin(angles)


def per_device(
    layer_input, segment_ids, out_grad, norm_gain, query_w, key_w, value_w, out_w, mamba_gate_w,
    mamba_in_w, state_in_w, step_w, channel_conv, state_conv, step_bias, decay_log, skip_gain,
    mamba_out_w, ffn_gain, ffn_gate_w, ffn_up_w, ffn_down_w,
):
    dp = lax.axis_size("dp")
    rank = lax.axis_index("tensor")
    me = lax.axis_index("dp").astype(jnp.int32).reshape(1)
    heads = query_w.shape[1] // HEAD_DIM
    ssm = step_w.shape[1]
    width = mamba_in_w.shape[1]
    q_width = query_w.shape[1]
    units = ffn_gate_w.shape[1]
    kv_index = rank * heads // (HEADS // KV_HEADS)
    features = layer_input.shape[1]
    block_rows = query_w.shape[0]
    half_rows = block_rows // 2
    orders = bit_orders("dp")

    key_own = lax.dynamic_slice_in_dim(key_w, kv_index * HEAD_DIM, HEAD_DIM, 1)
    value_own = lax.dynamic_slice_in_dim(value_w, kv_index * HEAD_DIM, HEAD_DIM, 1)
    qkv_shard = jnp.concatenate([query_w, key_own, value_own], axis=1)
    mix_shard = jnp.concatenate(
        [mamba_gate_w, mamba_in_w, state_in_w, jnp.pad(step_w, ((0, 0), (0, STATE - ssm)))], axis=1)
    total_cols = mix_shard.shape[1] + qkv_shard.shape[1]
    mix_cols = thirds(total_cols)
    mix_cols = [(a, min(b, mix_shard.shape[1])) for a, b in mix_cols if a < mix_shard.shape[1]]
    rels, plan, befores = [], [], []
    for j, (a, b) in enumerate(mix_cols):
        rel, places, before = gather_rel(mix_shard[:, a:b], "dp", orders[j])
        rels.append(rel)
        befores.append(before)
        plan.append((places, 0, 0, a, block_rows))
    rel, places, before = gather_rel(qkv_shard, "dp", orders[2])
    rels.append(rel)
    befores.append(before)
    plan.append((places, 1, 0, 0, block_rows))
    mix_w, qkv_w = assemble(me, rels, plan, [(features, mix_shard.shape[1]),
                                            (features, qkv_shard.shape[1])])

    later = jnp.concatenate([ffn_gate_w, ffn_up_w, ffn_down_w.T], axis=1)
    later, _ = lax.optimization_barrier((later, tuple(befores)))
    later = lax.all_gather(later, "dp", axis=0, tiled=True)
    ffn_gate, ffn_up, ffn_down_t = (later[:, k * units:(k + 1) * units] for k in range(3))

    (out_shard, mout_shard), rels = lax.optimization_barrier(((out_w.T, mamba_out_w.T), tuple(rels)))
    rels2, plan2 = [], []
    for piece, dest, row_off, order in (
        (mout_shard[:half_rows], 1, 0, 0), (mout_shard[half_rows:], 1, half_rows, 1),
        (out_shard, 0, 0, 2),
    ):
        rel, places, _ = gather_rel(piece, "dp", orders[order])
        rels2.append(rel)
        plan2.append((places, dest, row_off, 0, block_rows))
    out_t, mout_t = assemble(me, rels2, plan2, [(features, q_width), (features, width)])

    tokens = layer_input.astype(F32)
    inverse = inverse_rms(tokens)
    normed = tensor_gather((tokens * inverse * norm_gain).astype(BF16), True)
    top_grad = tensor_gather(out_grad, False)
    rows = normed.shape[0]
    seqs = rows // LEN

    seg = segment_ids.reshape(seqs, LEN)
    seg_col = segment_ids[:, None]
    masks = token_masks(seg)
    starts = jnp.sum(seg[:, None, :] < seg[:, ::BQ, None], axis=-1, dtype=jnp.int32)
    first = (starts // BQ).reshape(-1)
    cos, sin = rope_tables()

    queries, key_rows, value_rows = rope(dot_nn(normed, qkv_w), cos, sin)
    seg_blocks = segment_ids.reshape(-1, 1, BQ)
    attended, lse = attend_fwd(first, queries, key_rows, value_rows, seg_col, seg_blocks)

    pre = dot_nn(normed, mix_w)
    pad_heads = lambda a: jnp.pad(a[None], ((0, 0), (0, STATE - ssm)))
    bias, rate = pad_heads(step_bias), pad_heads(decay_log)
    skip = jnp.repeat(skip_gain, HEAD_DIM)[None]
    spread = jnp.pad(jnp.repeat(jnp.eye(ssm, dtype=BF16), HEAD_DIM, axis=1), ((0, STATE - ssm), (0, 0)))
    chunk_rows = segment_ids.reshape(-1, 1, Q)
    gated, scanned, states = mix_fwd(
        seg_col, chunk_rows, masks, pre, channel_conv, state_conv, bias, rate, skip, spread, ssm)

    branch = tensor_scatter(
        lambda a, b: dot_nt(a, out_t) + dot_nt(b, mout_t), (attended, gated), True)
    middle = tokens + branch
    mid_inverse = inverse_rms(middle)
    mid = tensor_gather((middle * mid_inverse * ffn_gain).astype(BF16), False)
    gate_vals = dot_nn(mid, ffn_gate).astype(BF16).astype(F32)
    up_vals = dot_nn(mid, ffn_up).astype(BF16).astype(F32)
    act = (jax.nn.silu(gate_vals) * up_vals).astype(BF16)
    block_out = (middle + tensor_scatter(lambda a: dot_nt(a, ffn_down_t), (act,), False)).astype(BF16)

    act_grad = dot_nn(top_grad, ffn_down_t)
    gate_sig = jax.nn.sigmoid(gate_vals)
    gate_grad = (act_grad * up_vals * silu_slope(gate_vals, gate_sig)).astype(BF16)
    up_grad = (act_grad * (gate_vals * gate_sig)).astype(BF16)
    mid_norm_grad = tensor_scatter(
        lambda a, b: dot_nt(a, ffn_gate) + dot_nt(b, ffn_up), (gate_grad, up_grad), False)
    down_part = dot_tn(top_grad, act).astype(BF16)
    gate_part = dot_tn(mid, gate_grad).astype(BF16)
    up_part = dot_tn(mid, up_grad).astype(BF16)
    by_owner = lambda a: a.reshape(dp, block_rows, units)
    ffn_sum = lax.psum_scatter(
        jnp.concatenate([by_owner(gate_part), by_owner(up_part), by_owner(down_part)], axis=1),
        "dp", scatter_dimension=0, tiled=True)[0]
    ffn_gate_w_grad, ffn_up_w_grad, ffn_down_w_grad = (
        ffn_sum[k * block_rows:(k + 1) * block_rows].astype(F32) for k in range(3))

    mid_into, ffn_gain_part = norm_back(middle, mid_inverse, ffn_gain, mid_norm_grad)
    middle_grad = out_grad.astype(F32) + mid_into
    branch_grad = tensor_gather(middle_grad.astype(BF16), True)
    attended_grad = dot_nn(branch_grad, out_t).astype(BF16)
    gated_grad = dot_nn(branch_grad, mout_t)
    out_part = dot_tn(branch_grad, attended).astype(BF16)
    mout_part = dot_tn(branch_grad, gated).astype(BF16)
    pieces2 = [(mout_part, 0, half_rows, 0), (mout_part, half_rows, half_rows, 1),
               (out_part, 0, block_rows, 2)]
    halves2 = [
        reduce_halves(reduce_open(p, "dp", off, count), "dp", orders[j][-1]) for p, off, count, j in pieces2]
    attended_grad, halves2 = lax.optimization_barrier((attended_grad, halves2))
    held2 = [reduce_step(h, "dp", orders[p[3]][-1], False) for h, p in zip(halves2, pieces2)]
    query_grad, key_grad, value_grad = attend_bwd(
        first, queries, key_rows, value_rows, attended_grad, seg_col, seg_blocks, lse, attended, cos, sin)
    qkv_grad = jnp.concatenate([query_grad, key_grad, value_grad], axis=1)
    halves2 = [reduce_halves(c, "dp", orders[p[3]][-2]) for c, p in zip(held2, pieces2)]
    gated_grad, qkv_grad, halves2 = lax.optimization_barrier((gated_grad, qkv_grad, halves2))
    held2 = [reduce_step(h, "dp", orders[p[3]][-2], False) for h, p in zip(halves2, pieces2)]
    mix_grad, conv_part, state_conv_part, head_part, skip_part = mix_bwd(
        seg_col, chunk_rows, masks, pre, scanned, states, gated_grad, channel_conv, state_conv, bias,
        rate, skip, spread, ssm)

    pieces1 = [(dot_tn(normed, mix_grad[:, a:b]).astype(BF16), j) for j, (a, b) in enumerate(mix_cols)]
    pieces1.append((dot_tn(normed, qkv_grad).astype(BF16), 2))
    halves1 = [reduce_halves(reduce_open(p, "dp", 0, block_rows), "dp", orders[j][-1]) for p, j in pieces1]
    mix_grad_late, halves1 = lax.optimization_barrier((mix_grad, halves1))
    held1 = [reduce_step(h, "dp", orders[p[1]][-1], False) for h, p in zip(halves1, pieces1)]
    sums = [reduce_rest(c, "dp", orders[p[1]][:-1]) for c, p in zip(held1, pieces1)]
    mix_sum = jnp.concatenate(sums[:-1], axis=1)
    qkv_sum = sums[-1]
    mout_a, mout_b, out_sum = (
        reduce_rest(c, "dp", orders[p[3]][:-2]) for c, p in zip(held2, pieces2))
    mamba_out_w_grad = jnp.concatenate([mout_a, mout_b], axis=0).T
    out_w_grad = out_sum.T
    normed_grad = tensor_scatter(
        lambda a, b: dot_nt(a, qkv_w) + dot_nt(b, mix_w), (qkv_grad, mix_grad_late), True)
    norm_into, norm_gain_part = norm_back(tokens, inverse, norm_gain, normed_grad)
    input_grad = middle_grad + norm_into

    place = lambda a, whole: lax.dynamic_update_slice_in_dim(
        jnp.zeros((block_rows, whole.shape[1]), BF16), a.astype(BF16), kv_index * HEAD_DIM, 1)
    shared = sum_cube(jnp.concatenate([
        place(qkv_sum[:, q_width:q_width + HEAD_DIM], key_w),
        place(qkv_sum[:, q_width + HEAD_DIM:], value_w),
        mix_sum[:, 2 * width:2 * width + 2 * STATE].astype(BF16)], axis=1), "tensor").astype(F32)
    kv_cols = key_w.shape[1]

    heads_part = jnp.concatenate([
        head_part[0, :ssm], head_part[1, :ssm],
        jnp.sum(skip_part.reshape(ssm, HEAD_DIM), axis=1)])
    own = 4 * width + 3 * ssm
    small = sum_cube(jnp.concatenate([
        conv_part.reshape(-1), heads_part, state_conv_part.reshape(-1), ffn_gain_part,
        norm_gain_part]), "dp")
    conv_grad = small[:4 * width].reshape(4, width)
    bias_grad, decay_grad, skip_grad = (
        small[4 * width + k * ssm:4 * width + (k + 1) * ssm] for k in range(3))
    both = sum_cube(small[own:], "tensor")
    state_conv_grad = both[:8 * STATE].reshape(4, 2 * STATE)
    ffn_gain_grad = both[8 * STATE:8 * STATE + features]
    gain = both[8 * STATE + features:]
    return (
        block_out,
        input_grad,
        gain,
        qkv_sum[:, :q_width],
        shared[:, :kv_cols],
        shared[:, kv_cols:2 * kv_cols],
        out_w_grad,
        mix_sum[:, :width],
        mix_sum[:, width:2 * width],
        shared[:, 2 * kv_cols:],
        mix_sum[:, 2 * width + 2 * STATE:2 * width + 2 * STATE + ssm],
        conv_grad,
        state_conv_grad,
        bias_grad,
        decay_grad,
        skip_grad,
        mamba_out_w_grad,
        ffn_gain_grad,
        ffn_gate_w_grad,
        ffn_up_w_grad,
        ffn_down_w_grad.T,
    )


def solution(mesh):
    in_specs = (
        P(("dp", "tensor"), None),
        P("dp"),
        P(("dp", "tensor"), None),
        P(),
        P("dp", "tensor"),
        P("dp", None),
        P("dp", None),
        P("tensor", "dp"),
        P("dp", "tensor"),
        P("dp", "tensor"),
        P("dp", None),
        P("dp", "tensor"),
        P(None, "tensor"),
        P(),
        P("tensor"),
        P("tensor"),
        P("tensor"),
        P("tensor", "dp"),
        P(),
        P("dp", "tensor"),
        P("dp", "tensor"),
        P("tensor", "dp"),
    )
    out_specs = (
        P(("dp", "tensor"), None),
        P(("dp", "tensor"), None),
        P(),
        P("dp", "tensor"),
        P("dp", None),
        P("dp", None),
        P("tensor", "dp"),
        P("dp", "tensor"),
        P("dp", "tensor"),
        P("dp", None),
        P("dp", "tensor"),
        P(None, "tensor"),
        P(),
        P("tensor"),
        P("tensor"),
        P("tensor"),
        P("tensor", "dp"),
        P(),
        P("dp", "tensor"),
        P("dp", "tensor"),
        P("tensor", "dp"),
    )
    return jax.shard_map(
        per_device, mesh=mesh, in_specs=in_specs, out_specs=out_specs, check_vma=False
    )
```

```python
import functools
import math

import jax
import jax.numpy as jnp
from jax import lax
from jax.experimental import pallas as pl
from jax.experimental.pallas import tpu as pltpu
from jax.sharding import PartitionSpec as P

HEAD_DIM = 64
STATE = 128
LEN = 2048
BQ = 512
Q = 128
HALO = 8
NEG = -1e30
PRECISE = lax.Precision.HIGHEST
F32 = jnp.float32
BF16 = jnp.bfloat16
VMEM_BYTES = 48 * 1024 * 1024


def dot_nn(left, right):
    return lax.dot_general(left, right, (((1,), (0,)), ((), ())), preferred_element_type=F32)


def dot_nt(left, right):
    return lax.dot_general(left, right, (((1,), (1,)), ((), ())), preferred_element_type=F32)


def dot_tn(left, right):
    return lax.dot_general(left, right, (((0,), (0,)), ((), ())), preferred_element_type=F32)


def pieces(a, count):
    parts = []
    for _ in range(count):
        parts.append(a.astype(BF16))
        a = a - parts[-1].astype(F32)
    return parts


def rope_kernel(heads, qkv_ref, cos_ref, sin_ref, q_ref, k_ref, v_ref):
    half = HEAD_DIM // 2
    cos, sin = cos_ref[...], sin_ref[...]

    def turn(x):
        return x * cos + jnp.concatenate([-x[:, half:], x[:, :half]], axis=1) * sin

    for h in range(heads):
        lanes = slice(h * HEAD_DIM, (h + 1) * HEAD_DIM)
        q_ref[:, lanes] = (turn(qkv_ref[:, lanes]).astype(BF16) * HEAD_DIM ** -0.5).astype(BF16)
    edge = heads * HEAD_DIM
    k_ref[...] = turn(qkv_ref[:, edge:edge + HEAD_DIM]).astype(BF16)
    v_ref[:, :HEAD_DIM] = qkv_ref[:, edge + HEAD_DIM:].astype(BF16)
    v_ref[:, HEAD_DIM:] = jnp.ones((v_ref.shape[0], HEAD_DIM), BF16)


def rope(qkv, cos, sin):
    rows, width = qkv.shape
    heads = width // HEAD_DIM - 2
    per = LEN // BQ
    blk = lambda w: pl.BlockSpec((BQ, w), lambda i: (i, 0))
    table = pl.BlockSpec((BQ, HEAD_DIM), lambda i: (lax.rem(i, per), 0))
    return pl.pallas_call(
        functools.partial(rope_kernel, heads),
        grid=(rows // BQ,),
        in_specs=[blk(width), table, table],
        out_specs=[blk(heads * HEAD_DIM), blk(HEAD_DIM), blk(2 * HEAD_DIM)],
        out_shape=[
            jax.ShapeDtypeStruct((rows, heads * HEAD_DIM), BF16),
            jax.ShapeDtypeStruct((rows, HEAD_DIM), BF16),
            jax.ShapeDtypeStruct((rows, 2 * HEAD_DIM), BF16),
        ],
        compiler_params=pltpu.CompilerParams(vmem_limit_bytes=VMEM_BYTES),
        cost_estimate=pl.CostEstimate(
            flops=rows * width * 8, bytes_accessed=rows * width * 6, transcendentals=0),
        name="rope",
    )(qkv, cos, sin)


def attend_fwd_kernel(heads, first_ref, q_ref, k_ref, v_ref, seg_ref, segrow_ref, out_ref, lse_ref,
                      top_ref, acc_ref):
    seq = pl.program_id(0)
    block = pl.program_id(1)
    top_ref[...] = jnp.full_like(top_ref, NEG)
    acc_ref[...] = jnp.zeros_like(acc_ref)
    key_pos = lax.broadcasted_iota(jnp.int32, (BQ, BQ), 0)
    row_pos = lax.broadcasted_iota(jnp.int32, (BQ, BQ), 1)

    def step(j, carry):
        at = pl.ds(pl.multiple_of(j * BQ, BQ), BQ)
        k = k_ref[at, :]
        v = v_ref[at, :]
        allowed = (segrow_ref[0] == seg_ref[at, :]) & (key_pos + (j - block) * BQ <= row_pos)
        bias = jnp.where(allowed, 0.0, NEG)
        for h in range(heads):
            s = dot_nt(k, q_ref[:, h * HEAD_DIM:(h + 1) * HEAD_DIM]) + bias
            old = top_ref[h]
            new = jnp.maximum(old, jnp.max(s, axis=0, keepdims=True))
            shrink = jnp.broadcast_to(jnp.exp(old - new), (2 * HEAD_DIM, BQ)).T
            p = jnp.exp(s - new).astype(BF16)
            acc_ref[h] = acc_ref[h] * shrink + dot_tn(p, v)
            top_ref[h] = new
        return carry

    lax.fori_loop(first_ref[seq * (LEN // BQ) + block], block + 1, step, 0)
    for h in range(heads):
        acc = acc_ref[h]
        out_ref[:, h * HEAD_DIM:(h + 1) * HEAD_DIM] = (
            acc[:, :HEAD_DIM] / acc[:, HEAD_DIM:]).astype(BF16)
        lse_ref[0, h:h + 1, :] = top_ref[h] + jnp.log(acc.T[HEAD_DIM:HEAD_DIM + 1, :])


def attend_fwd(first, q, k, v, seg_col, seg_rows):
    rows, width = q.shape
    heads = width // HEAD_DIM
    seqs = rows // LEN
    per = LEN // BQ
    return pl.pallas_call(
        functools.partial(attend_fwd_kernel, heads),
        grid_spec=pltpu.PrefetchScalarGridSpec(
            num_scalar_prefetch=1,
            grid=(seqs, per),
            in_specs=[
                pl.BlockSpec((BQ, width), lambda s, i, f: (s * per + i, 0)),
                pl.BlockSpec((LEN, HEAD_DIM), lambda s, i, f: (s, 0)),
                pl.BlockSpec((LEN, 2 * HEAD_DIM), lambda s, i, f: (s, 0)),
                pl.BlockSpec((LEN, 1), lambda s, i, f: (s, 0)),
                pl.BlockSpec((1, 1, BQ), lambda s, i, f: (s * per + i, 0, 0)),
            ],
            out_specs=[
                pl.BlockSpec((BQ, width), lambda s, i, f: (s * per + i, 0)),
                pl.BlockSpec((1, heads, BQ), lambda s, i, f: (s * per + i, 0, 0)),
            ],
            scratch_shapes=[
                pltpu.VMEM((heads, 1, BQ), F32),
                pltpu.VMEM((heads, BQ, 2 * HEAD_DIM), F32),
            ],
        ),
        out_shape=[
            jax.ShapeDtypeStruct((rows, width), BF16),
            jax.ShapeDtypeStruct((seqs * per, heads, BQ), F32),
        ],
        compiler_params=pltpu.CompilerParams(vmem_limit_bytes=VMEM_BYTES),
        cost_estimate=pl.CostEstimate(
            flops=2 * rows * LEN * width, bytes_accessed=4 * rows * width,
            transcendentals=rows * LEN * heads // 2),
        name="attend_fwd",
    )(first, q, k, v, seg_col, seg_rows)


def attend_bwd_kernel(heads, first_ref, q_ref, k_ref, v_ref, g_ref, seg_ref, segrow_ref, lse_ref,
                      out_ref, cos_ref, sin_ref, cosk_ref, sink_ref, dq_ref, dk_ref, dv_ref,
                      dqs_ref, dks_ref, dvs_ref, delta_ref):
    seq = pl.program_id(0)
    block = pl.program_id(1)
    half = HEAD_DIM // 2
    scale = HEAD_DIM ** -0.5

    @pl.when(block == 0)
    def _():
        dks_ref[...] = jnp.zeros_like(dks_ref)
        dvs_ref[...] = jnp.zeros_like(dvs_ref)

    dqs_ref[...] = jnp.zeros_like(dqs_ref)
    ones = jnp.ones((16, HEAD_DIM), BF16)
    high, less = pieces(g_ref[...].astype(F32) * out_ref[...].astype(F32), 2)
    for h in range(heads):
        lanes = slice(h * HEAD_DIM, (h + 1) * HEAD_DIM)
        delta_ref[h] = (dot_nt(ones, high[:, lanes]) + dot_nt(ones, less[:, lanes]))[0:1, :]
    key_pos = lax.broadcasted_iota(jnp.int32, (BQ, BQ), 0)
    row_pos = lax.broadcasted_iota(jnp.int32, (BQ, BQ), 1)

    def step(j, carry):
        at = pl.ds(pl.multiple_of(j * BQ, BQ), BQ)
        k = k_ref[at, :]
        v = v_ref[at, :HEAD_DIM]
        allowed = (segrow_ref[0] == seg_ref[at, :]) & (key_pos + (j - block) * BQ <= row_pos)
        bias = jnp.where(allowed, 0.0, NEG)
        dk = jnp.zeros((BQ, HEAD_DIM), F32)
        dv = jnp.zeros((BQ, HEAD_DIM), F32)
        for h in range(heads):
            lanes = slice(h * HEAD_DIM, (h + 1) * HEAD_DIM)
            q = q_ref[:, lanes]
            g = g_ref[:, lanes]
            s = dot_nt(k, q) + bias
            p = jnp.exp(s - lse_ref[0, h:h + 1, :])
            dp = dot_nt(v, g)
            ds = (p * (dp - delta_ref[h])).astype(BF16)
            dv = dv + dot_nn(p.astype(BF16), g)
            dk = dk + dot_nn(ds, q)
            dqs_ref[h] = dqs_ref[h] + dot_tn(ds, k)
        dks_ref[at, :] = dks_ref[at, :] + dk
        dvs_ref[at, :] = dvs_ref[at, :] + dv
        return carry

    lax.fori_loop(first_ref[seq * (LEN // BQ) + block], block + 1, step, 0)

    def turn_back(x, cos, sin):
        swapped = jnp.concatenate([x[:, half:], -x[:, :half]], axis=1)
        return x * cos + swapped * sin

    for h in range(heads):
        dq = turn_back(dqs_ref[h] * scale, cos_ref[...], sin_ref[...])
        dq_ref[:, h * HEAD_DIM:(h + 1) * HEAD_DIM] = dq.astype(BF16)

    @pl.when(block == pl.num_programs(1) - 1)
    def _():
        dk_ref[...] = turn_back(dks_ref[...], cosk_ref[...], sink_ref[...]).astype(BF16)
        dv_ref[...] = dvs_ref[...].astype(BF16)


def attend_bwd(first, q, k, v, g, seg_col, seg_rows, lse_rows, attended, cos, sin):
    rows, width = q.shape
    heads = width // HEAD_DIM
    seqs = rows // LEN
    per = LEN // BQ
    return pl.pallas_call(
        functools.partial(attend_bwd_kernel, heads),
        grid_spec=pltpu.PrefetchScalarGridSpec(
            num_scalar_prefetch=1,
            grid=(seqs, per),
            in_specs=[
                pl.BlockSpec((BQ, width), lambda s, i, f: (s * per + i, 0)),
                pl.BlockSpec((LEN, HEAD_DIM), lambda s, i, f: (s, 0)),
                pl.BlockSpec((LEN, 2 * HEAD_DIM), lambda s, i, f: (s, 0)),
                pl.BlockSpec((BQ, width), lambda s, i, f: (s * per + i, 0)),
                pl.BlockSpec((LEN, 1), lambda s, i, f: (s, 0)),
                pl.BlockSpec((1, 1, BQ), lambda s, i, f: (s * per + i, 0, 0)),
                pl.BlockSpec((1, heads, BQ), lambda s, i, f: (s * per + i, 0, 0)),
                pl.BlockSpec((BQ, width), lambda s, i, f: (s * per + i, 0)),
                pl.BlockSpec((BQ, HEAD_DIM), lambda s, i, f: (i, 0)),
                pl.BlockSpec((BQ, HEAD_DIM), lambda s, i, f: (i, 0)),
                pl.BlockSpec((LEN, HEAD_DIM), lambda s, i, f: (0, 0)),
                pl.BlockSpec((LEN, HEAD_DIM), lambda s, i, f: (0, 0)),
            ],
            out_specs=[
                pl.BlockSpec((BQ, width), lambda s, i, f: (s * per + i, 0)),
                pl.BlockSpec((LEN, HEAD_DIM), lambda s, i, f: (s, 0)),
                pl.BlockSpec((LEN, HEAD_DIM), lambda s, i, f: (s, 0)),
            ],
            scratch_shapes=[
                pltpu.VMEM((heads, BQ, HEAD_DIM), F32),
                pltpu.VMEM((LEN, HEAD_DIM), F32),
                pltpu.VMEM((LEN, HEAD_DIM), F32),
                pltpu.VMEM((heads, 1, BQ), F32),
            ],
        ),
        out_shape=[
            jax.ShapeDtypeStruct((rows, width), BF16),
            jax.ShapeDtypeStruct((rows, HEAD_DIM), BF16),
            jax.ShapeDtypeStruct((rows, HEAD_DIM), BF16),
        ],
        compiler_params=pltpu.CompilerParams(vmem_limit_bytes=VMEM_BYTES),
        cost_estimate=pl.CostEstimate(
            flops=5 * rows * LEN * width, bytes_accessed=8 * rows * width,
            transcendentals=rows * LEN * heads // 2),
        name="attend_bwd",
    )(first, q, k, v, g, seg_col, seg_rows, lse_rows, attended, cos, sin, cos, sin)


LAG, LEAD, CARRIED, ENDING = 0, 3, 6, 7


def token_masks(seg):
    seqs = seg.shape[0]
    padded = jnp.pad(seg, ((0, 0), (3, 3)), constant_values=-1)
    columns = [padded[:, 3 - k:3 - k + LEN] == seg for k in (1, 2, 3)]
    columns += [padded[:, 3 + k:3 + k + LEN] == seg for k in (1, 2, 3)]
    chunks = seg.reshape(seqs, LEN // Q, Q)
    prior = jnp.pad(chunks[:, :-1, -1:], ((0, 0), (1, 0), (0, 0)), constant_values=-1)
    columns.append((chunks == prior).reshape(seqs, LEN))
    columns.append((chunks == chunks[:, :, -1:]).reshape(seqs, LEN))
    return jnp.stack(columns, axis=-1).astype(F32).reshape(seqs * LEN, 8)


def shifted_conv(buf_ref, width, masks, taps):
    rows = [buf_ref[HALO - k:HALO - k + Q, :width] for k in range(4)]
    rows = [rows[0]] + [rows[k] * masks[:, LAG + k - 1:LAG + k] for k in (1, 2, 3)]
    total = rows[0] * taps[3:4, :]
    for k in (1, 2, 3):
        total = total + rows[k] * taps[3 - k:4 - k, :]
    return total, rows


def softplus(x):
    return jnp.maximum(x, 0.0) + jnp.log1p(jnp.exp(-jnp.abs(x)))


def spread_heads(columns, spread):
    stack = jnp.concatenate(columns, axis=0)
    high, less = pieces(stack, 2)
    wide = dot_nn(high, spread) + dot_nn(less, spread)
    return [wide[k * Q:(k + 1) * Q] for k in range(len(columns))]


def ones_times(ones, a, count):
    width = a.shape[1]
    total = dot_nn(ones, jnp.concatenate(pieces(a, count), axis=1))
    parts = [total[:, k * width:(k + 1) * width] for k in range(count)]
    return functools.reduce(jnp.add, parts)


def chunk_masks(seg_ref, segrow_ref):
    row = lax.broadcasted_iota(jnp.int32, (Q, Q), 0)
    col = lax.broadcasted_iota(jnp.int32, (Q, Q), 1)
    same = seg_ref[...] == segrow_ref[0]
    return row, col, same


def split_pre(ref, width):
    return (ref.at[:, pl.ds(0, width)], ref.at[:, pl.ds(width, width)],
            ref.at[:, pl.ds(2 * width, 3 * STATE)])


def mix_fwd_kernel(heads, seg_ref, segrow_ref, mask_ref, pre_ref, cw_ref,
                   sw_ref, bias_ref, rate_ref, skip_ref, spread_ref, gated_ref, y_ref, states_ref,
                   carry_ref, buf_ref, sbuf_ref):
    width = y_ref.shape[1]
    gate_ref, inner_ref, ss_ref = split_pre(pre_ref, width)

    @pl.when(pl.program_id(1) == 0)
    def _():
        carry_ref[...] = jnp.zeros_like(carry_ref)
        buf_ref[0:HALO, :] = jnp.zeros((HALO, buf_ref.shape[1]), F32)
        sbuf_ref[0:HALO, :] = jnp.zeros((HALO, sbuf_ref.shape[1]), F32)

    masks = mask_ref[...]
    buf_ref[HALO:HALO + Q, :] = inner_ref[...]
    sbuf_ref[HALO:HALO + Q, :] = ss_ref[:, :2 * STATE]
    z, _ = shifted_conv(buf_ref, buf_ref.shape[1], masks, cw_ref[...])
    zs, _ = shifted_conv(sbuf_ref, 2 * STATE, masks, sw_ref[...])
    buf_ref[0:HALO, :] = buf_ref[Q:Q + HALO, :]
    sbuf_ref[0:HALO, :] = sbuf_ref[Q:Q + HALO, :]
    x = z * jax.nn.sigmoid(z)
    states = (zs * jax.nn.sigmoid(zs)).astype(BF16)
    entry = states[:, :STATE]
    readout = states[:, STATE:]
    size = softplus(ss_ref[:, 2 * STATE:] + bias_ref[...])
    decay = -size * jnp.exp(rate_ref[...])
    row, col, same = chunk_masks(seg_ref, segrow_ref)
    cum = ones_times(jnp.where(row >= col, 1.0, 0.0).astype(BF16), decay, 3)
    cum_rows = cum.T
    bias = jnp.where((row >= col) & same, 0.0, NEG)
    spread = spread_ref[...]
    into = jnp.exp(cum) * masks[:, CARRIED:CARRIED + 1]
    tail = jnp.exp(cum[Q - 1:Q, :] - cum) * masks[:, ENDING:ENDING + 1]
    size_wide, into_wide, tail_wide = spread_heads([size, into, tail], spread)
    xs = (x * size_wide)
    xs_low = xs.astype(BF16)
    pair = dot_nt(readout, entry)
    prior = carry_ref[...]
    states_ref[0] = prior
    y = dot_nn(readout, prior.astype(BF16)) * into_wide
    for h in range(heads):
        lanes = slice(h * HEAD_DIM, (h + 1) * HEAD_DIM)
        mix = (pair * jnp.exp(cum[:, h:h + 1] - cum_rows[h:h + 1, :] + bias)).astype(BF16)
        y_ref[:, lanes] = dot_nn(mix, xs_low[:, lanes])
    y = y + y_ref[...]
    y_ref[...] = y
    fresh = dot_tn(entry, (xs * tail_wide).astype(BF16))
    carry_ref[...] = prior * into_wide[Q - 1:Q, :] + fresh
    gate = gate_ref[...]
    gated_ref[...] = ((y + skip_ref[...] * x) * (gate * jax.nn.sigmoid(gate))).astype(BF16)


def mix_fwd(seg_col, seg_rows, masks, pre, cw, sw, bias, rate, skip, spread,
            heads):
    rows, width = pre.shape[0], cw.shape[1]
    seqs = rows // LEN
    per = LEN // Q
    pre_width = pre.shape[1]
    blk = lambda w: pl.BlockSpec((Q, w), lambda s, c: (s * per + c, 0))
    whole = lambda a: pl.BlockSpec(a.shape, lambda s, c: (0, 0))
    return pl.pallas_call(
        functools.partial(mix_fwd_kernel, heads),
        grid=(seqs, per),
        in_specs=[
            blk(1),
            pl.BlockSpec((1, 1, Q), lambda s, c: (s * per + c, 0, 0)),
            blk(8), blk(pre_width),
            whole(cw), whole(sw), whole(bias), whole(rate), whole(skip), whole(spread),
        ],
        out_specs=[
            blk(width), blk(width),
            pl.BlockSpec((1, STATE, width), lambda s, c: (s * per + c, 0, 0)),
        ],
        out_shape=[
            jax.ShapeDtypeStruct((rows, width), BF16),
            jax.ShapeDtypeStruct((rows, width), F32),
            jax.ShapeDtypeStruct((seqs * per, STATE, width), F32),
        ],
        scratch_shapes=[
            pltpu.VMEM((STATE, width), F32),
            pltpu.VMEM((Q + HALO, width), F32),
            pltpu.VMEM((Q + HALO, 2 * STATE), F32),
        ],
        compiler_params=pltpu.CompilerParams(vmem_limit_bytes=VMEM_BYTES),
        cost_estimate=pl.CostEstimate(
            flops=rows * width * 1200, bytes_accessed=rows * width * 22,
            transcendentals=rows * width * 4),
        name="mix_fwd",
    )(seg_col, seg_rows, masks, pre, cw, sw, bias, rate, skip, spread)


def lead_sum(buf_ref, masks, taps):
    total = buf_ref[0:Q, :] * taps[3:4, :]
    for k in (1, 2, 3):
        total = total + buf_ref[k:k + Q, :] * masks[:, LEAD + k - 1:LEAD + k] * taps[3 - k:4 - k, :]
    return total


def column_sum(a):
    return jnp.sum(a, axis=0, keepdims=True)


def silu_slope(v, sig):
    return sig * (1.0 + v * (1.0 - sig))


def mix_bwd_kernel(heads, seg_ref, segrow_ref, mask_ref, pre_ref, pre_prev_ref, y_ref, states_ref, dout_ref, cw_ref, sw_ref, bias_ref, rate_ref,
                   skip_ref, spread_ref, dpre_ref, dcw_ref, dsw_ref, dhead_ref,
                   dskip_ref, carry_ref, buf_ref, sbuf_ref, dxs_ref, dz_ref, dzs_ref):
    width = y_ref.shape[1]
    gate_ref, inner_ref, ss_ref = split_pre(pre_ref, width)
    _, inner_prev_ref, ss_prev_ref = split_pre(pre_prev_ref, width)
    dgate_ref, dinner_ref, dss_ref = split_pre(dpre_ref, width)

    @pl.when((pl.program_id(0) == 0) & (pl.program_id(1) == 0))
    def _():
        dcw_ref[...] = jnp.zeros_like(dcw_ref)
        dsw_ref[...] = jnp.zeros_like(dsw_ref)
        dhead_ref[...] = jnp.zeros_like(dhead_ref)
        dskip_ref[...] = jnp.zeros_like(dskip_ref)

    @pl.when(pl.program_id(1) == 0)
    def _():
        carry_ref[...] = jnp.zeros_like(carry_ref)
        dz_ref[Q:Q + HALO, :] = jnp.zeros((HALO, width), F32)
        dzs_ref[Q:Q + HALO, :] = jnp.zeros((HALO, 2 * STATE), F32)

    masks = mask_ref[...]
    buf_ref[0:HALO, :] = inner_prev_ref[...]
    buf_ref[HALO:HALO + Q, :] = inner_ref[...]
    sbuf_ref[0:HALO, :] = ss_prev_ref[:, :2 * STATE]
    sbuf_ref[HALO:HALO + Q, :] = ss_ref[:, :2 * STATE]
    z, z_rows = shifted_conv(buf_ref, width, masks, cw_ref[...])
    zs, zs_rows = shifted_conv(sbuf_ref, 2 * STATE, masks, sw_ref[...])
    sig_z = jax.nn.sigmoid(z)
    sig_zs = jax.nn.sigmoid(zs)
    x = z * sig_z
    states = (zs * sig_zs).astype(BF16)
    entry = states[:, :STATE]
    readout = states[:, STATE:]
    raw = ss_ref[:, 2 * STATE:] + bias_ref[...]
    size = softplus(raw)
    rate = jnp.exp(rate_ref[...])
    decay = -size * rate
    row, col, same = chunk_masks(seg_ref, segrow_ref)
    cum = ones_times(jnp.where(row >= col, 1.0, 0.0).astype(BF16), decay, 3)
    cum_rows = cum.T
    bias = jnp.where((row <= col) & same, 0.0, NEG)
    spread = spread_ref[...]
    into = jnp.exp(cum) * masks[:, CARRIED:CARRIED + 1]
    tail = jnp.exp(cum[Q - 1:Q, :] - cum) * masks[:, ENDING:ENDING + 1]
    size_wide, into_wide, tail_wide = spread_heads([size, into, tail], spread)
    xs = x * size_wide
    xs_low = xs.astype(BF16)
    gate = gate_ref[...]
    sig = jax.nn.sigmoid(gate)
    dout = dout_ref[...]
    y = y_ref[...]
    skip = skip_ref[...]
    dgate_ref[...] = (dout * (y + skip * x) * silu_slope(gate, sig)).astype(BF16)
    g = dout * (gate * sig)
    g_low = g.astype(BF16)
    dskip_ref[...] += column_sum(g * x)
    pair = dot_nt(entry, readout)
    dpair = jnp.zeros((Q, Q), F32)
    for h in range(heads):
        lanes = slice(h * HEAD_DIM, (h + 1) * HEAD_DIM)
        fade = jnp.exp(cum_rows[h:h + 1, :] - cum[:, h:h + 1] + bias)
        dxs_ref[:, lanes] = dot_nn((pair * fade).astype(BF16), g_low[:, lanes])
        dpair = dpair + dot_nt(xs_low[:, lanes], g_low[:, lanes]) * fade
    prior = states_ref[0]
    after = carry_ref[...]
    after_low = after.astype(BF16)
    from_tail = dot_nn(entry, after_low) * tail_wide
    dxs = dxs_ref[...] + from_tail
    g_into = (g * into_wide).astype(BF16)
    dpair_low = dpair.astype(BF16)
    dreadout = dot_tn(dpair_low, entry) + dot_nt(g_into, prior.astype(BF16))
    dentry = dot_nn(dpair_low, readout) + dot_nt((xs * tail_wide).astype(BF16), after_low)
    keep = into_wide[Q - 1:Q, :]
    carry_ref[...] = after * keep + dot_tn(readout, g_into)
    xs_round = xs_low.astype(F32)
    end_sum = column_sum(xs_round * from_tail) + keep * column_sum(after * prior)
    terms = jnp.concatenate([
        g_low.astype(F32) * y - xs_round * dxs, x * dxs, jnp.broadcast_to(end_sum, (16, width))], axis=0)
    high, less = pieces(terms, 2)
    sums = dot_nt(high, spread) + dot_nt(less, spread)
    end_heads = sums[2 * Q:2 * Q + 1]
    last_row = lax.broadcasted_iota(jnp.int32, (Q, STATE), 0) == Q - 1
    dcum = sums[:Q] + jnp.where(last_row, end_heads, 0.0)
    ddecay = ones_times(jnp.where(row <= col, 1.0, 0.0).astype(BF16), dcum, 3)
    dsize = sums[Q:2 * Q] - ddecay * rate
    draw = dsize * jax.nn.sigmoid(raw)
    dhead_ref[0:1, :] += column_sum(draw)
    dhead_ref[1:2, :] += column_sum(ddecay * decay)
    dz = (size_wide * dxs + skip * g) * silu_slope(z, sig_z)
    dz_ref[0:Q, :] = dz
    for k in range(4):
        dcw_ref[3 - k:4 - k, :] += column_sum(dz * z_rows[k])
    dinner_ref[...] = lead_sum(dz_ref, masks, cw_ref[...]).astype(BF16)
    dz_ref[Q:Q + HALO, :] = dz_ref[0:HALO, :]
    dzs = jnp.concatenate([dentry, dreadout], axis=1) * silu_slope(zs, sig_zs)
    dzs_ref[0:Q, :] = dzs
    for k in range(4):
        dsw_ref[3 - k:4 - k, :] += column_sum(dzs * zs_rows[k])
    dss_ref[:, :2 * STATE] = lead_sum(dzs_ref, masks, sw_ref[...]).astype(BF16)
    dzs_ref[Q:Q + HALO, :] = dzs_ref[0:HALO, :]
    dss_ref[:, 2 * STATE:] = draw.astype(BF16)


def mix_bwd(seg_col, seg_rows, masks, pre, y, states, dout, cw, sw, bias, rate, skip, spread, heads):
    rows, width = pre.shape[0], cw.shape[1]
    seqs = rows // LEN
    per = LEN // Q
    pre_width = pre.shape[1]
    at = lambda s, c: s * per + per - 1 - c
    blk = lambda w: pl.BlockSpec((Q, w), lambda s, c: (at(s, c), 0))
    prev = lambda w: pl.BlockSpec(
        (HALO, w), lambda s, c: (jnp.maximum(at(s, c) * (Q // HALO) - 1, 0), 0))
    whole = lambda shape: pl.BlockSpec(shape, lambda s, c: (0, 0))
    return pl.pallas_call(
        functools.partial(mix_bwd_kernel, heads),
        grid=(seqs, per),
        in_specs=[
            blk(1),
            pl.BlockSpec((1, 1, Q), lambda s, c: (at(s, c), 0, 0)),
            blk(8), blk(pre_width), prev(pre_width), blk(width),
            pl.BlockSpec((1, STATE, width), lambda s, c: (at(s, c), 0, 0)),
            blk(width),
            whole(cw.shape), whole(sw.shape), whole(bias.shape), whole(rate.shape),
            whole(skip.shape), whole(spread.shape),
        ],
        out_specs=[
            blk(pre_width),
            whole((4, width)), whole((4, 2 * STATE)), whole((8, STATE)), whole((1, width)),
        ],
        out_shape=[
            jax.ShapeDtypeStruct((rows, pre_width), BF16),
            jax.ShapeDtypeStruct((4, width), F32),
            jax.ShapeDtypeStruct((4, 2 * STATE), F32),
            jax.ShapeDtypeStruct((8, STATE), F32),
            jax.ShapeDtypeStruct((1, width), F32),
        ],
        scratch_shapes=[
            pltpu.VMEM((STATE, width), F32),
            pltpu.VMEM((Q + HALO, width), F32),
            pltpu.VMEM((Q + HALO, 2 * STATE), F32),
            pltpu.VMEM((Q, width), F32),
            pltpu.VMEM((Q + HALO, width), F32),
            pltpu.VMEM((Q + HALO, 2 * STATE), F32),
        ],
        compiler_params=pltpu.CompilerParams(vmem_limit_bytes=VMEM_BYTES),
        cost_estimate=pl.CostEstimate(
            flops=rows * width * 3000, bytes_accessed=rows * width * 28,
            transcendentals=rows * width * 4),
        name="mix_bwd",
    )(seg_col, seg_rows, masks, pre, pre, y, states, dout, cw, sw, bias,
      rate, skip, spread)


NORM_EPS = 1e-05
ROPE_THETA = 100000000000.0
KV_HEADS = 2
HEADS = 8
LANES = 128


def permute_bit(x, axis, bit):
    n = lax.axis_size(axis)
    return lax.ppermute(x, axis, [(i, i ^ bit) for i in range(n)])


def bit_orders(axis):
    n = lax.axis_size(axis)
    bits = [n >> (k + 1) for k in range(n.bit_length() - 1)]
    rest = bits[1:]
    turn = lambda j: rest[j % len(rest):] + rest[:j % len(rest)] if rest else []
    return [bits[:1] + turn(j) for j in range(3)]


def gather_step(held, axis, bit):
    return jnp.concatenate([held, permute_bit(held, axis, bit)], axis=0)


def gather_last(held, axis, order):
    places = [0]
    for bit in order[:-1]:
        places = places + [p ^ bit for p in places]
    return (held, places), (permute_bit(held, axis, order[-1]), [p ^ order[-1] for p in places])


def assemble_kernel(plan, count, me_ref, *refs):
    sources = refs[:len(plan)]
    dests = refs[len(plan):len(plan) + count]
    sems = refs[-1]
    copies = []
    for j, (places, dest, row_off, lane_off, block_rows) in enumerate(plan):
        rows, width = sources[j].shape[1:]
        for p, place in enumerate(places):
            start = pl.multiple_of((me_ref[0] ^ place) * block_rows + row_off, 16)
            copies.append(pltpu.make_async_copy(
                sources[j].at[p],
                dests[dest].at[pl.ds(start, rows), pl.ds(lane_off, width)],
                sems.at[j, p]))
    for copy in copies:
        copy.start()
    for copy in copies:
        copy.wait()


def assemble(me, rels, plan, shapes):
    hbm = pl.BlockSpec(memory_space=pl.ANY)
    return pl.pallas_call(
        functools.partial(assemble_kernel, plan, len(shapes)),
        grid_spec=pltpu.PrefetchScalarGridSpec(
            num_scalar_prefetch=1,
            grid=(1,),
            in_specs=[hbm] * len(rels),
            out_specs=[hbm] * len(shapes),
            scratch_shapes=[pltpu.SemaphoreType.DMA((len(rels), max(r.shape[0] for r in rels)))],
        ),
        out_shape=[jax.ShapeDtypeStruct(s, BF16) for s in shapes],
        compiler_params=pltpu.CompilerParams(vmem_limit_bytes=4 * 1024 * 1024),
        cost_estimate=pl.CostEstimate(
            flops=0, bytes_accessed=sum(4 * s[0] * s[1] for s in shapes), transcendentals=0),
        name="assemble",
    )(me, *rels)


def thirds(width):
    cuts = [0] + [min(width, -(-width * k // (3 * LANES)) * LANES) for k in (1, 2)] + [width]
    return [(a, b) for a, b in zip(cuts, cuts[1:]) if b > a]


def reduce_open(part, axis, row_off, row_count):
    n = lax.axis_size(axis)
    levels = n.bit_length() - 1
    own = part.shape[0] // n
    cur = part.reshape((2,) * levels + (own, part.shape[1]))
    if (row_off, row_count) != (0, own):
        cur = lax.slice_in_dim(cur, row_off, row_off + row_count, axis=levels)
    return cur


def reduce_halves(cur, axis, bit):
    mine = (lax.axis_index(axis) // bit) % 2
    dim = cur.ndim - 2 - bit.bit_length()
    return lax.dynamic_slice_in_dim(cur, mine, 1, dim), lax.dynamic_slice_in_dim(cur, 1 - mine, 1, dim)


def reduce_step(halves, axis, bit, last):
    keep, send = halves
    total = keep.astype(F32) + permute_bit(send, axis, bit).astype(F32)
    return total if last else total.astype(BF16)


def reduce_rest(cur, axis, order):
    for bit in reversed(order):
        cur = reduce_step(reduce_halves(cur, axis, bit), axis, bit, bit == order[0])
    return cur.reshape(cur.shape[-2:])


def sum_cube(x, axis):
    n = lax.axis_size(axis)
    bit = 1
    while bit < n:
        x = (x.astype(F32) + permute_bit(x, axis, bit).astype(F32)).astype(x.dtype)
        bit *= 2
    return x


def tensor_gather(x, natural):
    n = lax.axis_size("tensor")
    rank = lax.axis_index("tensor")
    bit = 1
    while bit < n:
        other = permute_bit(x, "tensor", bit)
        if natural:
            low = (rank // bit) % 2 == 0
            x = jnp.concatenate([jnp.where(low, x, other), jnp.where(low, other, x)], axis=0)
        else:
            x = jnp.concatenate([x, other], axis=0)
        bit *= 2
    return x


def tensor_scatter(product, arrays, natural):
    n = lax.axis_size("tensor")
    rank = lax.axis_index("tensor")
    if n == 2:
        half = arrays[0].shape[0] // 2
        cut = lambda a, k: lax.dynamic_slice_in_dim(a, k * half, half, 0) if natural else (
            lax.slice_in_dim(a, k * half, (k + 1) * half, axis=0))
        mine, other = (rank, 1 - rank) if natural else (0, 1)
        send = product(*[cut(a, other) for a in arrays]).astype(BF16)
        arrived = permute_bit(send, "tensor", 1)
        return product(*[cut(a, mine) for a in arrays]) + arrived.astype(F32)
    x = product(*arrays)
    bit = n // 2
    while bit >= 1:
        half = x.shape[0] // 2
        if natural:
            mine = (rank // bit) % 2
            keep = lax.dynamic_slice_in_dim(x, mine * half, half, 0)
            send = lax.dynamic_slice_in_dim(x, (1 - mine) * half, half, 0)
        else:
            keep, send = x[:half], x[half:]
        x = keep.astype(F32) + permute_bit(send.astype(BF16), "tensor", bit).astype(F32)
        bit //= 2
    return x


def inverse_rms(v):
    return lax.rsqrt(jnp.mean(v * v, axis=-1, keepdims=True) + NORM_EPS)


def norm_back(v, inverse, gain, grad):
    u = grad * gain
    into = inverse * u - inverse ** 3 * v * jnp.mean(u * v, axis=-1, keepdims=True)
    return into, jnp.sum(grad * v * inverse, axis=0)


def rope_tables():
    half = HEAD_DIM // 2
    index = (jnp.arange(HEAD_DIM, dtype=jnp.int32) % half).astype(F32)
    frequency = jnp.exp(index * (-2.0 * math.log(ROPE_THETA) / HEAD_DIM))
    angles = jnp.arange(LEN, dtype=jnp.int32).astype(F32)[:, None] * frequency[None, :]
    return jnp.cos(angles), jnp.sin(angles)


def per_device(
    layer_input, segment_ids, out_grad, norm_gain, query_w, key_w, value_w, out_w, mamba_gate_w,
    mamba_in_w, state_in_w, step_w, channel_conv, state_conv, step_bias, decay_log, skip_gain,
    mamba_out_w, ffn_gain, ffn_gate_w, ffn_up_w, ffn_down_w,
):
    dp = lax.axis_size("dp")
    rank = lax.axis_index("tensor")
    me = lax.axis_index("dp").astype(jnp.int32).reshape(1)
    heads = query_w.shape[1] // HEAD_DIM
    ssm = step_w.shape[1]
    width = mamba_in_w.shape[1]
    q_width = query_w.shape[1]
    units = ffn_gate_w.shape[1]
    kv_index = rank * heads // (HEADS // KV_HEADS)
    features = layer_input.shape[1]
    block_rows = query_w.shape[0]
    half_rows = block_rows // 2
    orders = bit_orders("dp")

    key_own = lax.dynamic_slice_in_dim(key_w, kv_index * HEAD_DIM, HEAD_DIM, 1)
    value_own = lax.dynamic_slice_in_dim(value_w, kv_index * HEAD_DIM, HEAD_DIM, 1)
    qkv_shard = jnp.concatenate([query_w, key_own, value_own], axis=1)
    mix_shard = jnp.concatenate(
        [mamba_gate_w, mamba_in_w, state_in_w, jnp.pad(step_w, ((0, 0), (0, STATE - ssm)))], axis=1)
    total_cols = mix_shard.shape[1] + qkv_shard.shape[1]
    mix_cols = thirds(total_cols)
    mix_cols = [(a, min(b, mix_shard.shape[1])) for a, b in mix_cols if a < mix_shard.shape[1]]
    steps = len(orders[0])
    shards = [(mix_shard[:, a:b], 0, a, j) for j, (a, b) in enumerate(mix_cols)]
    shards.append((qkv_shard, 1, 0, 2))
    held = [p[0][None] for p in shards]
    for k in range(steps - 1):
        held = [gather_step(h, "dp", orders[p[3]][k]) for h, p in zip(held, shards)]

    later = jnp.concatenate([ffn_gate_w, ffn_up_w, ffn_down_w.T], axis=1)
    later, held = lax.optimization_barrier((later, held))
    later = lax.all_gather(later, "dp", axis=0, tiled=True)
    ffn_gate, ffn_up, ffn_down_t = (later[:, k * units:(k + 1) * units] for k in range(3))

    rels, plan = [], []
    for h, (_, dest, lane_off, j) in zip(held, shards):
        for rel, places in gather_last(h, "dp", orders[j]):
            rels.append(rel)
            plan.append((places, dest, 0, lane_off, block_rows))

    (out_shard, mout_shard), rels = lax.optimization_barrier(((out_w.T, mamba_out_w.T), rels))
    mix_w, qkv_w = assemble(me, rels, plan, [(features, mix_shard.shape[1]),
                                            (features, qkv_shard.shape[1])])
    shards2 = [(mout_shard[:half_rows], 1, 0, 0), (mout_shard[half_rows:], 1, half_rows, 1),
               (out_shard, 0, 0, 2)]
    held2 = [p[0][None] for p in shards2]

    def output_step(held, k):
        return [gather_step(h, "dp", orders[p[3]][k]) for h, p in zip(held, shards2)]

    tokens = layer_input.astype(F32)
    inverse = inverse_rms(tokens)
    normed = tensor_gather((tokens * inverse * norm_gain).astype(BF16), True)
    top_grad = tensor_gather(out_grad, False)
    rows = normed.shape[0]
    seqs = rows // LEN

    seg = segment_ids.reshape(seqs, LEN)
    seg_col = segment_ids[:, None]
    masks = token_masks(seg)
    starts = jnp.sum(seg[:, None, :] < seg[:, ::BQ, None], axis=-1, dtype=jnp.int32)
    first = (starts // BQ).reshape(-1)
    cos, sin = rope_tables()

    qkv = dot_nn(normed, qkv_w)
    for k in range(steps - 3):
        held2 = output_step(held2, k)
    normed_late, held2, qkv = lax.optimization_barrier((normed, held2, qkv))
    pre = dot_nn(normed_late, mix_w)
    held2 = output_step(held2, steps - 3)
    pre, held2 = lax.optimization_barrier((pre, held2))
    pad_heads = lambda a: jnp.pad(a[None], ((0, 0), (0, STATE - ssm)))
    bias, rate = pad_heads(step_bias), pad_heads(decay_log)
    skip = jnp.repeat(skip_gain, HEAD_DIM)[None]
    spread = jnp.pad(jnp.repeat(jnp.eye(ssm, dtype=BF16), HEAD_DIM, axis=1), ((0, STATE - ssm), (0, 0)))
    chunk_rows = segment_ids.reshape(-1, 1, Q)
    gated, scanned, states = mix_fwd(
        seg_col, chunk_rows, masks, pre, channel_conv, state_conv, bias, rate, skip, spread, ssm)

    held2 = output_step(held2, steps - 2)
    qkv, gated, held2 = lax.optimization_barrier((qkv, gated, held2))
    queries, key_rows, value_rows = rope(qkv, cos, sin)
    seg_blocks = segment_ids.reshape(-1, 1, BQ)
    attended, lse = attend_fwd(first, queries, key_rows, value_rows, seg_col, seg_blocks)
    rels2, plan2 = [], []
    for h, (_, dest, row_off, j) in zip(held2, shards2):
        for rel, places in gather_last(h, "dp", orders[j]):
            rels2.append(rel)
            plan2.append((places, dest, row_off, 0, block_rows))
    out_t, mout_t = assemble(me, rels2, plan2, [(features, q_width), (features, width)])

    branch = tensor_scatter(
        lambda a, b: dot_nt(a, out_t) + dot_nt(b, mout_t), (attended, gated), True)
    middle = tokens + branch
    mid_inverse = inverse_rms(middle)
    mid = tensor_gather((middle * mid_inverse * ffn_gain).astype(BF16), False)
    gate_vals = dot_nn(mid, ffn_gate).astype(BF16).astype(F32)
    up_vals = dot_nn(mid, ffn_up).astype(BF16).astype(F32)
    act = (jax.nn.silu(gate_vals) * up_vals).astype(BF16)
    block_out = (middle + tensor_scatter(lambda a: dot_nt(a, ffn_down_t), (act,), False)).astype(BF16)

    act_grad = dot_nn(top_grad, ffn_down_t)
    gate_sig = jax.nn.sigmoid(gate_vals)
    gate_grad = (act_grad * up_vals * silu_slope(gate_vals, gate_sig)).astype(BF16)
    up_grad = (act_grad * (gate_vals * gate_sig)).astype(BF16)
    mid_norm_grad = tensor_scatter(
        lambda a, b: dot_nt(a, ffn_gate) + dot_nt(b, ffn_up), (gate_grad, up_grad), False)
    down_part = dot_tn(top_grad, act).astype(BF16)
    gate_part = dot_tn(mid, gate_grad).astype(BF16)
    up_part = dot_tn(mid, up_grad).astype(BF16)
    by_owner = lambda a: a.reshape(dp, block_rows, units)
    ffn_sum = lax.psum_scatter(
        jnp.concatenate([by_owner(gate_part), by_owner(up_part), by_owner(down_part)], axis=1),
        "dp", scatter_dimension=0, tiled=True)[0]
    ffn_gate_w_grad, ffn_up_w_grad, ffn_down_w_grad = (
        ffn_sum[k * block_rows:(k + 1) * block_rows].astype(F32) for k in range(3))

    mid_into, ffn_gain_part = norm_back(middle, mid_inverse, ffn_gain, mid_norm_grad)
    middle_grad = out_grad.astype(F32) + mid_into
    branch_grad = tensor_gather(middle_grad.astype(BF16), True)
    attended_grad = dot_nn(branch_grad, out_t).astype(BF16)
    gated_grad = dot_nn(branch_grad, mout_t)
    out_part = dot_tn(branch_grad, attended).astype(BF16)
    mout_part = dot_tn(branch_grad, gated).astype(BF16)
    pieces2 = [(mout_part, 0, half_rows, 0), (mout_part, half_rows, half_rows, 1),
               (out_part, 0, block_rows, 2)]
    halves2 = [
        reduce_halves(reduce_open(p, "dp", off, count), "dp", orders[j][-1]) for p, off, count, j in pieces2]
    attended_grad, halves2 = lax.optimization_barrier((attended_grad, halves2))
    held2 = [reduce_step(h, "dp", orders[p[3]][-1], False) for h, p in zip(halves2, pieces2)]
    query_grad, key_grad, value_grad = attend_bwd(
        first, queries, key_rows, value_rows, attended_grad, seg_col, seg_blocks, lse, attended, cos, sin)
    qkv_grad = jnp.concatenate([query_grad, key_grad, value_grad], axis=1)
    halves2 = [reduce_halves(c, "dp", orders[p[3]][-2]) for c, p in zip(held2, pieces2)]
    gated_grad, qkv_grad, halves2 = lax.optimization_barrier((gated_grad, qkv_grad, halves2))
    held2 = [reduce_step(h, "dp", orders[p[3]][-2], False) for h, p in zip(halves2, pieces2)]
    mix_grad, conv_part, state_conv_part, head_part, skip_part = mix_bwd(
        seg_col, chunk_rows, masks, pre, scanned, states, gated_grad, channel_conv, state_conv, bias,
        rate, skip, spread, ssm)

    pieces1 = [(dot_tn(normed, mix_grad[:, a:b]).astype(BF16), j) for j, (a, b) in enumerate(mix_cols)]
    pieces1.append((dot_tn(normed, qkv_grad).astype(BF16), 2))
    halves1 = [reduce_halves(reduce_open(p, "dp", 0, block_rows), "dp", orders[j][-1]) for p, j in pieces1]
    mix_grad_late, halves1 = lax.optimization_barrier((mix_grad, halves1))
    held1 = [reduce_step(h, "dp", orders[p[1]][-1], False) for h, p in zip(halves1, pieces1)]
    normed_grad = tensor_scatter(
        lambda a, b: dot_nt(a, qkv_w) + dot_nt(b, mix_w), (qkv_grad, mix_grad_late), True)
    norm_into, norm_gain_part = norm_back(tokens, inverse, norm_gain, normed_grad)
    input_grad = middle_grad + norm_into

    heads_part = jnp.concatenate([
        head_part[0, :ssm], head_part[1, :ssm],
        jnp.sum(skip_part.reshape(ssm, HEAD_DIM), axis=1)])
    small = jnp.concatenate([
        conv_part.reshape(-1), heads_part, state_conv_part.reshape(-1), ffn_gain_part,
        norm_gain_part])
    small_bits = list(bit_orders("dp")[0])
    tail = [(c, list(reversed(orders[p[1]][:-1]))) for c, p in zip(held1, pieces1)]
    tail += [(c, list(reversed(orders[p[3]][:-2]))) for c, p in zip(held2, pieces2)]
    cur = [c for c, _ in tail]
    for k in range(steps - 1):
        cur, small = lax.optimization_barrier((cur, small))
        bit = small_bits.pop()
        small = small + permute_bit(small, "dp", bit)
        cur = [
            reduce_step(reduce_halves(c, "dp", bits[k]), "dp", bits[k], k == len(bits) - 1)
            if k < len(bits) else c for c, (_, bits) in zip(cur, tail)]
    while small_bits:
        small = small + permute_bit(small, "dp", small_bits.pop())
    sums = [c.reshape(c.shape[-2:]) for c in cur]
    mix_sum = jnp.concatenate(sums[:len(mix_cols)], axis=1)
    qkv_sum = sums[len(mix_cols)]
    mout_a, mout_b, out_sum = sums[len(mix_cols) + 1:]
    mamba_out_w_grad = jnp.concatenate([mout_a, mout_b], axis=0).T
    out_w_grad = out_sum.T

    place = lambda a, whole: lax.dynamic_update_slice_in_dim(
        jnp.zeros((block_rows, whole.shape[1]), BF16), a.astype(BF16), kv_index * HEAD_DIM, 1)
    shared = sum_cube(jnp.concatenate([
        place(qkv_sum[:, q_width:q_width + HEAD_DIM], key_w),
        place(qkv_sum[:, q_width + HEAD_DIM:], value_w),
        mix_sum[:, 2 * width:2 * width + 2 * STATE].astype(BF16)], axis=1), "tensor").astype(F32)
    kv_cols = key_w.shape[1]

    own = 4 * width + 3 * ssm
    conv_grad = small[:4 * width].reshape(4, width)
    bias_grad, decay_grad, skip_grad = (
        small[4 * width + k * ssm:4 * width + (k + 1) * ssm] for k in range(3))
    both = sum_cube(small[own:], "tensor")
    state_conv_grad = both[:8 * STATE].reshape(4, 2 * STATE)
    ffn_gain_grad = both[8 * STATE:8 * STATE + features]
    gain = both[8 * STATE + features:]
    return (
        block_out,
        input_grad,
        gain,
        qkv_sum[:, :q_width],
        shared[:, :kv_cols],
        shared[:, kv_cols:2 * kv_cols],
        out_w_grad,
        mix_sum[:, :width],
        mix_sum[:, width:2 * width],
        shared[:, 2 * kv_cols:],
        mix_sum[:, 2 * width + 2 * STATE:2 * width + 2 * STATE + ssm],
        conv_grad,
        state_conv_grad,
        bias_grad,
        decay_grad,
        skip_grad,
        mamba_out_w_grad,
        ffn_gain_grad,
        ffn_gate_w_grad,
        ffn_up_w_grad,
        ffn_down_w_grad.T,
    )


def solution(mesh):
    in_specs = (
        P(("dp", "tensor"), None),
        P("dp"),
        P(("dp", "tensor"), None),
        P(),
        P("dp", "tensor"),
        P("dp", None),
        P("dp", None),
        P("tensor", "dp"),
        P("dp", "tensor"),
        P("dp", "tensor"),
        P("dp", None),
        P("dp", "tensor"),
        P(None, "tensor"),
        P(),
        P("tensor"),
        P("tensor"),
        P("tensor"),
        P("tensor", "dp"),
        P(),
        P("dp", "tensor"),
        P("dp", "tensor"),
        P("tensor", "dp"),
    )
    out_specs = (
        P(("dp", "tensor"), None),
        P(("dp", "tensor"), None),
        P(),
        P("dp", "tensor"),
        P("dp", None),
        P("dp", None),
        P("tensor", "dp"),
        P("dp", "tensor"),
        P("dp", "tensor"),
        P("dp", None),
        P("dp", "tensor"),
        P(None, "tensor"),
        P(),
        P("tensor"),
        P("tensor"),
        P("tensor"),
        P("tensor", "dp"),
        P(),
        P("dp", "tensor"),
        P("dp", "tensor"),
        P("tensor", "dp"),
    )
    return jax.shard_map(
        per_device, mesh=mesh, in_specs=in_specs, out_specs=out_specs, check_vma=False
    )
```

```python
import functools
import math

import jax
import jax.numpy as jnp
from jax import lax
from jax.experimental import pallas as pl
from jax.experimental.pallas import tpu as pltpu
from jax.sharding import PartitionSpec as P

HEAD_DIM = 64
STATE = 128
LEN = 2048
BQ = 512
Q = 128
HALO = 8
NEG = -1e30
PRECISE = lax.Precision.HIGHEST
F32 = jnp.float32
BF16 = jnp.bfloat16
VMEM_BYTES = 48 * 1024 * 1024


def dot_nn(left, right):
    return lax.dot_general(left, right, (((1,), (0,)), ((), ())), preferred_element_type=F32)


def dot_nt(left, right):
    return lax.dot_general(left, right, (((1,), (1,)), ((), ())), preferred_element_type=F32)


def dot_tn(left, right):
    return lax.dot_general(left, right, (((0,), (0,)), ((), ())), preferred_element_type=F32)


def pieces(a, count):
    parts = []
    for _ in range(count):
        parts.append(a.astype(BF16))
        a = a - parts[-1].astype(F32)
    return parts


def rope_kernel(heads, qkv_ref, cos_ref, sin_ref, q_ref, k_ref, v_ref):
    half = HEAD_DIM // 2
    cos, sin = cos_ref[...], sin_ref[...]

    def turn(x):
        return x * cos + jnp.concatenate([-x[:, half:], x[:, :half]], axis=1) * sin

    for h in range(heads):
        lanes = slice(h * HEAD_DIM, (h + 1) * HEAD_DIM)
        q_ref[:, lanes] = (turn(qkv_ref[:, lanes]).astype(BF16) * HEAD_DIM ** -0.5).astype(BF16)
    edge = heads * HEAD_DIM
    k_ref[...] = turn(qkv_ref[:, edge:edge + HEAD_DIM]).astype(BF16)
    v_ref[:, :HEAD_DIM] = qkv_ref[:, edge + HEAD_DIM:].astype(BF16)
    v_ref[:, HEAD_DIM:] = jnp.ones((v_ref.shape[0], HEAD_DIM), BF16)


def rope(qkv, cos, sin):
    rows, width = qkv.shape
    heads = width // HEAD_DIM - 2
    per = LEN // BQ
    blk = lambda w: pl.BlockSpec((BQ, w), lambda i: (i, 0))
    table = pl.BlockSpec((BQ, HEAD_DIM), lambda i: (lax.rem(i, per), 0))
    return pl.pallas_call(
        functools.partial(rope_kernel, heads),
        grid=(rows // BQ,),
        in_specs=[blk(width), table, table],
        out_specs=[blk(heads * HEAD_DIM), blk(HEAD_DIM), blk(2 * HEAD_DIM)],
        out_shape=[
            jax.ShapeDtypeStruct((rows, heads * HEAD_DIM), BF16),
            jax.ShapeDtypeStruct((rows, HEAD_DIM), BF16),
            jax.ShapeDtypeStruct((rows, 2 * HEAD_DIM), BF16),
        ],
        compiler_params=pltpu.CompilerParams(vmem_limit_bytes=VMEM_BYTES),
        cost_estimate=pl.CostEstimate(
            flops=rows * width * 8, bytes_accessed=rows * width * 6, transcendentals=0),
        name="rope",
    )(qkv, cos, sin)


def attend_fwd_kernel(heads, first_ref, q_ref, k_ref, v_ref, seg_ref, segrow_ref, out_ref, lse_ref,
                      top_ref, acc_ref):
    seq = pl.program_id(0)
    block = pl.program_id(1)
    top_ref[...] = jnp.full_like(top_ref, NEG)
    acc_ref[...] = jnp.zeros_like(acc_ref)
    key_pos = lax.broadcasted_iota(jnp.int32, (BQ, BQ), 0)
    row_pos = lax.broadcasted_iota(jnp.int32, (BQ, BQ), 1)

    def step(j, carry):
        at = pl.ds(pl.multiple_of(j * BQ, BQ), BQ)
        k = k_ref[at, :]
        v = v_ref[at, :]
        allowed = (segrow_ref[0] == seg_ref[at, :]) & (key_pos + (j - block) * BQ <= row_pos)
        bias = jnp.where(allowed, 0.0, NEG)
        for h in range(heads):
            s = dot_nt(k, q_ref[:, h * HEAD_DIM:(h + 1) * HEAD_DIM]) + bias
            old = top_ref[h]
            new = jnp.maximum(old, jnp.max(s, axis=0, keepdims=True))
            shrink = jnp.broadcast_to(jnp.exp(old - new), (2 * HEAD_DIM, BQ)).T
            p = jnp.exp(s - new).astype(BF16)
            acc_ref[h] = acc_ref[h] * shrink + dot_tn(p, v)
            top_ref[h] = new
        return carry

    lax.fori_loop(first_ref[seq * (LEN // BQ) + block], block + 1, step, 0)
    for h in range(heads):
        acc = acc_ref[h]
        out_ref[:, h * HEAD_DIM:(h + 1) * HEAD_DIM] = (
            acc[:, :HEAD_DIM] / acc[:, HEAD_DIM:]).astype(BF16)
        lse_ref[0, h:h + 1, :] = top_ref[h] + jnp.log(acc.T[HEAD_DIM:HEAD_DIM + 1, :])


def attend_fwd(first, q, k, v, seg_col, seg_rows):
    rows, width = q.shape
    heads = width // HEAD_DIM
    seqs = rows // LEN
    per = LEN // BQ
    return pl.pallas_call(
        functools.partial(attend_fwd_kernel, heads),
        grid_spec=pltpu.PrefetchScalarGridSpec(
            num_scalar_prefetch=1,
            grid=(seqs, per),
            in_specs=[
                pl.BlockSpec((BQ, width), lambda s, i, f: (s * per + i, 0)),
                pl.BlockSpec((LEN, HEAD_DIM), lambda s, i, f: (s, 0)),
                pl.BlockSpec((LEN, 2 * HEAD_DIM), lambda s, i, f: (s, 0)),
                pl.BlockSpec((LEN, 1), lambda s, i, f: (s, 0)),
                pl.BlockSpec((1, 1, BQ), lambda s, i, f: (s * per + i, 0, 0)),
            ],
            out_specs=[
                pl.BlockSpec((BQ, width), lambda s, i, f: (s * per + i, 0)),
                pl.BlockSpec((1, heads, BQ), lambda s, i, f: (s * per + i, 0, 0)),
            ],
            scratch_shapes=[
                pltpu.VMEM((heads, 1, BQ), F32),
                pltpu.VMEM((heads, BQ, 2 * HEAD_DIM), F32),
            ],
        ),
        out_shape=[
            jax.ShapeDtypeStruct((rows, width), BF16),
            jax.ShapeDtypeStruct((seqs * per, heads, BQ), F32),
        ],
        compiler_params=pltpu.CompilerParams(vmem_limit_bytes=VMEM_BYTES),
        cost_estimate=pl.CostEstimate(
            flops=2 * rows * LEN * width, bytes_accessed=4 * rows * width,
            transcendentals=rows * LEN * heads // 2),
        name="attend_fwd",
    )(first, q, k, v, seg_col, seg_rows)


def attend_bwd_kernel(heads, first_ref, q_ref, k_ref, v_ref, g_ref, seg_ref, segrow_ref, lse_ref,
                      out_ref, cos_ref, sin_ref, cosk_ref, sink_ref, dq_ref, dk_ref, dv_ref,
                      dqs_ref, dks_ref, dvs_ref, delta_ref):
    seq = pl.program_id(0)
    block = pl.program_id(1)
    half = HEAD_DIM // 2
    scale = HEAD_DIM ** -0.5

    @pl.when(block == 0)
    def _():
        dks_ref[...] = jnp.zeros_like(dks_ref)
        dvs_ref[...] = jnp.zeros_like(dvs_ref)

    dqs_ref[...] = jnp.zeros_like(dqs_ref)
    ones = jnp.ones((16, HEAD_DIM), BF16)
    high, less = pieces(g_ref[...].astype(F32) * out_ref[...].astype(F32), 2)
    for h in range(heads):
        lanes = slice(h * HEAD_DIM, (h + 1) * HEAD_DIM)
        delta_ref[h] = (dot_nt(ones, high[:, lanes]) + dot_nt(ones, less[:, lanes]))[0:1, :]
    key_pos = lax.broadcasted_iota(jnp.int32, (BQ, BQ), 0)
    row_pos = lax.broadcasted_iota(jnp.int32, (BQ, BQ), 1)

    def step(j, carry):
        at = pl.ds(pl.multiple_of(j * BQ, BQ), BQ)
        k = k_ref[at, :]
        v = v_ref[at, :HEAD_DIM]
        allowed = (segrow_ref[0] == seg_ref[at, :]) & (key_pos + (j - block) * BQ <= row_pos)
        bias = jnp.where(allowed, 0.0, NEG)
        dk = jnp.zeros((BQ, HEAD_DIM), F32)
        dv = jnp.zeros((BQ, HEAD_DIM), F32)
        for h in range(heads):
            lanes = slice(h * HEAD_DIM, (h + 1) * HEAD_DIM)
            q = q_ref[:, lanes]
            g = g_ref[:, lanes]
            s = dot_nt(k, q) + bias
            p = jnp.exp(s - lse_ref[0, h:h + 1, :])
            dp = dot_nt(v, g)
            ds = (p * (dp - delta_ref[h])).astype(BF16)
            dv = dv + dot_nn(p.astype(BF16), g)
            dk = dk + dot_nn(ds, q)
            dqs_ref[h] = dqs_ref[h] + dot_tn(ds, k)
        dks_ref[at, :] = dks_ref[at, :] + dk
        dvs_ref[at, :] = dvs_ref[at, :] + dv
        return carry

    lax.fori_loop(first_ref[seq * (LEN // BQ) + block], block + 1, step, 0)

    def turn_back(x, cos, sin):
        swapped = jnp.concatenate([x[:, half:], -x[:, :half]], axis=1)
        return x * cos + swapped * sin

    for h in range(heads):
        dq = turn_back(dqs_ref[h] * scale, cos_ref[...], sin_ref[...])
        dq_ref[:, h * HEAD_DIM:(h + 1) * HEAD_DIM] = dq.astype(BF16)

    @pl.when(block == pl.num_programs(1) - 1)
    def _():
        dk_ref[...] = turn_back(dks_ref[...], cosk_ref[...], sink_ref[...]).astype(BF16)
        dv_ref[...] = dvs_ref[...].astype(BF16)


def attend_bwd(first, q, k, v, g, seg_col, seg_rows, lse_rows, attended, cos, sin):
    rows, width = q.shape
    heads = width // HEAD_DIM
    seqs = rows // LEN
    per = LEN // BQ
    return pl.pallas_call(
        functools.partial(attend_bwd_kernel, heads),
        grid_spec=pltpu.PrefetchScalarGridSpec(
            num_scalar_prefetch=1,
            grid=(seqs, per),
            in_specs=[
                pl.BlockSpec((BQ, width), lambda s, i, f: (s * per + i, 0)),
                pl.BlockSpec((LEN, HEAD_DIM), lambda s, i, f: (s, 0)),
                pl.BlockSpec((LEN, 2 * HEAD_DIM), lambda s, i, f: (s, 0)),
                pl.BlockSpec((BQ, width), lambda s, i, f: (s * per + i, 0)),
                pl.BlockSpec((LEN, 1), lambda s, i, f: (s, 0)),
                pl.BlockSpec((1, 1, BQ), lambda s, i, f: (s * per + i, 0, 0)),
                pl.BlockSpec((1, heads, BQ), lambda s, i, f: (s * per + i, 0, 0)),
                pl.BlockSpec((BQ, width), lambda s, i, f: (s * per + i, 0)),
                pl.BlockSpec((BQ, HEAD_DIM), lambda s, i, f: (i, 0)),
                pl.BlockSpec((BQ, HEAD_DIM), lambda s, i, f: (i, 0)),
                pl.BlockSpec((LEN, HEAD_DIM), lambda s, i, f: (0, 0)),
                pl.BlockSpec((LEN, HEAD_DIM), lambda s, i, f: (0, 0)),
            ],
            out_specs=[
                pl.BlockSpec((BQ, width), lambda s, i, f: (s * per + i, 0)),
                pl.BlockSpec((LEN, HEAD_DIM), lambda s, i, f: (s, 0)),
                pl.BlockSpec((LEN, HEAD_DIM), lambda s, i, f: (s, 0)),
            ],
            scratch_shapes=[
                pltpu.VMEM((heads, BQ, HEAD_DIM), F32),
                pltpu.VMEM((LEN, HEAD_DIM), F32),
                pltpu.VMEM((LEN, HEAD_DIM), F32),
                pltpu.VMEM((heads, 1, BQ), F32),
            ],
        ),
        out_shape=[
            jax.ShapeDtypeStruct((rows, width), BF16),
            jax.ShapeDtypeStruct((rows, HEAD_DIM), BF16),
            jax.ShapeDtypeStruct((rows, HEAD_DIM), BF16),
        ],
        compiler_params=pltpu.CompilerParams(vmem_limit_bytes=VMEM_BYTES),
        cost_estimate=pl.CostEstimate(
            flops=5 * rows * LEN * width, bytes_accessed=8 * rows * width,
            transcendentals=rows * LEN * heads // 2),
        name="attend_bwd",
    )(first, q, k, v, g, seg_col, seg_rows, lse_rows, attended, cos, sin, cos, sin)


LAG, LEAD, CARRIED, ENDING = 0, 3, 6, 7


def token_masks(seg):
    seqs = seg.shape[0]
    padded = jnp.pad(seg, ((0, 0), (3, 3)), constant_values=-1)
    columns = [padded[:, 3 - k:3 - k + LEN] == seg for k in (1, 2, 3)]
    columns += [padded[:, 3 + k:3 + k + LEN] == seg for k in (1, 2, 3)]
    chunks = seg.reshape(seqs, LEN // Q, Q)
    prior = jnp.pad(chunks[:, :-1, -1:], ((0, 0), (1, 0), (0, 0)), constant_values=-1)
    columns.append((chunks == prior).reshape(seqs, LEN))
    columns.append((chunks == chunks[:, :, -1:]).reshape(seqs, LEN))
    return jnp.stack(columns, axis=-1).astype(F32).reshape(seqs * LEN, 8)


def shifted_conv(buf_ref, width, masks, taps):
    rows = [buf_ref[HALO - k:HALO - k + Q, :width] for k in range(4)]
    rows = [rows[0]] + [rows[k] * masks[:, LAG + k - 1:LAG + k] for k in (1, 2, 3)]
    total = rows[0] * taps[3:4, :]
    for k in (1, 2, 3):
        total = total + rows[k] * taps[3 - k:4 - k, :]
    return total, rows


def softplus(x):
    return jnp.maximum(x, 0.0) + jnp.log1p(jnp.exp(-jnp.abs(x)))


def spread_heads(columns, spread):
    stack = jnp.concatenate(columns, axis=0)
    high, less = pieces(stack, 2)
    wide = dot_nn(high, spread) + dot_nn(less, spread)
    return [wide[k * Q:(k + 1) * Q] for k in range(len(columns))]


def ones_times(ones, a, count):
    width = a.shape[1]
    total = dot_nn(ones, jnp.concatenate(pieces(a, count), axis=1))
    parts = [total[:, k * width:(k + 1) * width] for k in range(count)]
    return functools.reduce(jnp.add, parts)


def chunk_masks(seg_ref, segrow_ref):
    row = lax.broadcasted_iota(jnp.int32, (Q, Q), 0)
    col = lax.broadcasted_iota(jnp.int32, (Q, Q), 1)
    same = seg_ref[...] == segrow_ref[0]
    return row, col, same


def split_pre(ref, width):
    return (ref.at[:, pl.ds(0, width)], ref.at[:, pl.ds(width, width)],
            ref.at[:, pl.ds(2 * width, 3 * STATE)])


def mix_fwd_kernel(heads, seg_ref, segrow_ref, mask_ref, pre_ref, cw_ref,
                   sw_ref, bias_ref, rate_ref, skip_ref, spread_ref, gated_ref, y_ref, states_ref,
                   carry_ref, buf_ref, sbuf_ref):
    width = y_ref.shape[1]
    gate_ref, inner_ref, ss_ref = split_pre(pre_ref, width)

    @pl.when(pl.program_id(1) == 0)
    def _():
        carry_ref[...] = jnp.zeros_like(carry_ref)
        buf_ref[0:HALO, :] = jnp.zeros((HALO, buf_ref.shape[1]), F32)
        sbuf_ref[0:HALO, :] = jnp.zeros((HALO, sbuf_ref.shape[1]), F32)

    masks = mask_ref[...]
    buf_ref[HALO:HALO + Q, :] = inner_ref[...]
    sbuf_ref[HALO:HALO + Q, :] = ss_ref[:, :2 * STATE]
    z, _ = shifted_conv(buf_ref, buf_ref.shape[1], masks, cw_ref[...])
    zs, _ = shifted_conv(sbuf_ref, 2 * STATE, masks, sw_ref[...])
    buf_ref[0:HALO, :] = buf_ref[Q:Q + HALO, :]
    sbuf_ref[0:HALO, :] = sbuf_ref[Q:Q + HALO, :]
    x = z * jax.nn.sigmoid(z)
    states = (zs * jax.nn.sigmoid(zs)).astype(BF16)
    entry = states[:, :STATE]
    readout = states[:, STATE:]
    size = softplus(ss_ref[:, 2 * STATE:] + bias_ref[...])
    decay = -size * jnp.exp(rate_ref[...])
    row, col, same = chunk_masks(seg_ref, segrow_ref)
    cum = ones_times(jnp.where(row >= col, 1.0, 0.0).astype(BF16), decay, 3)
    cum_rows = cum.T
    bias = jnp.where((row >= col) & same, 0.0, NEG)
    spread = spread_ref[...]
    into = jnp.exp(cum) * masks[:, CARRIED:CARRIED + 1]
    tail = jnp.exp(cum[Q - 1:Q, :] - cum) * masks[:, ENDING:ENDING + 1]
    size_wide, into_wide, tail_wide = spread_heads([size, into, tail], spread)
    xs = (x * size_wide)
    xs_low = xs.astype(BF16)
    pair = dot_nt(readout, entry)
    prior = carry_ref[...]
    states_ref[0] = prior
    y = dot_nn(readout, prior.astype(BF16)) * into_wide
    for h in range(heads):
        lanes = slice(h * HEAD_DIM, (h + 1) * HEAD_DIM)
        mix = (pair * jnp.exp(cum[:, h:h + 1] - cum_rows[h:h + 1, :] + bias)).astype(BF16)
        y_ref[:, lanes] = dot_nn(mix, xs_low[:, lanes])
    y = y + y_ref[...]
    y_ref[...] = y
    fresh = dot_tn(entry, (xs * tail_wide).astype(BF16))
    carry_ref[...] = prior * into_wide[Q - 1:Q, :] + fresh
    gate = gate_ref[...]
    gated_ref[...] = ((y + skip_ref[...] * x) * (gate * jax.nn.sigmoid(gate))).astype(BF16)


def mix_fwd(seg_col, seg_rows, masks, pre, cw, sw, bias, rate, skip, spread,
            heads):
    rows, width = pre.shape[0], cw.shape[1]
    seqs = rows // LEN
    per = LEN // Q
    pre_width = pre.shape[1]
    blk = lambda w: pl.BlockSpec((Q, w), lambda s, c: (s * per + c, 0))
    whole = lambda a: pl.BlockSpec(a.shape, lambda s, c: (0, 0))
    return pl.pallas_call(
        functools.partial(mix_fwd_kernel, heads),
        grid=(seqs, per),
        in_specs=[
            blk(1),
            pl.BlockSpec((1, 1, Q), lambda s, c: (s * per + c, 0, 0)),
            blk(8), blk(pre_width),
            whole(cw), whole(sw), whole(bias), whole(rate), whole(skip), whole(spread),
        ],
        out_specs=[
            blk(width), blk(width),
            pl.BlockSpec((1, STATE, width), lambda s, c: (s * per + c, 0, 0)),
        ],
        out_shape=[
            jax.ShapeDtypeStruct((rows, width), BF16),
            jax.ShapeDtypeStruct((rows, width), F32),
            jax.ShapeDtypeStruct((seqs * per, STATE, width), F32),
        ],
        scratch_shapes=[
            pltpu.VMEM((STATE, width), F32),
            pltpu.VMEM((Q + HALO, width), F32),
            pltpu.VMEM((Q + HALO, 2 * STATE), F32),
        ],
        compiler_params=pltpu.CompilerParams(vmem_limit_bytes=VMEM_BYTES),
        cost_estimate=pl.CostEstimate(
            flops=rows * width * 1200, bytes_accessed=rows * width * 22,
            transcendentals=rows * width * 4),
        name="mix_fwd",
    )(seg_col, seg_rows, masks, pre, cw, sw, bias, rate, skip, spread)


def lead_sum(buf_ref, masks, taps):
    total = buf_ref[0:Q, :] * taps[3:4, :]
    for k in (1, 2, 3):
        total = total + buf_ref[k:k + Q, :] * masks[:, LEAD + k - 1:LEAD + k] * taps[3 - k:4 - k, :]
    return total


def column_sum(a):
    return jnp.sum(a, axis=0, keepdims=True)


def silu_slope(v, sig):
    return sig * (1.0 + v * (1.0 - sig))


def mix_bwd_kernel(heads, seg_ref, segrow_ref, mask_ref, pre_ref, pre_prev_ref, y_ref, states_ref, dout_ref, cw_ref, sw_ref, bias_ref, rate_ref,
                   skip_ref, spread_ref, dpre_ref, dcw_ref, dsw_ref, dhead_ref,
                   dskip_ref, carry_ref, buf_ref, sbuf_ref, dxs_ref, dz_ref, dzs_ref):
    width = y_ref.shape[1]
    gate_ref, inner_ref, ss_ref = split_pre(pre_ref, width)
    _, inner_prev_ref, ss_prev_ref = split_pre(pre_prev_ref, width)
    dgate_ref, dinner_ref, dss_ref = split_pre(dpre_ref, width)

    @pl.when((pl.program_id(0) == 0) & (pl.program_id(1) == 0))
    def _():
        dcw_ref[...] = jnp.zeros_like(dcw_ref)
        dsw_ref[...] = jnp.zeros_like(dsw_ref)
        dhead_ref[...] = jnp.zeros_like(dhead_ref)
        dskip_ref[...] = jnp.zeros_like(dskip_ref)

    @pl.when(pl.program_id(1) == 0)
    def _():
        carry_ref[...] = jnp.zeros_like(carry_ref)
        dz_ref[Q:Q + HALO, :] = jnp.zeros((HALO, width), F32)
        dzs_ref[Q:Q + HALO, :] = jnp.zeros((HALO, 2 * STATE), F32)

    masks = mask_ref[...]
    buf_ref[0:HALO, :] = inner_prev_ref[...]
    buf_ref[HALO:HALO + Q, :] = inner_ref[...]
    sbuf_ref[0:HALO, :] = ss_prev_ref[:, :2 * STATE]
    sbuf_ref[HALO:HALO + Q, :] = ss_ref[:, :2 * STATE]
    z, z_rows = shifted_conv(buf_ref, width, masks, cw_ref[...])
    zs, zs_rows = shifted_conv(sbuf_ref, 2 * STATE, masks, sw_ref[...])
    sig_z = jax.nn.sigmoid(z)
    sig_zs = jax.nn.sigmoid(zs)
    x = z * sig_z
    states = (zs * sig_zs).astype(BF16)
    entry = states[:, :STATE]
    readout = states[:, STATE:]
    raw = ss_ref[:, 2 * STATE:] + bias_ref[...]
    size = softplus(raw)
    rate = jnp.exp(rate_ref[...])
    decay = -size * rate
    row, col, same = chunk_masks(seg_ref, segrow_ref)
    cum = ones_times(jnp.where(row >= col, 1.0, 0.0).astype(BF16), decay, 3)
    cum_rows = cum.T
    bias = jnp.where((row <= col) & same, 0.0, NEG)
    spread = spread_ref[...]
    into = jnp.exp(cum) * masks[:, CARRIED:CARRIED + 1]
    tail = jnp.exp(cum[Q - 1:Q, :] - cum) * masks[:, ENDING:ENDING + 1]
    size_wide, into_wide, tail_wide = spread_heads([size, into, tail], spread)
    xs = x * size_wide
    xs_low = xs.astype(BF16)
    gate = gate_ref[...]
    sig = jax.nn.sigmoid(gate)
    dout = dout_ref[...]
    y = y_ref[...]
    skip = skip_ref[...]
    dgate_ref[...] = (dout * (y + skip * x) * silu_slope(gate, sig)).astype(BF16)
    g = dout * (gate * sig)
    g_low = g.astype(BF16)
    dskip_ref[...] += column_sum(g * x)
    pair = dot_nt(entry, readout)
    dpair = jnp.zeros((Q, Q), F32)
    for h in range(heads):
        lanes = slice(h * HEAD_DIM, (h + 1) * HEAD_DIM)
        fade = jnp.exp(cum_rows[h:h + 1, :] - cum[:, h:h + 1] + bias)
        dxs_ref[:, lanes] = dot_nn((pair * fade).astype(BF16), g_low[:, lanes])
        dpair = dpair + dot_nt(xs_low[:, lanes], g_low[:, lanes]) * fade
    prior = states_ref[0]
    after = carry_ref[...]
    after_low = after.astype(BF16)
    from_tail = dot_nn(entry, after_low) * tail_wide
    dxs = dxs_ref[...] + from_tail
    g_into = (g * into_wide).astype(BF16)
    dpair_low = dpair.astype(BF16)
    dreadout = dot_tn(dpair_low, entry) + dot_nt(g_into, prior.astype(BF16))
    dentry = dot_nn(dpair_low, readout) + dot_nt((xs * tail_wide).astype(BF16), after_low)
    keep = into_wide[Q - 1:Q, :]
    carry_ref[...] = after * keep + dot_tn(readout, g_into)
    xs_round = xs_low.astype(F32)
    end_sum = column_sum(xs_round * from_tail) + keep * column_sum(after * prior)
    terms = jnp.concatenate([
        g_low.astype(F32) * y - xs_round * dxs, x * dxs, jnp.broadcast_to(end_sum, (16, width))], axis=0)
    high, less = pieces(terms, 2)
    sums = dot_nt(high, spread) + dot_nt(less, spread)
    end_heads = sums[2 * Q:2 * Q + 1]
    last_row = lax.broadcasted_iota(jnp.int32, (Q, STATE), 0) == Q - 1
    dcum = sums[:Q] + jnp.where(last_row, end_heads, 0.0)
    ddecay = ones_times(jnp.where(row <= col, 1.0, 0.0).astype(BF16), dcum, 3)
    dsize = sums[Q:2 * Q] - ddecay * rate
    draw = dsize * jax.nn.sigmoid(raw)
    dhead_ref[0:1, :] += column_sum(draw)
    dhead_ref[1:2, :] += column_sum(ddecay * decay)
    dz = (size_wide * dxs + skip * g) * silu_slope(z, sig_z)
    dz_ref[0:Q, :] = dz
    for k in range(4):
        dcw_ref[3 - k:4 - k, :] += column_sum(dz * z_rows[k])
    dinner_ref[...] = lead_sum(dz_ref, masks, cw_ref[...]).astype(BF16)
    dz_ref[Q:Q + HALO, :] = dz_ref[0:HALO, :]
    dzs = jnp.concatenate([dentry, dreadout], axis=1) * silu_slope(zs, sig_zs)
    dzs_ref[0:Q, :] = dzs
    for k in range(4):
        dsw_ref[3 - k:4 - k, :] += column_sum(dzs * zs_rows[k])
    dss_ref[:, :2 * STATE] = lead_sum(dzs_ref, masks, sw_ref[...]).astype(BF16)
    dzs_ref[Q:Q + HALO, :] = dzs_ref[0:HALO, :]
    dss_ref[:, 2 * STATE:] = draw.astype(BF16)


def mix_bwd(seg_col, seg_rows, masks, pre, y, states, dout, cw, sw, bias, rate, skip, spread, heads):
    rows, width = pre.shape[0], cw.shape[1]
    seqs = rows // LEN
    per = LEN // Q
    pre_width = pre.shape[1]
    at = lambda s, c: s * per + per - 1 - c
    blk = lambda w: pl.BlockSpec((Q, w), lambda s, c: (at(s, c), 0))
    prev = lambda w: pl.BlockSpec(
        (HALO, w), lambda s, c: (jnp.maximum(at(s, c) * (Q // HALO) - 1, 0), 0))
    whole = lambda shape: pl.BlockSpec(shape, lambda s, c: (0, 0))
    return pl.pallas_call(
        functools.partial(mix_bwd_kernel, heads),
        grid=(seqs, per),
        in_specs=[
            blk(1),
            pl.BlockSpec((1, 1, Q), lambda s, c: (at(s, c), 0, 0)),
            blk(8), blk(pre_width), prev(pre_width), blk(width),
            pl.BlockSpec((1, STATE, width), lambda s, c: (at(s, c), 0, 0)),
            blk(width),
            whole(cw.shape), whole(sw.shape), whole(bias.shape), whole(rate.shape),
            whole(skip.shape), whole(spread.shape),
        ],
        out_specs=[
            blk(pre_width),
            whole((4, width)), whole((4, 2 * STATE)), whole((8, STATE)), whole((1, width)),
        ],
        out_shape=[
            jax.ShapeDtypeStruct((rows, pre_width), BF16),
            jax.ShapeDtypeStruct((4, width), F32),
            jax.ShapeDtypeStruct((4, 2 * STATE), F32),
            jax.ShapeDtypeStruct((8, STATE), F32),
            jax.ShapeDtypeStruct((1, width), F32),
        ],
        scratch_shapes=[
            pltpu.VMEM((STATE, width), F32),
            pltpu.VMEM((Q + HALO, width), F32),
            pltpu.VMEM((Q + HALO, 2 * STATE), F32),
            pltpu.VMEM((Q, width), F32),
            pltpu.VMEM((Q + HALO, width), F32),
            pltpu.VMEM((Q + HALO, 2 * STATE), F32),
        ],
        compiler_params=pltpu.CompilerParams(vmem_limit_bytes=VMEM_BYTES),
        cost_estimate=pl.CostEstimate(
            flops=rows * width * 3000, bytes_accessed=rows * width * 28,
            transcendentals=rows * width * 4),
        name="mix_bwd",
    )(seg_col, seg_rows, masks, pre, pre, y, states, dout, cw, sw, bias,
      rate, skip, spread)


NORM_EPS = 1e-05
ROPE_THETA = 100000000000.0
KV_HEADS = 2
HEADS = 8
LANES = 128


def permute_bit(x, axis, bit):
    n = lax.axis_size(axis)
    return lax.ppermute(x, axis, [(i, i ^ bit) for i in range(n)])


def bit_orders(axis):
    n = lax.axis_size(axis)
    bits = [n >> (k + 1) for k in range(n.bit_length() - 1)]
    rest = bits[1:]
    turn = lambda j: rest[j % len(rest):] + rest[:j % len(rest)] if rest else []
    return [bits[:1] + turn(j) for j in range(3)]


def gather_step(held, axis, bit):
    return jnp.concatenate([held, permute_bit(held, axis, bit)], axis=0)


def gather_last(held, axis, order):
    places = [0]
    for bit in order[:-1]:
        places = places + [p ^ bit for p in places]
    return (held, places), (permute_bit(held, axis, order[-1]), [p ^ order[-1] for p in places])


def assemble_kernel(plan, count, me_ref, *refs):
    sources = refs[:len(plan)]
    dests = refs[len(plan):len(plan) + count]
    sems = refs[-1]
    copies = []
    for j, (places, dest, row_off, lane_off, block_rows) in enumerate(plan):
        rows, width = sources[j].shape[1:]
        for p, place in enumerate(places):
            start = pl.multiple_of((me_ref[0] ^ place) * block_rows + row_off, 16)
            copies.append(pltpu.make_async_copy(
                sources[j].at[p],
                dests[dest].at[pl.ds(start, rows), pl.ds(lane_off, width)],
                sems.at[j, p]))
    for copy in copies:
        copy.start()
    for copy in copies:
        copy.wait()


def assemble(me, rels, plan, shapes):
    hbm = pl.BlockSpec(memory_space=pl.ANY)
    return pl.pallas_call(
        functools.partial(assemble_kernel, plan, len(shapes)),
        grid_spec=pltpu.PrefetchScalarGridSpec(
            num_scalar_prefetch=1,
            grid=(1,),
            in_specs=[hbm] * len(rels),
            out_specs=[hbm] * len(shapes),
            scratch_shapes=[pltpu.SemaphoreType.DMA((len(rels), max(r.shape[0] for r in rels)))],
        ),
        out_shape=[jax.ShapeDtypeStruct(s, BF16) for s in shapes],
        compiler_params=pltpu.CompilerParams(vmem_limit_bytes=4 * 1024 * 1024),
        cost_estimate=pl.CostEstimate(
            flops=0, bytes_accessed=sum(4 * s[0] * s[1] for s in shapes), transcendentals=0),
        name="assemble",
    )(me, *rels)


def thirds(width):
    cuts = [0] + [min(width, -(-width * k // (3 * LANES)) * LANES) for k in (1, 2)] + [width]
    return [(a, b) for a, b in zip(cuts, cuts[1:]) if b > a]


def reduce_open(part, axis, row_off, row_count):
    n = lax.axis_size(axis)
    levels = n.bit_length() - 1
    own = part.shape[0] // n
    cur = part.reshape((2,) * levels + (own, part.shape[1]))
    if (row_off, row_count) != (0, own):
        cur = lax.slice_in_dim(cur, row_off, row_off + row_count, axis=levels)
    return cur


def reduce_halves(cur, axis, bit):
    mine = (lax.axis_index(axis) // bit) % 2
    dim = cur.ndim - 2 - bit.bit_length()
    return lax.dynamic_slice_in_dim(cur, mine, 1, dim), lax.dynamic_slice_in_dim(cur, 1 - mine, 1, dim)


def reduce_step(halves, axis, bit, last):
    keep, send = halves
    total = keep.astype(F32) + permute_bit(send, axis, bit).astype(F32)
    return total if last else total.astype(BF16)


def reduce_rest(cur, axis, order):
    for bit in reversed(order):
        cur = reduce_step(reduce_halves(cur, axis, bit), axis, bit, bit == order[0])
    return cur.reshape(cur.shape[-2:])


def sum_cube(x, axis):
    n = lax.axis_size(axis)
    bit = 1
    while bit < n:
        x = (x.astype(F32) + permute_bit(x, axis, bit).astype(F32)).astype(x.dtype)
        bit *= 2
    return x


def sum_bits(x, axis, bits):
    total = x
    for bit in bits + ([bits[0] | bits[1]] if len(bits) == 2 else []):
        total = total + permute_bit(x, axis, bit)
    return total


def tensor_gather(x, natural):
    n = lax.axis_size("tensor")
    rank = lax.axis_index("tensor")
    bit = 1
    while bit < n:
        other = permute_bit(x, "tensor", bit)
        if natural:
            low = (rank // bit) % 2 == 0
            x = jnp.concatenate([jnp.where(low, x, other), jnp.where(low, other, x)], axis=0)
        else:
            x = jnp.concatenate([x, other], axis=0)
        bit *= 2
    return x


def tensor_scatter(product, arrays, natural, late=lambda arrays: arrays):
    n = lax.axis_size("tensor")
    rank = lax.axis_index("tensor")
    if n == 2:
        half = arrays[0].shape[0] // 2
        cut = lambda a, k: lax.dynamic_slice_in_dim(a, k * half, half, 0) if natural else (
            lax.slice_in_dim(a, k * half, (k + 1) * half, axis=0))
        mine, other = (rank, 1 - rank) if natural else (0, 1)
        send = product(*[cut(a, other) for a in arrays]).astype(BF16)
        arrived = permute_bit(send, "tensor", 1)
        arrays = late(arrays)
        return product(*[cut(a, mine) for a in arrays]) + arrived.astype(F32)
    x = product(*late(arrays))
    bit = n // 2
    while bit >= 1:
        half = x.shape[0] // 2
        if natural:
            mine = (rank // bit) % 2
            keep = lax.dynamic_slice_in_dim(x, mine * half, half, 0)
            send = lax.dynamic_slice_in_dim(x, (1 - mine) * half, half, 0)
        else:
            keep, send = x[:half], x[half:]
        x = keep.astype(F32) + permute_bit(send.astype(BF16), "tensor", bit).astype(F32)
        bit //= 2
    return x


def inverse_rms(v):
    return lax.rsqrt(jnp.mean(v * v, axis=-1, keepdims=True) + NORM_EPS)


def norm_back(v, inverse, gain, grad):
    u = grad * gain
    into = inverse * u - inverse ** 3 * v * jnp.mean(u * v, axis=-1, keepdims=True)
    return into, jnp.sum(grad * v * inverse, axis=0)


def rope_tables():
    half = HEAD_DIM // 2
    index = (jnp.arange(HEAD_DIM, dtype=jnp.int32) % half).astype(F32)
    frequency = jnp.exp(index * (-2.0 * math.log(ROPE_THETA) / HEAD_DIM))
    angles = jnp.arange(LEN, dtype=jnp.int32).astype(F32)[:, None] * frequency[None, :]
    return jnp.cos(angles), jnp.sin(angles)


def per_device(
    layer_input, segment_ids, out_grad, norm_gain, query_w, key_w, value_w, out_w, mamba_gate_w,
    mamba_in_w, state_in_w, step_w, channel_conv, state_conv, step_bias, decay_log, skip_gain,
    mamba_out_w, ffn_gain, ffn_gate_w, ffn_up_w, ffn_down_w,
):
    dp = lax.axis_size("dp")
    rank = lax.axis_index("tensor")
    me = lax.axis_index("dp").astype(jnp.int32).reshape(1)
    heads = query_w.shape[1] // HEAD_DIM
    ssm = step_w.shape[1]
    width = mamba_in_w.shape[1]
    q_width = query_w.shape[1]
    units = ffn_gate_w.shape[1]
    kv_index = rank * heads // (HEADS // KV_HEADS)
    features = layer_input.shape[1]
    block_rows = query_w.shape[0]
    half_rows = block_rows // 2
    orders = bit_orders("dp")

    key_own = lax.dynamic_slice_in_dim(key_w, kv_index * HEAD_DIM, HEAD_DIM, 1)
    value_own = lax.dynamic_slice_in_dim(value_w, kv_index * HEAD_DIM, HEAD_DIM, 1)
    qkv_shard = jnp.concatenate([query_w, key_own, value_own], axis=1)
    mix_shard = jnp.concatenate(
        [mamba_gate_w, mamba_in_w, state_in_w, jnp.pad(step_w, ((0, 0), (0, STATE - ssm)))], axis=1)
    total_cols = mix_shard.shape[1] + qkv_shard.shape[1]
    mix_cols = thirds(total_cols)
    mix_cols = [(a, min(b, mix_shard.shape[1])) for a, b in mix_cols if a < mix_shard.shape[1]]
    steps = len(orders[0])
    shards = [(mix_shard[:, a:b], 0, a, j) for j, (a, b) in enumerate(mix_cols)]
    shards.append((qkv_shard, 1, 0, 2))
    held = [p[0][None] for p in shards]
    for k in range(steps - 1):
        held = [gather_step(h, "dp", orders[p[3]][k]) for h, p in zip(held, shards)]

    later = jnp.concatenate([ffn_gate_w, ffn_up_w, ffn_down_w.T], axis=1)
    later, held = lax.optimization_barrier((later, held))
    later = lax.all_gather(later, "dp", axis=0, tiled=True)
    ffn_gate, ffn_up, ffn_down_t = (later[:, k * units:(k + 1) * units] for k in range(3))

    rels, plan = [], []
    for h, (_, dest, lane_off, j) in zip(held, shards):
        for rel, places in gather_last(h, "dp", orders[j]):
            rels.append(rel)
            plan.append((places, dest, 0, lane_off, block_rows))

    (out_shard, mout_shard), rels = lax.optimization_barrier(((out_w.T, mamba_out_w.T), rels))
    mix_w, qkv_w = assemble(me, rels, plan, [(features, mix_shard.shape[1]),
                                            (features, qkv_shard.shape[1])])
    shards2 = [(mout_shard[:half_rows], 1, 0, 0), (mout_shard[half_rows:], 1, half_rows, 1),
               (out_shard, 0, 0, 2)]
    held2 = [p[0][None] for p in shards2]

    def output_step(held, k):
        return [gather_step(h, "dp", orders[p[3]][k]) for h, p in zip(held, shards2)]

    tokens = layer_input.astype(F32)
    inverse = inverse_rms(tokens)
    normed = tensor_gather((tokens * inverse * norm_gain).astype(BF16), True)
    top_grad = tensor_gather(out_grad, False)
    rows = normed.shape[0]
    seqs = rows // LEN

    seg = segment_ids.reshape(seqs, LEN)
    seg_col = segment_ids[:, None]
    masks = token_masks(seg)
    starts = jnp.sum(seg[:, None, :] < seg[:, ::BQ, None], axis=-1, dtype=jnp.int32)
    first = (starts // BQ).reshape(-1)
    cos, sin = rope_tables()

    qkv = dot_nn(normed, qkv_w)
    for k in range(steps - 3):
        held2 = output_step(held2, k)
    normed_late, held2, qkv = lax.optimization_barrier((normed, held2, qkv))
    pre = dot_nn(normed_late, mix_w)
    held2 = output_step(held2, steps - 3)
    pre, held2 = lax.optimization_barrier((pre, held2))
    pad_heads = lambda a: jnp.pad(a[None], ((0, 0), (0, STATE - ssm)))
    bias, rate = pad_heads(step_bias), pad_heads(decay_log)
    skip = jnp.repeat(skip_gain, HEAD_DIM)[None]
    spread = jnp.pad(jnp.repeat(jnp.eye(ssm, dtype=BF16), HEAD_DIM, axis=1), ((0, STATE - ssm), (0, 0)))
    chunk_rows = segment_ids.reshape(-1, 1, Q)
    gated, scanned, states = mix_fwd(
        seg_col, chunk_rows, masks, pre, channel_conv, state_conv, bias, rate, skip, spread, ssm)

    held2 = output_step(held2, steps - 2)
    qkv, gated, held2 = lax.optimization_barrier((qkv, gated, held2))
    queries, key_rows, value_rows = rope(qkv, cos, sin)
    seg_blocks = segment_ids.reshape(-1, 1, BQ)
    attended, lse = attend_fwd(first, queries, key_rows, value_rows, seg_col, seg_blocks)
    rels2, plan2 = [], []
    for h, (_, dest, row_off, j) in zip(held2, shards2):
        for rel, places in gather_last(h, "dp", orders[j]):
            rels2.append(rel)
            plan2.append((places, dest, row_off, 0, block_rows))
    out_t, mout_t = assemble(me, rels2, plan2, [(features, q_width), (features, width)])

    branch = tensor_scatter(
        lambda a, b: dot_nt(a, out_t) + dot_nt(b, mout_t), (attended, gated), True)
    middle = tokens + branch
    mid_inverse = inverse_rms(middle)
    mid = tensor_gather((middle * mid_inverse * ffn_gain).astype(BF16), False)
    gate_vals = dot_nn(mid, ffn_gate).astype(BF16).astype(F32)
    up_vals = dot_nn(mid, ffn_up).astype(BF16).astype(F32)
    act = (jax.nn.silu(gate_vals) * up_vals).astype(BF16)
    block_out = (middle + tensor_scatter(lambda a: dot_nt(a, ffn_down_t), (act,), False)).astype(BF16)

    act_grad = dot_nn(top_grad, ffn_down_t)
    gate_sig = jax.nn.sigmoid(gate_vals)
    gate_grad = (act_grad * up_vals * silu_slope(gate_vals, gate_sig)).astype(BF16)
    up_grad = (act_grad * (gate_vals * gate_sig)).astype(BF16)
    mid_norm_grad = tensor_scatter(
        lambda a, b: dot_nt(a, ffn_gate) + dot_nt(b, ffn_up), (gate_grad, up_grad), False)
    down_part = dot_tn(top_grad, act).astype(BF16)
    gate_part = dot_tn(mid, gate_grad).astype(BF16)
    up_part = dot_tn(mid, up_grad).astype(BF16)
    by_owner = lambda a: a.reshape(dp, block_rows, units)
    ffn_sum = lax.psum_scatter(
        jnp.concatenate([by_owner(gate_part), by_owner(up_part), by_owner(down_part)], axis=1),
        "dp", scatter_dimension=0, tiled=True)[0]
    ffn_gate_w_grad, ffn_up_w_grad, ffn_down_w_grad = (
        ffn_sum[k * block_rows:(k + 1) * block_rows].astype(F32) for k in range(3))

    mid_into, ffn_gain_part = norm_back(middle, mid_inverse, ffn_gain, mid_norm_grad)
    middle_grad = out_grad.astype(F32) + mid_into
    branch_grad = tensor_gather(middle_grad.astype(BF16), True)
    attended_grad = dot_nn(branch_grad, out_t).astype(BF16)
    gated_grad = dot_nn(branch_grad, mout_t)
    out_part = dot_tn(branch_grad, attended).astype(BF16)
    mout_part = dot_tn(branch_grad, gated).astype(BF16)
    pieces2 = [(mout_part, 0, half_rows, 0), (mout_part, half_rows, half_rows, 1),
               (out_part, 0, block_rows, 2)]
    halves2 = [
        reduce_halves(reduce_open(p, "dp", off, count), "dp", orders[j][-1]) for p, off, count, j in pieces2]
    attended_grad, halves2 = lax.optimization_barrier((attended_grad, halves2))
    held2 = [reduce_step(h, "dp", orders[p[3]][-1], False) for h, p in zip(halves2, pieces2)]
    query_grad, key_grad, value_grad = attend_bwd(
        first, queries, key_rows, value_rows, attended_grad, seg_col, seg_blocks, lse, attended, cos, sin)
    qkv_grad = jnp.concatenate([query_grad, key_grad, value_grad], axis=1)
    halves2 = [reduce_halves(c, "dp", orders[p[3]][-2]) for c, p in zip(held2, pieces2)]
    gated_grad, qkv_grad, halves2 = lax.optimization_barrier((gated_grad, qkv_grad, halves2))
    held2 = [reduce_step(h, "dp", orders[p[3]][-2], False) for h, p in zip(halves2, pieces2)]
    mix_grad, conv_part, state_conv_part, head_part, skip_part = mix_bwd(
        seg_col, chunk_rows, masks, pre, scanned, states, gated_grad, channel_conv, state_conv, bias,
        rate, skip, spread, ssm)

    pieces1 = [(dot_tn(normed, mix_grad[:, a:b]).astype(BF16), j) for j, (a, b) in enumerate(mix_cols)]
    pieces1.append((dot_tn(normed, qkv_grad).astype(BF16), 2))
    halves1 = [reduce_halves(reduce_open(p, "dp", 0, block_rows), "dp", orders[j][-1]) for p, j in pieces1]
    mix_grad_late, halves1 = lax.optimization_barrier((mix_grad, halves1))
    held1 = [reduce_step(h, "dp", orders[p[1]][-1], False) for h, p in zip(halves1, pieces1)]
    cur = held1 + held2
    bits_left = [list(reversed(orders[p[1]][:-1])) for p in pieces1]
    bits_left += [list(reversed(orders[p[3]][:-2])) for p in pieces2]

    def late(arrays):
        nonlocal cur
        arrays, cur = lax.optimization_barrier((arrays, cur))
        cur = tail_step(cur)
        return arrays

    def tail_step(cur):
        out = []
        for c, bits in zip(cur, bits_left):
            if bits:
                bit = bits.pop(0)
                c = reduce_step(reduce_halves(c, "dp", bit), "dp", bit, not bits)
            out.append(c)
        return out

    normed_grad = tensor_scatter(
        lambda a, b: dot_nt(a, qkv_w) + dot_nt(b, mix_w), (qkv_grad, mix_grad_late), True, late)
    norm_into, norm_gain_part = norm_back(tokens, inverse, norm_gain, normed_grad)
    input_grad = middle_grad + norm_into

    heads_part = jnp.concatenate([
        head_part[0, :ssm], head_part[1, :ssm],
        jnp.sum(skip_part.reshape(ssm, HEAD_DIM), axis=1)])
    small = jnp.concatenate([
        conv_part.reshape(-1), heads_part, state_conv_part.reshape(-1), ffn_gain_part,
        norm_gain_part])
    small_bits = list(bit_orders("dp")[0])
    for _ in range(steps - 2):
        cur, small = lax.optimization_barrier((cur, small))
        if small_bits:
            small = sum_bits(small, "dp", [small_bits.pop() for _ in range(min(2, len(small_bits)))])
        cur = tail_step(cur)
    sums = [c.reshape(c.shape[-2:]) for c in cur]
    mix_sum = jnp.concatenate(sums[:len(mix_cols)], axis=1)
    qkv_sum = sums[len(mix_cols)]
    mout_a, mout_b, out_sum = sums[len(mix_cols) + 1:]
    mamba_out_w_grad = jnp.concatenate([mout_a, mout_b], axis=0).T
    out_w_grad = out_sum.T

    place = lambda a, whole: lax.dynamic_update_slice_in_dim(
        jnp.zeros((block_rows, whole.shape[1]), BF16), a.astype(BF16), kv_index * HEAD_DIM, 1)
    shared = sum_cube(jnp.concatenate([
        place(qkv_sum[:, q_width:q_width + HEAD_DIM], key_w),
        place(qkv_sum[:, q_width + HEAD_DIM:], value_w),
        mix_sum[:, 2 * width:2 * width + 2 * STATE].astype(BF16)], axis=1), "tensor").astype(F32)
    kv_cols = key_w.shape[1]

    own = 4 * width + 3 * ssm
    conv_grad = small[:4 * width].reshape(4, width)
    bias_grad, decay_grad, skip_grad = (
        small[4 * width + k * ssm:4 * width + (k + 1) * ssm] for k in range(3))
    both = sum_cube(small[own:], "tensor")
    state_conv_grad = both[:8 * STATE].reshape(4, 2 * STATE)
    ffn_gain_grad = both[8 * STATE:8 * STATE + features]
    gain = both[8 * STATE + features:]
    return (
        block_out,
        input_grad,
        gain,
        qkv_sum[:, :q_width],
        shared[:, :kv_cols],
        shared[:, kv_cols:2 * kv_cols],
        out_w_grad,
        mix_sum[:, :width],
        mix_sum[:, width:2 * width],
        shared[:, 2 * kv_cols:],
        mix_sum[:, 2 * width + 2 * STATE:2 * width + 2 * STATE + ssm],
        conv_grad,
        state_conv_grad,
        bias_grad,
        decay_grad,
        skip_grad,
        mamba_out_w_grad,
        ffn_gain_grad,
        ffn_gate_w_grad,
        ffn_up_w_grad,
        ffn_down_w_grad.T,
    )


def solution(mesh):
    in_specs = (
        P(("dp", "tensor"), None),
        P("dp"),
        P(("dp", "tensor"), None),
        P(),
        P("dp", "tensor"),
        P("dp", None),
        P("dp", None),
        P("tensor", "dp"),
        P("dp", "tensor"),
        P("dp", "tensor"),
        P("dp", None),
        P("dp", "tensor"),
        P(None, "tensor"),
        P(),
        P("tensor"),
        P("tensor"),
        P("tensor"),
        P("tensor", "dp"),
        P(),
        P("dp", "tensor"),
        P("dp", "tensor"),
        P("tensor", "dp"),
    )
    out_specs = (
        P(("dp", "tensor"), None),
        P(("dp", "tensor"), None),
        P(),
        P("dp", "tensor"),
        P("dp", None),
        P("dp", None),
        P("tensor", "dp"),
        P("dp", "tensor"),
        P("dp", "tensor"),
        P("dp", None),
        P("dp", "tensor"),
        P(None, "tensor"),
        P(),
        P("tensor"),
        P("tensor"),
        P("tensor"),
        P("tensor", "dp"),
        P(),
        P("dp", "tensor"),
        P("dp", "tensor"),
        P("tensor", "dp"),
    )
    return jax.shard_map(
        per_device, mesh=mesh, in_specs=in_specs, out_specs=out_specs, check_vma=False
    )
```
